32 devices in a mesh: ang: 4 (over x, core), tile: 8 (over z, y).
Axes of the slice: x: 2, y: 2, z: 4, core: 2. Of those that a mesh axis runs over, the one named last changes fastest.
Arguments:
- volume: float32 [256, 128, 256], P('ang', 'tile'), may hold values from -6 to 6
- phase: float32 [4, 128, 256], P('ang', 'tile'), may hold values from -6 to 6
- dual: float32 [4, 128, 256], P('ang', 'tile'), may hold values from -3 to 3
- probe_real: float32 [128, 128], replicated, may hold values from -4 to 4
- probe_imag: float32 [128, 128], replicated, may hold values from -4 to 4
- intensity: float32 [4, 32, 128, 128], P('ang', 'tile'), may hold values from 0.05 to 4
- offsets: int32 [4, 32], P('ang', 'tile'), may hold values from 0 to 128
- angle_index: int32 [4], P('ang'), may hold values from 0 to 180
Outputs:
- phase_new: float32 [4, 128, 256], P('ang', 'tile')
- volume_new: float32 [256, 128, 256], P('ang', 'tile')
- dual_new: float32 [4, 128, 256], P('ang', 'tile')
The draws below stay inside these ranges and needn't reach their ends.
Inputs may be any that keep to these rules, and one draw needn't show every extreme that they name: `offsets`: the probe's 128 columns starting at the offset lie inside the 256 columns of a projection.
All inputs are finite; a program needn't handle non-finite values.
Results may differ from the reference program's by a relative error of at most 0.015.
Values may be sent and summed in bfloat16 or wider, within the bound.
No kernel may reach another device: no remote copies, remote signals or barrier semaphores. Data moves between devices by JAX's collectives and lax.ppermute only.
A program may use at most 64 MiB of HBM per device.

```python
import math
import jax
import jax.numpy as jnp
from jax import lax

N = 256
PROBE = 128
BAND = 128
POS = 32
ANG = 4


def plant(entries, key, least, largest):
    dims = entries.shape
    spot = [jax.random.randint(jax.random.fold_in(key, axis), (), 0, dims[axis]) for axis in range(len(dims))]
    entries = entries.at[tuple(spot)].set(least)
    longest = dims.index(max(dims))
    spot[longest] = (spot[longest] + 1) % dims[longest]
    return entries.at[tuple(spot)].set(largest)


def shard_levels(rng, dims, pieces, smallest, high):
    factor_of, own = 1.0, jax.random.fold_in(rng, 6)
    for dim, shards_of in pieces:
        draws = jnp.exp(jax.random.uniform(jax.random.fold_in(own, dim), (shards_of,), jnp.float32, smallest / len(pieces), high / len(pieces)))
        factor_of = factor_of * jnp.repeat(draws, dims[dim] // shards_of).reshape([-1 if axis == dim else 1 for axis in range(len(dims))])
    return factor_of


def normal_values(key, dims, deviation, most, shards=(), kind=jnp.bfloat16):
    array = deviation * jax.random.normal(key, dims, jnp.float32)
    if shards:
        array = array * shard_levels(key, dims, shards, -0.22, 0.18)
    return jnp.clip(array, -most, most).astype(kind)


def setup_inputs(seed: int = 0) -> dict:
    arg_keys = jax.random.split(jax.random.key(seed), 9)
    volume = normal_values(arg_keys[0], (N, BAND, N), 1.0, 6.0, ((0, 4), (1, 8)), jnp.float32)
    phase = normal_values(arg_keys[1], (ANG, BAND, N), 1.0, 6.0, ((0, 4), (1, 8)), jnp.float32)
    dual = normal_values(arg_keys[2], (ANG, BAND, N), 0.5, 3.0, ((0, 4), (1, 8)), jnp.float32)
    probe_real = normal_values(arg_keys[3], (PROBE, PROBE), 0.7, 4.0, (), jnp.float32)
    probe_imag = normal_values(arg_keys[4], (PROBE, PROBE), 0.7, 4.0, (), jnp.float32)
    intensity = jnp.clip(jnp.exp(math.log(4.0) - 4.3820266 * jax.random.uniform(arg_keys[5], (ANG, POS, PROBE, PROBE), jnp.float32) ** shard_levels(arg_keys[5], (ANG, POS, PROBE, PROBE), ((0, 4), (1, 8)), -0.2, 0.2)), 0.05, 4.0)
    offsets = plant(jax.random.randint(arg_keys[6], (ANG, POS), 0, N - PROBE + 1), jax.random.fold_in(arg_keys[6], 1), 0, N - PROBE).astype(jnp.int32)
    angle_index = plant(jax.random.randint(arg_keys[7], (ANG,), 0, 181), jax.random.fold_in(arg_keys[7], 1), 0, 180).astype(jnp.int32)
    return {"volume": volume, "phase": phase, "dual": dual, "probe_real": probe_real, "probe_imag": probe_imag, "intensity": intensity, "offsets": offsets, "angle_index": angle_index}


angle_center = 90.0
rho_weight = 1.0
eta_step = 0.01
tau_step = 1.0
smooth_weight = 0.25

def dft_tables(length):
    index = jnp.arange(length, dtype=jnp.int32)
    product = index[:, None] * index[None, :] % length
    phases = product.astype(jnp.float32) * (2.0 * math.pi / length)
    return (jnp.cos(phases), jnp.sin(phases))

def signed_freq(length):
    index = jnp.arange(length, dtype=jnp.int32)
    return jnp.where(index < length // 2, index, index - length).astype(jnp.float32)

def shear_coefficients(angle_number):
    theta = (angle_number.astype(jnp.float32) - angle_center) * (math.pi / 360.0)
    return (-jnp.tan(0.5 * theta), jnp.sin(theta))

def shear_last(volume_part, shifts, cos_half, sin_half, frequency):
    row_count, depth_count, length = volume_part.shape
    flattened = volume_part.reshape(row_count * depth_count, length)
    real_part = jnp.dot(flattened, cos_half, preferred_element_type=jnp.float32).reshape(row_count, depth_count, length)
    imag_part = -jnp.dot(flattened, sin_half, preferred_element_type=jnp.float32).reshape(row_count, depth_count, length)
    angles = 2.0 * math.pi / length * shifts[:, None] * frequency[None, :]
    cosine_turn = jnp.cos(angles)[:, None, :]
    sine_turn = jnp.sin(angles)[:, None, :]
    turned_r = (real_part * cosine_turn + imag_part * sine_turn).astype(jnp.bfloat16).reshape(row_count * depth_count, length)
    turned_i = (imag_part * cosine_turn - real_part * sine_turn).astype(jnp.bfloat16).reshape(row_count * depth_count, length)
    result = jnp.dot(turned_r, cos_half, preferred_element_type=jnp.float32) - jnp.dot(turned_i, sin_half, preferred_element_type=jnp.float32)
    return (result / length).reshape(row_count, depth_count, length)

def shear_first(volume_part, shifts, cos_half, sin_half, frequency):
    row_count, depth_count, length = volume_part.shape
    flattened = volume_part.reshape(row_count, depth_count * length)
    real_part = jnp.dot(cos_half, flattened, preferred_element_type=jnp.float32).reshape(row_count, depth_count, length)
    imag_part = -jnp.dot(sin_half, flattened, preferred_element_type=jnp.float32).reshape(row_count, depth_count, length)
    angles = 2.0 * math.pi / row_count * frequency[:, None] * shifts[None, :]
    cosine_turn = jnp.cos(angles)[:, None, :]
    sine_turn = jnp.sin(angles)[:, None, :]
    turned_r = (real_part * cosine_turn + imag_part * sine_turn).astype(jnp.bfloat16).reshape(row_count, depth_count * length)
    turned_i = (imag_part * cosine_turn - real_part * sine_turn).astype(jnp.bfloat16).reshape(row_count, depth_count * length)
    result = jnp.dot(cos_half, turned_r, preferred_element_type=jnp.float32) - jnp.dot(sin_half, turned_i, preferred_element_type=jnp.float32)
    return (result / row_count).reshape(row_count, depth_count, length)

def project_lines(volume_part, coef_a, cos_half, sin_half, cos_full, sin_full, frequency):
    row_count, depth_count, length = volume_part.shape
    flattened = volume_part.reshape(row_count * depth_count, length)
    real_part = jnp.dot(flattened, cos_half, preferred_element_type=jnp.float32).reshape(row_count, depth_count, length)
    imag_part = -jnp.dot(flattened, sin_half, preferred_element_type=jnp.float32).reshape(row_count, depth_count, length)
    centred = jnp.arange(row_count, dtype=jnp.int32).astype(jnp.float32) - 0.5 * row_count
    angles = 2.0 * math.pi / length * (coef_a * centred)[:, None] * frequency[None, :]
    cosine_turn = jnp.cos(angles)[:, None, :]
    sine_turn = jnp.sin(angles)[:, None, :]
    summed_r = lax.optimization_barrier(jnp.sum(real_part * cosine_turn + imag_part * sine_turn, axis=0))
    summed_i = lax.optimization_barrier(jnp.sum(imag_part * cosine_turn - real_part * sine_turn, axis=0))
    lines = jnp.dot(summed_r, cos_full, precision=lax.Precision.HIGHEST) - jnp.dot(summed_i, sin_full, precision=lax.Precision.HIGHEST)
    return lines / (length * math.sqrt(length))

def back_lines(lines, row_count, coef_a, cos_half, sin_half, cos_full, sin_full, frequency):
    depth_count, length = lines.shape
    spectrum_r = jnp.dot(lines, cos_full, precision=lax.Precision.HIGHEST)
    spectrum_i = -jnp.dot(lines, sin_full, precision=lax.Precision.HIGHEST)
    centred = jnp.arange(row_count, dtype=jnp.int32).astype(jnp.float32) - 0.5 * row_count
    angles = 2.0 * math.pi / length * (coef_a * centred)[:, None] * frequency[None, :]
    cosine_turn = jnp.cos(angles)[:, None, :]
    sine_turn = jnp.sin(angles)[:, None, :]
    turned_r = (spectrum_r[None] * cosine_turn - spectrum_i[None] * sine_turn).astype(jnp.bfloat16).reshape(row_count * depth_count, length)
    turned_i = (spectrum_r[None] * sine_turn + spectrum_i[None] * cosine_turn).astype(jnp.bfloat16).reshape(row_count * depth_count, length)
    spread = jnp.dot(turned_r, cos_half, preferred_element_type=jnp.float32) - jnp.dot(turned_i, sin_half, preferred_element_type=jnp.float32)
    return (spread / (length * math.sqrt(length))).reshape(row_count, depth_count, length).astype(jnp.bfloat16)

def patch_gradient(patch, measured, probe_real, probe_imag, dft_cos, dft_sin):

    def product_of(left, right):
        return jnp.dot(left, right, precision=lax.Precision.HIGHEST)
    wave_r = probe_real * jnp.cos(patch) - probe_imag * jnp.sin(patch)
    wave_i = probe_real * jnp.sin(patch) + probe_imag * jnp.cos(patch)
    half_r = product_of(wave_r, dft_cos) + product_of(wave_i, dft_sin)
    half_i = product_of(wave_i, dft_cos) - product_of(wave_r, dft_sin)
    far_r = product_of(dft_cos, half_r) + product_of(dft_sin, half_i)
    far_i = product_of(dft_cos, half_i) - product_of(dft_sin, half_r)
    misfit = far_r * far_r + far_i * far_i - measured
    weighted_r = misfit * far_r
    weighted_i = misfit * far_i
    back_r = product_of(weighted_r, dft_cos) - product_of(weighted_i, dft_sin)
    back_i = product_of(weighted_i, dft_cos) + product_of(weighted_r, dft_sin)
    exit_r = product_of(dft_cos, back_r) - product_of(dft_sin, back_i)
    exit_i = product_of(dft_cos, back_i) + product_of(dft_sin, back_r)
    return 2.0 * (exit_i * wave_r - exit_r * wave_i)

def reference(volume, phase, dual, probe_real, probe_imag, intensity, offsets, angle_index):
    length = volume.shape[2]
    width = probe_real.shape[1]
    cos_full, sin_full = dft_tables(length)
    cos_half = cos_full.astype(jnp.bfloat16)
    sin_half = sin_full.astype(jnp.bfloat16)
    frequency = signed_freq(length)
    centred = jnp.arange(length, dtype=jnp.int32).astype(jnp.float32) - 0.5 * length
    probe_cos, probe_sin = dft_tables(width)
    dft_cos = probe_cos / math.sqrt(width)
    dft_sin = probe_sin / math.sqrt(width)

    def project_all(volume_now):
        rounded = volume_now.astype(jnp.bfloat16)

        def one_angle(angle_number):
            coef_a, coef_b = shear_coefficients(angle_number)
            first = shear_last(rounded, coef_a * centred, cos_half, sin_half, frequency).astype(jnp.bfloat16)
            second = shear_first(first, coef_b * centred, cos_half, sin_half, frequency).astype(jnp.bfloat16)
            return project_lines(second, coef_a, cos_half, sin_half, cos_full, sin_full, frequency)
        return lax.map(one_angle, angle_index)
    proj_old = project_all(volume)

    def angle_gradient(inputs):
        image, corners, measured_all = inputs

        def add_position(position, gradient_image):
            corner = corners[position]
            patch = lax.dynamic_slice_in_dim(image, corner, width, 1)
            term = patch_gradient(patch, measured_all[position], probe_real, probe_imag, dft_cos, dft_sin)
            current = lax.dynamic_slice_in_dim(gradient_image, corner, width, 1)
            return lax.dynamic_update_slice_in_dim(gradient_image, current + term, corner, 1)
        return lax.fori_loop(0, corners.shape[0], add_position, jnp.zeros_like(image))
    gradients = lax.map(angle_gradient, (phase, offsets, intensity))
    phase_new = phase - eta_step * (gradients + dual + rho_weight * (phase - proj_old))
    resid = rho_weight * (proj_old - phase_new) - dual

    def add_angle(total, inputs):
        angle_number, lines = inputs
        coef_a, coef_b = shear_coefficients(angle_number)
        spread = back_lines(lines, length, coef_a, cos_half, sin_half, cos_full, sin_full, frequency)
        second = shear_first(spread, -(coef_b * centred), cos_half, sin_half, frequency).astype(jnp.bfloat16)
        third = shear_last(second, -(coef_a * centred), cos_half, sin_half, frequency)
        return (total + third, None)
    back, unused = lax.scan(add_angle, jnp.zeros(volume.shape, jnp.float32), (angle_index, resid))
    padded = jnp.pad(volume, ((0, 0), (1, 1), (0, 0)))
    smooth = 2.0 * volume - padded[:, :-2, :] - padded[:, 2:, :]
    volume_new = volume - tau_step * (back + smooth_weight * smooth)
    proj_new = project_all(volume_new)
    dual_new = dual + rho_weight * (phase_new - proj_new)
    return (phase_new, volume_new, dual_new)
```

```python
import functools
import math

import jax
import jax.numpy as jnp
import numpy as np
from jax import lax
from jax.experimental import pallas as pl
from jax.experimental.pallas import tpu as pltpu
from jax.sharding import PartitionSpec as P

angle_center = 90.0
rho_weight = 1.0
eta_step = 0.01
tau_step = 1.0
smooth_weight = 0.25

F32 = jnp.float32
BF16 = jnp.bfloat16
VMEM_SPEC = pl.BlockSpec(memory_space=pltpu.VMEM)
SMEM_SPEC = pl.BlockSpec(memory_space=pltpu.SMEM)
VMEM_LIMIT = 56 * 1024 * 1024


def table_pair(length):
    index = np.arange(length)
    phases = (index[:, None] * index[None, :] % length) * (2.0 * np.pi / length)
    return np.cos(phases).astype(np.float32), np.sin(phases).astype(np.float32)


def packed_tables(length):
    half = length // 2
    cos_t, sin_t = table_pair(length)
    bf = np.asarray(jnp.bfloat16).dtype if False else jnp.bfloat16
    out = []
    for kind in (np.float32, bf):
        c = cos_t.astype(kind).astype(np.float32)
        s = sin_t.astype(kind).astype(np.float32)
        forward = np.concatenate([c[:, : half + 1], -s[:, 1:half]], axis=1)
        weight = np.full((length, 1), 2.0 / length, np.float32)
        weight[0] = weight[half] = 1.0 / length
        inverse = forward.T * weight
        out.append((forward.astype(kind), inverse.astype(kind)))
    return out


def split_const(array):
    high = array.astype(jnp.bfloat16)
    low = (array - high.astype(np.float32)).astype(jnp.bfloat16)
    return np.stack([high, low])


def patch_tables(width):
    cos_t, sin_t = table_pair(width)
    c = cos_t / np.float32(math.sqrt(width))
    s = sin_t / np.float32(math.sqrt(width))
    right = np.block([[c, -s], [s, c]])
    left = np.block([[c, s], [-s, c]])
    right_conj = np.block([[c, s], [-s, c]])
    left_conj = np.block([[c, -s], [s, c]])
    return tuple(split_const(m.astype(np.float32)) for m in (right, left, left_conj, right_conj))


def dot(left, right):
    return jnp.dot(left, right, preferred_element_type=F32)


def dot_high(left, right):
    return jnp.dot(left, right, precision=lax.Precision.HIGHEST, preferred_element_type=F32)


def dot_split(left, right):
    def parts(value):
        if value.dtype == BF16:
            return value[0], value[1]
        high = value.astype(BF16)
        return high, (value - high.astype(F32)).astype(BF16)

    left_high, left_low = parts(left)
    right_high, right_low = parts(right)
    return dot(left_high, right_high) + dot(left_low, right_high) + dot(left_high, right_low)


def turn(re, im, c1, s, c2, sign):
    if sign > 0:
        return re * c1 + im * s, im * c2 - re * s
    return re * c1 - im * s, im * c2 + re * s


def fill_turn_tables(angle, slot, length, row_ref, col_ref, nyq_ref):
    half = length // 2
    unit = 2.0 * math.pi / length
    theta = (jnp.full((8, half), angle, jnp.int32).astype(F32) - angle_center) * (math.pi / 360.0)
    coef_a = -(jnp.sin(0.5 * theta) / jnp.cos(0.5 * theta))
    coef_b = jnp.sin(theta)

    lane = lax.broadcasted_iota(jnp.int32, (8, half), 1)
    sub = lax.broadcasted_iota(jnp.int32, (8, half), 0)
    freq = jnp.where(lane == 0, half, lane).astype(F32)
    phase = unit * coef_a * freq
    base = phase * sub.astype(F32)
    base_c, base_s = jnp.cos(base), jnp.sin(base)
    for block in range(length // 64):
        first = 8 * block * 8 - half
        step = phase * (first + 8 * sub).astype(F32)
        step_c, step_s = jnp.cos(step), jnp.sin(step)
        for q in range(8):
            sc, ss = step_c[q : q + 1], step_s[q : q + 1]
            c2 = base_c * sc - base_s * ss
            s = base_s * sc + base_c * ss
            rows = pl.ds((block * 8 + q) * 8, 8)
            row_ref[slot, 0, rows, :] = jnp.where(lane == 0, 1.0, c2)
            row_ref[slot, 1, rows, :] = jnp.where(lane == 0, 0.0, s)
            row_ref[slot, 2, rows, :] = c2

    for side in range(2):
        place = (lane + (side * half - half)).astype(F32)
        phase = unit * coef_b * place
        lanes = slice(side * half, side * half + half)
        base = phase * sub.astype(F32)
        base_c, base_s = jnp.cos(base), jnp.sin(base)
        for block in range(half // 64):
            step = phase * (block * 64 + 8 * sub).astype(F32)
            step_c, step_s = jnp.cos(step), jnp.sin(step)
            for q in range(8):
                sc, ss = step_c[q : q + 1], step_s[q : q + 1]
                rows = pl.ds((block * 8 + q) * 8, 8)
                col_ref[slot, 0, rows, lanes] = base_c * sc - base_s * ss
                col_ref[slot, 1, rows, lanes] = base_s * sc + base_c * ss
        top = jnp.where(sub == 0, jnp.cos(phase * float(half)), base_c)
        nyq_ref[slot, :, lanes] = top


def fill_pair_rows(slot, share, row_ref, pair_ref):
    here = lax.axis_index("ang")
    other = here + 1 - 2 * lax.rem(here, 2)
    for part in range(3):
        for place, which in enumerate((here, other)):
            rows = pl.ds(pl.multiple_of(which * share, 8), share)
            pair_ref[slot, part, place * share : (place + 1) * share, :] = row_ref[slot, part, rows, :]


def turn_cols(spectrum, slot, col_ref, nyq_ref, sign):
    half = spectrum.shape[0] // 2
    c1 = col_ref[slot, 0]
    c2 = jnp.concatenate([nyq_ref[slot], col_ref[slot, 0, 8:half, :]], axis=0)
    re, im = turn(spectrum[:half], spectrum[half:], c1, col_ref[slot, 1], c2, sign)
    return jnp.concatenate([re, im], axis=0).astype(BF16)


def turn_rows(spectrum, table_ref, slot, sign):
    half = spectrum.shape[1] // 2
    return turn(
        spectrum[:, :half],
        spectrum[:, half:],
        table_ref[slot, 0],
        table_ref[slot, 1],
        table_ref[slot, 2],
        sign,
    )


def project_slice(slab, z, groups, refs, lines_ref):
    forward_ref, inverse_ref, down_ref, up_ref, row_ref, pair_ref, col_ref, nyq_ref = refs
    here = lax.axis_index("ang")
    spectrum = dot(slab, forward_ref[...])
    for g in range(groups):
        turned = jnp.concatenate(turn_rows(spectrum, pair_ref, g, 1), axis=1).astype(BF16)
        first = dot(turned, inverse_ref[...]).astype(BF16)
        columns = turn_cols(dot(down_ref[here], first), g, col_ref, nyq_ref, 1)
        second = dot(up_ref[...], columns).astype(BF16)
        re, im = turn_rows(dot(second, forward_ref[...]), row_ref, g, 1)
        line = jnp.concatenate(
            [jnp.sum(re, axis=0, keepdims=True), jnp.sum(im, axis=0, keepdims=True)], axis=1
        )
        lines_ref[g, pl.ds(z, 1), :] = line


def slice_rows(side_refs, z, share, slices):
    return jnp.concatenate([ref[pl.ds(z, share, stride=slices), :] for ref in side_refs], axis=1)


def prepare_kernel(left_ref, right_ref, out_ref):
    slices, share, _ = out_ref.shape
    for z in range(slices):
        out_ref[z] = slice_rows((left_ref, right_ref), z, share, slices).astype(BF16)


def base_kernel(left_ref, right_ref, before_ref, after_ref, base_ref, sent_ref):
    slices, share, _ = base_ref.shape

    def rows(z):
        return slice_rows((left_ref, right_ref), z, share, slices)

    for z in range(slices):
        now = rows(z)
        low = before_ref[...].astype(F32) if z == 0 else rows(z - 1)
        high = after_ref[...].astype(F32) if z == slices - 1 else rows(z + 1)
        base = now - tau_step * smooth_weight * (2.0 * now - low - high)
        base_ref[z] = base
        sent_ref[z] = base.astype(BF16)


def setup_tables(angles_ref, share, length, row_ref, pair_ref, col_ref, nyq_ref):
    for g in range(row_ref.shape[0]):
        fill_turn_tables(angles_ref[g], g, length, row_ref, col_ref, nyq_ref)
        fill_pair_rows(g, share, row_ref, pair_ref)


def project_kernel(
    unroll, angles_ref, own_ref, other_ref, forward_ref, inverse_ref, down_ref, up_ref,
    lines_ref, row_ref, pair_ref, col_ref, nyq_ref,
):
    groups, slices, length = lines_ref.shape
    share = own_ref.shape[1]
    setup_tables(angles_ref, share, length, row_ref, pair_ref, col_ref, nyq_ref)
    refs = (forward_ref, inverse_ref, down_ref, up_ref, row_ref, pair_ref, col_ref, nyq_ref)

    def body(step, carry):
        for u in range(unroll):
            z = step * unroll + u
            slab = jnp.concatenate([own_ref[z], other_ref[z]], axis=0)
            project_slice(slab, z, groups, refs, lines_ref)
        return carry

    lax.fori_loop(0, slices // unroll, body, 0)


def back_kernel(
    unroll, angles_ref, spectra_ref, forward_ref, inverse_ref, down_ref, up_ref,
    out_ref, row_ref, pair_ref, col_ref, nyq_ref,
):
    groups, slices, length = spectra_ref.shape
    half = length // 2
    share = out_ref.shape[1] // 2
    setup_tables(angles_ref, share, length, row_ref, pair_ref, col_ref, nyq_ref)
    here = lax.axis_index("ang")

    def body(step, carry):
        for u in range(unroll):
            z = step * unroll + u
            total_re = total_im = None
            for g in range(groups):
                line = spectra_ref[g, pl.ds(z, 1), :]
                re, im = turn(
                    line[:, :half], line[:, half:],
                    row_ref[g, 0], row_ref[g, 1], row_ref[g, 2], -1,
                )
                turned = jnp.concatenate([re, im], axis=1).astype(BF16)
                spread = dot(turned, inverse_ref[...]).astype(BF16)
                columns = turn_cols(dot(down_ref[...], spread), g, col_ref, nyq_ref, -1)
                second = dot(up_ref[here], columns).astype(BF16)
                re, im = turn_rows(dot(second, forward_ref[...]), pair_ref, g, -1)
                total_re = re if total_re is None else total_re + re
                total_im = im if total_im is None else total_im + im
            total = jnp.concatenate([total_re, total_im], axis=1).astype(BF16)
            out_ref[z] = dot(total, inverse_ref[...]).astype(BF16)
        return carry

    lax.fori_loop(0, slices // unroll, body, 0)


def update_kernel(
    unroll, angles_ref, base_ref, base_other_ref, mine_ref, theirs_ref,
    forward_ref, inverse_ref, down_ref, up_ref,
    volume_ref, lines_ref, row_ref, pair_ref, col_ref, nyq_ref, side_refs,
):
    groups, slices, length = lines_ref.shape
    share = base_ref.shape[1]
    setup_tables(angles_ref, share, length, row_ref, pair_ref, col_ref, nyq_ref)
    refs = (forward_ref, inverse_ref, down_ref, up_ref, row_ref, pair_ref, col_ref, nyq_ref)

    def body(step, carry):
        for u in range(unroll):
            z = step * unroll + u
            own = base_ref[z] - tau_step * (
                mine_ref[z, :share, :].astype(F32) + theirs_ref[z, share:, :].astype(F32)
            )
            for side in range(2):
                lanes = slice(side * length // 2, (side + 1) * length // 2)
                side_refs[side][pl.ds(z, share, stride=slices), :] = own[:, lanes]
            other = base_other_ref[z].astype(F32) - tau_step * (
                mine_ref[z, share:, :].astype(F32) + theirs_ref[z, :share, :].astype(F32)
            )
            slab = jnp.concatenate([own.astype(BF16), other.astype(BF16)], axis=0)
            project_slice(slab, z, groups, refs, lines_ref)
        return carry

    lax.fori_loop(0, slices // unroll, body, 0)
    volume_ref[...] = jnp.concatenate([ref[...] for ref in side_refs], axis=1)


def gradient_kernel(
    offsets_ref, image_ref, measured_ref, probe_r_ref, probe_i_ref,
    right_ref, left_ref, left_conj_ref, right_conj_ref, out_ref,
):
    positions, height, width = measured_ref.shape
    length = image_ref.shape[1]
    image = image_ref[...]
    cos_image, sin_image = jnp.cos(image), jnp.sin(image)
    probe_r, probe_i = probe_r_ref[...], probe_i_ref[...]
    waves = []
    for p in range(positions):
        back = length - offsets_ref[0, p]
        cos_p = pltpu.roll(cos_image, back, 1)[:, :width]
        sin_p = pltpu.roll(sin_image, back, 1)[:, :width]
        waves.append((probe_r * cos_p - probe_i * sin_p, probe_r * sin_p + probe_i * cos_p))
    total = jnp.zeros((height, length), F32)
    for p0 in range(0, positions, 2):
        some = range(p0, min(p0 + 2, positions))
        half = [
            dot_split(jnp.concatenate(waves[p], axis=1), right_ref[...]) for p in some
        ]
        stacked = jnp.concatenate(
            [jnp.concatenate([h[:, :width], h[:, width:]], axis=0) for h in half], axis=1
        )
        far = dot_split(left_ref[...], stacked)
        far_r, far_i = far[:height], far[height:]
        measured = jnp.concatenate([measured_ref[p] for p in some], axis=1)
        misfit = far_r * far_r + far_i * far_i - measured
        weighted = jnp.concatenate([misfit * far_r, misfit * far_i], axis=0)
        returned = dot_split(left_conj_ref[...], weighted)
        for i, p in enumerate(some):
            lanes = slice(i * width, (i + 1) * width)
            rows = jnp.concatenate([returned[:height, lanes], returned[height:, lanes]], axis=1)
            chi = dot_split(rows, right_conj_ref[...])
            wave_r, wave_i = waves[p]
            term = 2.0 * (chi[:, width:] * wave_r - chi[:, :width] * wave_i)
            padded = jnp.concatenate([term, jnp.zeros((height, length - width), F32)], axis=1)
            total = total + pltpu.roll(padded, offsets_ref[0, p], 1)
    out_ref[...] = total.astype(out_ref.dtype)


def phase_kernel(
    peers, grad_ref, phase_ref, dual_ref, forward_ref, inverse_ref, *rest
):
    lines = rest[:peers]
    phase_new_ref, spectrum_ref = rest[peers:]
    tiles, slices, length = grad_ref.shape
    grad = grad_ref[0].astype(F32)
    for t in range(1, tiles):
        grad = grad + grad_ref[t].astype(F32)
    line = lines[0][...]
    for other in lines[1:]:
        line = line + other[...]
    scale = 1.0 / math.sqrt(length)
    proj_old = dot_high(line, inverse_ref[...]) * scale
    phase, dual = phase_ref[...], dual_ref[...]
    phase_new = phase - eta_step * (grad + dual + rho_weight * (phase - proj_old))
    resid = rho_weight * (proj_old - phase_new) - dual
    phase_new_ref[...] = phase_new
    spectrum_ref[...] = dot_high(resid, forward_ref[...]) * scale


def dual_kernel(peers, phase_ref, dual_ref, inverse_ref, *rest):
    lines = rest[:peers]
    dual_new_ref = rest[peers]
    line = lines[0][...]
    for other in lines[1:]:
        line = line + other[...]
    proj_new = dot_high(line, inverse_ref[...]) * (1.0 / math.sqrt(line.shape[1]))
    dual_new_ref[...] = dual_ref[...] + rho_weight * (phase_ref[...] - proj_new)


def call(kernel, outs, specs, *args, scratch=(), cost=None, name=None, grid=()):
    return pl.pallas_call(
        kernel,
        grid=grid,
        out_shape=outs,
        in_specs=specs,
        out_specs=jax.tree.map(lambda _: VMEM_SPEC, outs),
        scratch_shapes=list(scratch),
        cost_estimate=cost,
        name=name,
        compiler_params=pltpu.CompilerParams(vmem_limit_bytes=VMEM_LIMIT),
    )(*args)


def shards(volume, phase, dual, probe_real, probe_imag, intensity, offsets, angle_index):
    share, slices, length = volume.shape
    width = probe_real.shape[1]
    half = length // 2
    ang = lax.axis_size("ang")
    tiles = lax.axis_size("tile")
    groups = ang // 2
    pair = 2 * share
    shape = jax.ShapeDtypeStruct

    (forward_full, inverse_full), (forward, inverse) = packed_tables(length)
    down, up = forward.T, inverse.T
    owners = [
        np.r_[i * share : (i + 1) * share, (i ^ 1) * share : ((i ^ 1) + 1) * share] for i in range(ang)
    ]
    down_part = np.stack([down[:, rows] for rows in owners])
    up_part = np.stack([up[rows] for rows in owners])
    right, left, left_conj, right_conj = patch_tables(width)

    scratch = (
        pltpu.VMEM((groups, 3, length, half), F32),
        pltpu.VMEM((groups, 3, pair, half), F32),
        pltpu.VMEM((groups, 2, half, length), F32),
        pltpu.VMEM((groups, 8, length), F32),
    )
    unroll = 2 if groups <= 2 else 1

    def swap(value):
        return lax.ppermute(value, "ang", [(i, i ^ 1) for i in range(ang)])

    def from_peer(value, j):
        return lax.ppermute(value, "ang", [((i + 2 * j) % ang, i) for i in range(ang)])

    def to_peer(value, j):
        return lax.ppermute(value, "ang", [(i, (i + 2 * j) % ang) for i in range(ang)])

    image = lax.all_to_all(
        jnp.broadcast_to(phase, (tiles, slices, length)), "tile", split_axis=0, concat_axis=0, tiled=True
    ).reshape(tiles * slices, length)
    angles = jnp.concatenate([angle_index] + [from_peer(angle_index, j) for j in range(1, groups)])

    flat = volume.reshape(share * slices, length)
    sides = [
        pl.BlockSpec((share * slices, half), functools.partial(lambda side, _: (0, side), side))
        for side in range(2)
    ]
    own = call(
        prepare_kernel,
        shape((slices, share, length), BF16),
        sides,
        flat, flat,
        grid=(1,),
        name="to_slices",
    )
    other = swap(own)

    edge_count = tiles - 1
    before = lax.ppermute(own[-1], "tile", [(i, i + 1) for i in range(edge_count)])
    after = lax.ppermute(own[0], "tile", [(i + 1, i) for i in range(edge_count)])
    base, base_sent = call(
        base_kernel,
        (shape((slices, share, length), F32), shape((slices, share, length), BF16)),
        sides + [VMEM_SPEC] * 2,
        flat, flat, before, after,
        grid=(1,),
        name="smooth",
    )
    base_other = swap(base_sent)

    grad = call(
        gradient_kernel,
        shape((tiles * slices, length), BF16),
        [SMEM_SPEC] + [VMEM_SPEC] * 8,
        offsets, image, intensity[0], probe_real, probe_imag, right, left, left_conj, right_conj,
        name="gradient",
    ).reshape(tiles, slices, length)
    grad = lax.all_to_all(grad, "tile", split_axis=0, concat_axis=0, tiled=True)

    lines = call(
        functools.partial(project_kernel, unroll),
        shape((groups, slices, length), F32),
        [SMEM_SPEC] + [VMEM_SPEC] * 6,
        angles, own, other, forward, inverse, down_part, up,
        scratch=scratch,
        name="project_old",
    )
    old = [lines[0]] + [to_peer(lines[j], j) for j in range(1, groups)]

    phase_new, spectrum = call(
        functools.partial(phase_kernel, groups),
        (shape((slices, length), F32), shape((slices, length), F32)),
        [VMEM_SPEC] * (5 + groups),
        grad, phase[0], dual[0], forward_full, inverse_full, *old,
        name="phase_step",
    )
    spectra = jnp.stack([spectrum] + [from_peer(spectrum, j) for j in range(1, groups)])

    mine = call(
        functools.partial(back_kernel, unroll),
        shape((slices, pair, length), BF16),
        [SMEM_SPEC] + [VMEM_SPEC] * 5,
        angles, spectra, forward, inverse, down, up_part,
        scratch=scratch,
        name="backproject",
    )
    theirs = swap(mine)
    volume_new, lines = call(
        functools.partial(update_kernel, unroll),
        (shape((share * slices, length), F32), shape((groups, slices, length), F32)),
        [SMEM_SPEC] + [VMEM_SPEC] * 8,
        angles, base, base_other, mine, theirs, forward, inverse, down_part, up,
        scratch=scratch + ([pltpu.VMEM((share * slices, half), F32)] * 2,),
        name="project_new",
    )
    new = [lines[0]] + [to_peer(lines[j], j) for j in range(1, groups)]
    dual_new = call(
        functools.partial(dual_kernel, groups),
        shape((slices, length), F32),
        [VMEM_SPEC] * (3 + groups),
        phase_new, dual[0], inverse_full, *new,
        name="dual_step",
    )
    return phase_new[None], volume_new.reshape(share, slices, length), dual_new[None]


def solution(mesh):
    placed = (
        P("ang", "tile", None),
        P("ang", "tile", None),
        P("ang", "tile", None),
        P(),
        P(),
        P("ang", "tile", None, None),
        P("ang", "tile"),
        P("ang"),
    )
    return jax.shard_map(
        shards,
        mesh=mesh,
        in_specs=placed,
        out_specs=(P("ang", "tile", None), P("ang", "tile", None), P("ang", "tile", None)),
        check_vma=False,
    )
```

```python
import functools
import math

import jax
import jax.numpy as jnp
import numpy as np
from jax import lax
from jax.experimental import pallas as pl
from jax.experimental.pallas import tpu as pltpu
from jax.sharding import PartitionSpec as P

angle_center = 90.0
rho_weight = 1.0
eta_step = 0.01
tau_step = 1.0
smooth_weight = 0.25

F32 = jnp.float32
BF16 = jnp.bfloat16
VMEM_SPEC = pl.BlockSpec(memory_space=pltpu.VMEM)
SMEM_SPEC = pl.BlockSpec(memory_space=pltpu.SMEM)
VMEM_LIMIT = 40 * 1024 * 1024


def table_pair(length):
    index = np.arange(length)
    phases = (index[:, None] * index[None, :] % length) * (2.0 * np.pi / length)
    return np.cos(phases).astype(np.float32), np.sin(phases).astype(np.float32)


def packed_tables(length):
    half = length // 2
    cos_t, sin_t = table_pair(length)
    bf = np.asarray(jnp.bfloat16).dtype if False else jnp.bfloat16
    out = []
    for kind in (np.float32, bf):
        c = cos_t.astype(kind).astype(np.float32)
        s = sin_t.astype(kind).astype(np.float32)
        forward = np.concatenate([c[:, : half + 1], -s[:, 1:half]], axis=1)
        weight = np.full((length, 1), 2.0 / length, np.float32)
        weight[0] = weight[half] = 1.0 / length
        inverse = forward.T * weight
        out.append((forward.astype(kind), inverse.astype(kind)))
    return out


def split_pair(array):
    high = array.astype(jnp.bfloat16)
    low = (array - high.astype(np.float32)).astype(jnp.bfloat16)
    return np.stack([high, low])


def patch_tables(width):
    cos_t, sin_t = table_pair(width)
    c = cos_t / np.float32(math.sqrt(width))
    s = sin_t / np.float32(math.sqrt(width))
    right = np.block([[c, -s], [s, c]])
    left = np.block([[c, s], [-s, c]])
    right_conj = np.block([[c, s], [-s, c]])
    left_conj = np.block([[c, -s], [s, c]])
    return tuple(split_pair(m.astype(np.float32)) for m in (right, left, left_conj, right_conj))


def dot(left, right):
    return jnp.dot(left, right, preferred_element_type=F32)


def dot_high(left, right):
    return jnp.dot(left, right, precision=lax.Precision.HIGHEST, preferred_element_type=F32)


def dot_split(left, right):
    def parts(value):
        if value.dtype == BF16:
            return value[0], value[1]
        high = value.astype(BF16)
        return high, (value - high.astype(F32)).astype(BF16)

    left_high, left_low = parts(left)
    right_high, right_low = parts(right)
    return dot(left_high, right_high) + dot(left_low, right_high) + dot(left_high, right_low)


def turn(re, im, c1, s, c2, sign):
    if sign > 0:
        return re * c1 + im * s, im * c2 - re * s
    return re * c1 - im * s, im * c2 + re * s


def fill_turn_tables(angle, length, row_ref, col_ref, nyq_ref):
    half = length // 2
    unit = 2.0 * math.pi / length
    theta = (jnp.full((8, half), angle, jnp.int32).astype(F32) - angle_center) * (math.pi / 360.0)
    coef_a = -(jnp.sin(0.5 * theta) / jnp.cos(0.5 * theta))
    coef_b = jnp.sin(theta)

    lane = lax.broadcasted_iota(jnp.int32, (8, half), 1)
    sub = lax.broadcasted_iota(jnp.int32, (8, half), 0)
    freq = jnp.where(lane == 0, half, lane).astype(F32)
    phase = unit * coef_a * freq
    base = phase * sub.astype(F32)
    base_c, base_s = jnp.cos(base), jnp.sin(base)
    for block in range(length // 64):
        first = 8 * block * 8 - half
        step = phase * (first + 8 * sub).astype(F32)
        step_c, step_s = jnp.cos(step), jnp.sin(step)
        for q in range(8):
            sc, ss = step_c[q : q + 1], step_s[q : q + 1]
            c2 = base_c * sc - base_s * ss
            s = base_s * sc + base_c * ss
            rows = pl.ds((block * 8 + q) * 8, 8)
            row_ref[0, rows, :] = jnp.where(lane == 0, 1.0, c2)
            row_ref[1, rows, :] = jnp.where(lane == 0, 0.0, s)
            row_ref[2, rows, :] = c2

    for side in range(2):
        place = (lane + (side * half - half)).astype(F32)
        phase = unit * coef_b * place
        lanes = slice(side * half, side * half + half)
        base = phase * sub.astype(F32)
        base_c, base_s = jnp.cos(base), jnp.sin(base)
        for block in range(half // 64):
            step = phase * (block * 64 + 8 * sub).astype(F32)
            step_c, step_s = jnp.cos(step), jnp.sin(step)
            for q in range(8):
                sc, ss = step_c[q : q + 1], step_s[q : q + 1]
                rows = pl.ds((block * 8 + q) * 8, 8)
                col_ref[0, rows, lanes] = base_c * sc - base_s * ss
                col_ref[1, rows, lanes] = base_s * sc + base_c * ss
        top = jnp.where(sub == 0, jnp.cos(phase * float(half)), base_c)
        nyq_ref[:, lanes] = top


class Tables:
    def __init__(self, row, col, nyq):
        self.row, self.col, self.nyq = row, col, nyq

    def rows(self):
        return self.row[0], self.row[1], self.row[2]

    def chip_rows(self, share):
        here = lax.axis_index("ang")
        other = here + 1 - 2 * lax.rem(here, 2)
        places = [pl.ds(pl.multiple_of(which * share, 8), share) for which in (here, other)]
        return tuple(jnp.concatenate([self.row[part, rows, :] for rows in places], axis=0) for part in range(3))

    def columns(self):
        c1 = self.col[0]
        return c1, self.col[1], jnp.concatenate([self.nyq[...], c1[8:]], axis=0)


def turn_rows(spectrum, tables, sign):
    half = spectrum.shape[1] // 2
    return turn(spectrum[:, :half], spectrum[:, half:], *tables, sign)


def turn_columns(spectrum, tables, sign):
    half = spectrum.shape[0] // 2
    pair = turn(spectrum[:half], spectrum[half:], *tables, sign)
    return jnp.concatenate(pair, axis=0).astype(BF16)


def side_by_side(value, count):
    rows = value.shape[0] // count
    return jnp.concatenate([value[i * rows : (i + 1) * rows] for i in range(count)], axis=1)


def stacked(value, count):
    columns = value.shape[1] // count
    return jnp.concatenate([value[:, i * columns : (i + 1) * columns] for i in range(count)], axis=0)


def block_of(value, i, count, axis):
    size = value.shape[axis] // count
    return lax.slice_in_dim(value, i * size, (i + 1) * size, axis=axis)


def project_slices(slab, count, share, tables, consts, lines_refs):
    forward_ref, inverse_ref, down_ref, up_ref = consts
    here = lax.axis_index("ang")
    spectrum = dot(slab, forward_ref[...])
    for table, lines_ref in zip(tables, lines_refs):
        chip_rows = table.chip_rows(share)
        turned = [
            jnp.concatenate(turn_rows(block_of(spectrum, i, count, 0), chip_rows, 1), axis=1).astype(BF16)
            for i in range(count)
        ]
        first = dot(jnp.concatenate(turned, axis=0), inverse_ref[...]).astype(BF16)
        columns = dot(down_ref[here], side_by_side(first, count))
        turned = [turn_columns(block_of(columns, i, count, 1), table.columns(), 1) for i in range(count)]
        second = dot(up_ref[...], jnp.concatenate(turned, axis=1)).astype(BF16)
        last = dot(stacked(second, count), forward_ref[...])
        for i in range(count):
            re, im = turn_rows(block_of(last, i, count, 0), table.rows(), 1)
            sums = [jnp.sum(part, axis=0, keepdims=True) for part in (re, im)]
            lines_ref[pl.ds(i, 1), :] = jnp.concatenate(sums, axis=1)


def take(refs, *counts):
    refs, out = list(refs), []
    for count in counts:
        out.append(refs[:count])
        refs = refs[count:]
    return out


def as_tables(refs):
    return [Tables(*refs[i : i + 3]) for i in range(0, len(refs), 3)]


def project_kernel(groups, slices, *refs):
    angle_refs, sides, consts, lines_refs, bases, edges, table_refs = take(
        refs, groups, 4, 4, groups, 2, 2, 3 * groups
    )
    share = sides[0].shape[0] // slices
    length = consts[0].shape[0]
    for g in range(groups):
        fill_turn_tables(angle_refs[g][0], length, *table_refs[3 * g : 3 * g + 3])

    def rows(z):
        parts = [ref[pl.ds(z, share, stride=slices), :] for ref in sides]
        return [jnp.concatenate(parts[:2], axis=1), jnp.concatenate(parts[2:], axis=1)]

    slab = []
    past = None
    now = rows(0)
    for z in range(slices):
        later = rows(z + 1) if z + 1 < slices else None
        for place in range(2):
            slab.append(now[place].astype(BF16))
            near = [side[place] for side in (past, later) if side is not None]
            base = (1.0 - 2.0 * tau_step * smooth_weight) * now[place]
            base = base + (tau_step * smooth_weight) * sum(near[1:], near[0])
            bases[place][z] = base.astype(bases[place].dtype)
        past, now = now, later
    for edge_ref, part in zip(edges, (slab[-2:], slab[:2])):
        edge_ref[...] = jnp.concatenate(part, axis=0)
    project_slices(
        jnp.concatenate(slab, axis=0), slices, share, as_tables(table_refs), consts, lines_refs
    )


def back_kernel(groups, *refs):
    spectra_refs, consts, table_refs, (out_ref,) = take(refs, groups, 4, 3 * groups, 1)
    forward_ref, inverse_ref, down_ref, up_ref = consts
    slices, pair, length = out_ref.shape
    half = length // 2
    here = lax.axis_index("ang")
    totals = None
    for table, spectra_ref in zip(as_tables(table_refs), spectra_refs):
        turned = []
        for z in range(slices):
            line = spectra_ref[pl.ds(z, 1), :]
            pieces = turn(line[:, :half], line[:, half:], *table.rows(), -1)
            turned.append(jnp.concatenate(pieces, axis=1).astype(BF16))
        spread = dot(jnp.concatenate(turned, axis=0), inverse_ref[...]).astype(BF16)
        columns = dot(down_ref[...], side_by_side(spread, slices))
        turned = [turn_columns(block_of(columns, i, slices, 1), table.columns(), -1) for i in range(slices)]
        second = dot(up_ref[here], jnp.concatenate(turned, axis=1)).astype(BF16)
        last = dot(stacked(second, slices), forward_ref[...])
        chip_rows = table.chip_rows(pair // 2)
        turned = [
            jnp.concatenate(turn_rows(block_of(last, i, slices, 0), chip_rows, -1), axis=1)
            for i in range(slices)
        ]
        totals = turned if totals is None else [old + new for old, new in zip(totals, turned)]
    total = jnp.concatenate([value.astype(BF16) for value in totals], axis=0)
    out_ref[...] = dot(total, inverse_ref[...]).astype(BF16).reshape(out_ref.shape)


def update_kernel(groups, first, last, aliased, *refs):
    bases, halos, shares, consts, table_refs, unused, (volume_ref,), lines_refs, sides = take(
        refs, 2, 2, 2, 4, 3 * groups, aliased, 1, groups, 2
    )
    own_ref, other_ref = bases
    mine_ref, theirs_ref = shares
    slices, share, length = own_ref.shape
    half = length // 2
    slab = []
    for z in range(slices):
        own = own_ref[z] - tau_step * (
            mine_ref[z, :share, :].astype(F32) + theirs_ref[z, share:, :].astype(F32)
        )
        other = other_ref[z].astype(F32) - tau_step * (
            mine_ref[z, share:, :].astype(F32) + theirs_ref[z, :share, :].astype(F32)
        )
        for needed, halo_ref in ((first and z == 0, halos[0]), (last and z == slices - 1, halos[1])):
            if needed:
                halo = (tau_step * smooth_weight) * halo_ref[...].astype(F32)
                own, other = own + halo[:share], other + halo[share:]
        for side in range(2):
            sides[side][pl.ds(z, share, stride=slices), :] = own[:, side * half : (side + 1) * half]
        slab += [own.astype(BF16), other.astype(BF16)]
    project_slices(
        jnp.concatenate(slab, axis=0), slices, share, as_tables(table_refs), consts, lines_refs
    )
    whole = jnp.concatenate([ref[...] for ref in sides], axis=1)
    volume_ref[...] = whole.reshape(volume_ref.shape)


def gradient_kernel(
    offsets_ref, image_ref, measured_ref, probe_r_ref, probe_i_ref,
    right_ref, left_ref, left_conj_ref, right_conj_ref, out_ref,
):
    positions, height, width = measured_ref.shape
    length = image_ref.shape[1]
    image = image_ref[...]
    cos_image, sin_image = jnp.cos(image), jnp.sin(image)
    probe_r, probe_i = probe_r_ref[...], probe_i_ref[...]
    waves = []
    for p in range(positions):
        back = length - offsets_ref[0, p]
        cos_p = pltpu.roll(cos_image, back, 1)[:, :width]
        sin_p = pltpu.roll(sin_image, back, 1)[:, :width]
        waves.append((probe_r * cos_p - probe_i * sin_p, probe_r * sin_p + probe_i * cos_p))

    def to_columns(value):
        parts = [block_of(value, p, positions, 0) for p in range(positions)]
        return jnp.concatenate(
            [jnp.concatenate([part[:, i * width : (i + 1) * width] for part in parts], axis=1) for i in range(2)],
            axis=0,
        )

    def to_rows(value):
        parts = [block_of(value, p, positions, 1) for p in range(positions)]
        return jnp.concatenate(
            [jnp.concatenate([part[:height], part[height:]], axis=1) for part in parts], axis=0
        )

    entry = jnp.concatenate([jnp.concatenate(wave, axis=1) for wave in waves], axis=0)
    far = dot_split(left_ref[...], to_columns(dot_split(entry, right_ref[...])))
    far_r, far_i = far[:height], far[height:]
    measured = jnp.concatenate([measured_ref[p] for p in range(positions)], axis=1)
    misfit = far_r * far_r + far_i * far_i - measured
    weighted = jnp.concatenate([misfit * far_r, misfit * far_i], axis=0)
    chi = dot_split(to_rows(dot_split(left_conj_ref[...], weighted)), right_conj_ref[...])
    total = jnp.zeros((height, length), F32)
    for p in range(positions):
        part = block_of(chi, p, positions, 0)
        wave_r, wave_i = waves[p]
        term = 2.0 * (part[:, width:] * wave_r - part[:, :width] * wave_i)
        padded = jnp.concatenate([term, jnp.zeros((height, length - width), F32)], axis=1)
        total = total + pltpu.roll(padded, offsets_ref[0, p], 1)
    out_ref[...] = total.astype(out_ref.dtype).reshape(out_ref.shape)


def projected(line_refs, inverse_ref):
    line = line_refs[0][...]
    for other in line_refs[1:]:
        line = line + other[...]
    return dot_split(line, inverse_ref[...]) * (1.0 / math.sqrt(line.shape[1]))


def line_kernel(peers, phase_ref, dual_ref, inverse_ref, *refs):
    line_refs, (phase_part_ref, resid_part_ref) = take(refs, peers, 2)
    proj_old = projected(line_refs, inverse_ref)
    phase, dual = phase_ref[...], dual_ref[...]
    phase_part = phase - eta_step * (dual + rho_weight * (phase - proj_old))
    phase_part_ref[...] = phase_part
    resid_part_ref[...] = rho_weight * (proj_old - phase_part) - dual


def phase_kernel(grad_ref, phase_part_ref, resid_part_ref, forward_ref, phase_new_ref, spectrum_ref):
    grad = grad_ref[0].astype(F32)
    for t in range(1, grad_ref.shape[0]):
        grad = grad + grad_ref[t].astype(F32)
    grad = eta_step * grad
    phase_new_ref[...] = phase_part_ref[...] - grad
    resid = resid_part_ref[...] + rho_weight * grad
    spectrum_ref[...] = dot_split(resid, forward_ref[...]) * (1.0 / math.sqrt(resid.shape[1]))


def dual_kernel(peers, phase_ref, dual_ref, inverse_ref, *refs):
    line_refs, (dual_new_ref,) = take(refs, peers, 1)
    proj_new = projected(line_refs, inverse_ref)
    dual_new_ref[...] = dual_ref[...] + rho_weight * (phase_ref[...] - proj_new)


def call(kernel, outs, args, specs=None, out_specs=None, scratch=(), flops=0, name=None, grid=(), aliases=None):
    return pl.pallas_call(
        kernel,
        grid=grid,
        out_shape=tuple(outs),
        in_specs=specs or [VMEM_SPEC] * len(args),
        out_specs=tuple(out_specs or [VMEM_SPEC] * len(outs)),
        scratch_shapes=list(scratch),
        input_output_aliases=aliases or {},
        cost_estimate=pl.CostEstimate(flops=flops, bytes_accessed=1 << 20, transcendentals=0),
        name=name,
        compiler_params=pltpu.CompilerParams(vmem_limit_bytes=VMEM_LIMIT),
    )(*args)


def shards(volume, phase, dual, probe_real, probe_imag, intensity, offsets, angle_index):
    share, slices, length = volume.shape
    width = probe_real.shape[1]
    half = length // 2
    ang = lax.axis_size("ang")
    tiles = lax.axis_size("tile")
    groups = ang // 2
    pair = 2 * share
    parts = 2 if slices % 16 == 0 else 1
    some = slices // parts
    shape = jax.ShapeDtypeStruct

    (forward_full, inverse_full), (forward, inverse) = packed_tables(length)
    forward_full, inverse_full = split_pair(forward_full), split_pair(inverse_full)
    down, up = forward.T, inverse.T
    owners = [
        np.r_[i * share : (i + 1) * share, (i ^ 1) * share : ((i ^ 1) + 1) * share] for i in range(ang)
    ]
    down_part = np.stack([down[:, rows] for rows in owners])
    up_part = np.stack([up[rows] for rows in owners])
    right, left, left_conj, right_conj = patch_tables(width)
    line = shape((slices, length), F32)
    work = 2 * 2 * length * length * length * slices * groups

    def swap(value):
        return lax.ppermute(value, "ang", [(i, i ^ 1) for i in range(ang)])

    def from_peer(value, j):
        return lax.ppermute(value, "ang", [((i + 2 * j) % ang, i) for i in range(ang)])

    def to_peer(value, j):
        return lax.ppermute(value, "ang", [(i, (i + 2 * j) % ang) for i in range(ang)])

    def lanes(side):
        return pl.BlockSpec((share * slices, half), lambda _: (0, side))

    def gathered(lines):
        return [lines[0]] + [to_peer(lines[j], j) for j in range(1, groups)]

    image = lax.all_to_all(
        jnp.broadcast_to(phase, (tiles, slices, length)), "tile", split_axis=0, concat_axis=0, tiled=True
    ).reshape(tiles * slices, length)
    flat = volume.reshape(share * slices, length)
    other = swap(flat)
    angles = [angle_index] + [from_peer(angle_index, j) for j in range(1, groups)]

    tables_shape = [
        shape((3, length, half), F32), shape((2, half, length), F32), shape((8, length), F32)
    ] * groups
    outs = call(
        functools.partial(project_kernel, groups, slices),
        [line] * groups
        + [shape((slices, share, length), F32), shape((slices, share, length), BF16)]
        + [shape((pair, length), BF16)] * 2
        + tables_shape,
        angles + [flat, flat, other, other, forward, inverse, down_part, up],
        [SMEM_SPEC] * groups + [lanes(0), lanes(1)] * 2 + [VMEM_SPEC] * 4,
        grid=(1,),
        flops=3 * work,
        name="project_old",
    )
    lines, bases, edges, tables = take(outs, groups, 2, 2, 3 * groups)
    old = gathered(lines)

    image, edges = lax.optimization_barrier((image, edges))
    (grad,) = call(
        gradient_kernel,
        [shape((tiles, slices, length), BF16)],
        [offsets, image, intensity[0], probe_real, probe_imag, right, left, left_conj, right_conj],
        [SMEM_SPEC] + [VMEM_SPEC] * 8,
        flops=2 * work,
        name="gradient",
    )
    grad, edges = lax.optimization_barrier((grad, edges))
    grad = lax.all_to_all(grad, "tile", split_axis=0, concat_axis=0, tiled=True)

    before = lax.ppermute(edges[0], "tile", [(i, i + 1) for i in range(tiles - 1)])
    after = lax.ppermute(edges[1], "tile", [(i + 1, i) for i in range(tiles - 1)])

    phase_part, resid_part = call(
        functools.partial(line_kernel, groups), [line, line], [phase[0], dual[0], inverse_full] + old,
        name="line_step",
    )
    grad, before, after = lax.optimization_barrier((grad, before, after))
    phase_new, spectrum = call(
        phase_kernel, [line, line], [grad, phase_part, resid_part, forward_full], name="phase_step"
    )
    spectra = [spectrum] + [from_peer(spectrum, j) for j in range(1, groups)]

    halves = []
    for h in range(parts):
        (mine,) = call(
            functools.partial(back_kernel, groups),
            [shape((some, pair, length), BF16)],
            spectra + [forward, inverse, down, up_part] + tables,
            [pl.BlockSpec((some, length), lambda _, h=h: (h, 0))] * groups + [VMEM_SPEC] * (4 + 3 * groups),
            grid=(1,),
            flops=3 * work // parts,
            name="backproject",
        )
        halves.append((mine, swap(mine)))

    results = []
    for h in range(parts):
        block = pl.BlockSpec((some, share, length), lambda _, h=h: (h, 0, 0))
        args = bases + [before, after] + list(halves[h]) + [forward, inverse, down_part, up] + tables
        results = call(
            functools.partial(update_kernel, groups, h == 0, h == parts - 1, len(results)),
            [shape((share, slices, length), F32)] + [line] * groups,
            args + list(results),
            [block] * 2 + [VMEM_SPEC] * (8 + 3 * groups) + [pl.BlockSpec(memory_space=pl.ANY)] * len(results),
            [pl.BlockSpec((share, some, length), lambda _, h=h: (0, h, 0))]
            + [pl.BlockSpec((some, length), lambda _, h=h: (h, 0))] * groups,
            scratch=[pltpu.VMEM((share * some, half), F32)] * 2,
            grid=(1,),
            flops=3 * work // parts,
            aliases={len(args) + i: i for i in range(len(results))},
            name="project_new",
        )
    volume_new, lines = results[0], results[1:]
    (dual_new,) = call(
        functools.partial(dual_kernel, groups), [line],
        [phase_new, dual[0], inverse_full] + gathered(lines),
        name="dual_step",
    )
    return phase_new[None], volume_new, dual_new[None]


def solution(mesh):
    placed = (
        P("ang", "tile", None),
        P("ang", "tile", None),
        P("ang", "tile", None),
        P(),
        P(),
        P("ang", "tile", None, None),
        P("ang", "tile"),
        P("ang"),
    )
    return jax.shard_map(
        shards,
        mesh=mesh,
        in_specs=placed,
        out_specs=(P("ang", "tile", None), P("ang", "tile", None), P("ang", "tile", None)),
        check_vma=False,
    )
```

```python
import functools
import math

import jax
import jax.numpy as jnp
import numpy as np
from jax import lax
from jax.experimental import pallas as pl
from jax.experimental.pallas import tpu as pltpu
from jax.sharding import PartitionSpec as P

angle_center = 90.0
rho_weight = 1.0
eta_step = 0.01
tau_step = 1.0
smooth_weight = 0.25

F32 = jnp.float32
BF16 = jnp.bfloat16
VMEM_SPEC = pl.BlockSpec(memory_space=pltpu.VMEM)
SMEM_SPEC = pl.BlockSpec(memory_space=pltpu.SMEM)
MIB = 1024 * 1024


def table_pair(length):
    index = np.arange(length)
    phases = (index[:, None] * index[None, :] % length) * (2.0 * np.pi / length)
    return np.cos(phases).astype(np.float32), np.sin(phases).astype(np.float32)


def packed_tables(length):
    half = length // 2
    cos_t, sin_t = table_pair(length)
    bf = np.asarray(jnp.bfloat16).dtype if False else jnp.bfloat16
    out = []
    for kind in (np.float32, bf):
        c = cos_t.astype(kind).astype(np.float32)
        s = sin_t.astype(kind).astype(np.float32)
        forward = np.concatenate([c[:, : half + 1], -s[:, 1:half]], axis=1)
        weight = np.full((length, 1), 2.0 / length, np.float32)
        weight[0] = weight[half] = 1.0 / length
        inverse = forward.T * weight
        out.append((forward.astype(kind), inverse.astype(kind)))
    return out


def split_pair(array):
    high = array.astype(jnp.bfloat16)
    low = (array - high.astype(np.float32)).astype(jnp.bfloat16)
    return np.stack([high, low])


def patch_tables(width):
    cos_t, sin_t = table_pair(width)
    c = cos_t / np.float32(math.sqrt(width))
    s = sin_t / np.float32(math.sqrt(width))
    right = np.block([[c, -s], [s, c]])
    left = np.block([[c, s], [-s, c]])
    right_conj = np.block([[c, s], [-s, c]])
    left_conj = np.block([[c, -s], [s, c]])
    return tuple(split_pair(m.astype(np.float32)) for m in (right, left, left_conj, right_conj))


def dot(left, right):
    return jnp.dot(left, right, preferred_element_type=F32)


def dot_high(left, right):
    return jnp.dot(left, right, precision=lax.Precision.HIGHEST, preferred_element_type=F32)


def dot_split(left, right):
    def parts(value):
        if value.dtype == BF16:
            return value[0], value[1]
        high = value.astype(BF16)
        return high, (value - high.astype(F32)).astype(BF16)

    left_high, left_low = parts(left)
    right_high, right_low = parts(right)
    return dot(left_high, right_high) + dot(left_low, right_high) + dot(left_high, right_low)


def turn(re, im, c1, s, c2, sign):
    if sign > 0:
        return re * c1 + im * s, im * c2 - re * s
    return re * c1 - im * s, im * c2 + re * s


def fill_turn_tables(angle, length, row_ref, col_ref, nyq_ref):
    half = length // 2
    unit = 2.0 * math.pi / length
    theta = (jnp.full((8, half), angle, jnp.int32).astype(F32) - angle_center) * (math.pi / 360.0)
    coef_a = -(jnp.sin(0.5 * theta) / jnp.cos(0.5 * theta))
    coef_b = jnp.sin(theta)

    lane = lax.broadcasted_iota(jnp.int32, (8, half), 1)
    sub = lax.broadcasted_iota(jnp.int32, (8, half), 0)
    freq = jnp.where(lane == 0, half, lane).astype(F32)
    phase = unit * coef_a * freq
    base = phase * sub.astype(F32)
    base_c, base_s = jnp.cos(base), jnp.sin(base)
    for block in range(length // 64):
        first = 8 * block * 8 - half
        step = phase * (first + 8 * sub).astype(F32)
        step_c, step_s = jnp.cos(step), jnp.sin(step)
        for q in range(8):
            sc, ss = step_c[q : q + 1], step_s[q : q + 1]
            c2 = base_c * sc - base_s * ss
            s = base_s * sc + base_c * ss
            rows = pl.ds((block * 8 + q) * 8, 8)
            row_ref[0, rows, :] = jnp.where(lane == 0, 1.0, c2)
            row_ref[1, rows, :] = jnp.where(lane == 0, 0.0, s)
            row_ref[2, rows, :] = c2

    for side in range(2):
        place = (lane + (side * half - half)).astype(F32)
        phase = unit * coef_b * place
        lanes = slice(side * half, side * half + half)
        base = phase * sub.astype(F32)
        base_c, base_s = jnp.cos(base), jnp.sin(base)
        for block in range(half // 64):
            step = phase * (block * 64 + 8 * sub).astype(F32)
            step_c, step_s = jnp.cos(step), jnp.sin(step)
            for q in range(8):
                sc, ss = step_c[q : q + 1], step_s[q : q + 1]
                rows = pl.ds((block * 8 + q) * 8, 8)
                col_ref[0, rows, lanes] = base_c * sc - base_s * ss
                col_ref[1, rows, lanes] = base_s * sc + base_c * ss
        top = jnp.where(sub == 0, jnp.cos(phase * float(half)), base_c)
        nyq_ref[:, lanes] = top


class Tables:
    def __init__(self, row, col, nyq):
        self.row, self.col, self.nyq = row, col, nyq

    def rows(self):
        return self.row[0], self.row[1], self.row[2]

    def chip_rows(self, share):
        here = lax.axis_index("ang")
        other = here + 1 - 2 * lax.rem(here, 2)
        places = [pl.ds(pl.multiple_of(which * share, 8), share) for which in (here, other)]
        return tuple(jnp.concatenate([self.row[part, rows, :] for rows in places], axis=0) for part in range(3))

    def columns(self):
        c1 = self.col[0]
        return c1, self.col[1], jnp.concatenate([self.nyq[...], c1[8:]], axis=0)


def turn_rows(spectrum, tables, sign):
    half = spectrum.shape[1] // 2
    return turn(spectrum[:, :half], spectrum[:, half:], *tables, sign)


def turn_columns(spectrum, tables, sign):
    half = spectrum.shape[0] // 2
    pair = turn(spectrum[:half], spectrum[half:], *tables, sign)
    return jnp.concatenate(pair, axis=0).astype(BF16)


def side_by_side(value, count):
    rows = value.shape[0] // count
    return jnp.concatenate([value[i * rows : (i + 1) * rows] for i in range(count)], axis=1)


def stacked(value, count):
    columns = value.shape[1] // count
    return jnp.concatenate([value[:, i * columns : (i + 1) * columns] for i in range(count)], axis=0)


def block_of(value, i, count, axis):
    size = value.shape[axis] // count
    return lax.slice_in_dim(value, i * size, (i + 1) * size, axis=axis)


def project_slices(slab, count, share, tables, consts, lines_refs):
    forward_ref, inverse_ref, down_ref, up_ref = consts
    here = lax.axis_index("ang")
    spectrum = dot(slab, forward_ref[...])
    for table, lines_ref in zip(tables, lines_refs):
        chip_rows = table.chip_rows(share)
        turned = [
            jnp.concatenate(turn_rows(block_of(spectrum, i, count, 0), chip_rows, 1), axis=1).astype(BF16)
            for i in range(count)
        ]
        first = dot(jnp.concatenate(turned, axis=0), inverse_ref[...]).astype(BF16)
        columns = dot(down_ref[here], side_by_side(first, count))
        turned = [turn_columns(block_of(columns, i, count, 1), table.columns(), 1) for i in range(count)]
        second = dot(up_ref[...], jnp.concatenate(turned, axis=1)).astype(BF16)
        last = dot(stacked(second, count), forward_ref[...])
        for i in range(count):
            re, im = turn_rows(block_of(last, i, count, 0), table.rows(), 1)
            sums = [jnp.sum(part, axis=0, keepdims=True) for part in (re, im)]
            lines_ref[pl.ds(i, 1), :] = jnp.concatenate(sums, axis=1)


def take(refs, *counts):
    refs, out = list(refs), []
    for count in counts:
        out.append(refs[:count])
        refs = refs[count:]
    return out


def as_tables(refs):
    return [Tables(*refs[i : i + 3]) for i in range(0, len(refs), 3)]


def project_kernel(groups, slices, *refs):
    angle_refs, sides, consts, lines_refs, bases, edges, table_refs = take(
        refs, groups, 4, 4, groups, 2, 2, 3 * groups
    )
    share = sides[0].shape[0] // slices
    length = consts[0].shape[0]
    for g in range(groups):
        fill_turn_tables(angle_refs[g][0], length, *table_refs[3 * g : 3 * g + 3])

    def rows(z):
        parts = [ref[pl.ds(z, share, stride=slices), :] for ref in sides]
        return [jnp.concatenate(parts[:2], axis=1), jnp.concatenate(parts[2:], axis=1)]

    slab = []
    past = None
    now = rows(0)
    for z in range(slices):
        later = rows(z + 1) if z + 1 < slices else None
        for place in range(2):
            slab.append(now[place].astype(BF16))
            near = [side[place] for side in (past, later) if side is not None]
            base = (1.0 - 2.0 * tau_step * smooth_weight) * now[place]
            base = base + (tau_step * smooth_weight) * sum(near[1:], near[0])
            bases[place][z] = base.astype(bases[place].dtype)
        past, now = now, later
    for edge_ref, part in zip(edges, (slab[-2:], slab[:2])):
        edge_ref[...] = jnp.concatenate(part, axis=0)
    project_slices(
        jnp.concatenate(slab, axis=0), slices, share, as_tables(table_refs), consts, lines_refs
    )


def back_kernel(groups, *refs):
    spectra_refs, consts, table_refs, (out_ref,) = take(refs, groups, 4, 3 * groups, 1)
    forward_ref, inverse_ref, down_ref, up_ref = consts
    slices, pair, length = out_ref.shape
    half = length // 2
    here = lax.axis_index("ang")
    totals = None
    for table, spectra_ref in zip(as_tables(table_refs), spectra_refs):
        turned = []
        for z in range(slices):
            line = spectra_ref[pl.ds(z, 1), :]
            pieces = turn(line[:, :half], line[:, half:], *table.rows(), -1)
            turned.append(jnp.concatenate(pieces, axis=1).astype(BF16))
        spread = dot(jnp.concatenate(turned, axis=0), inverse_ref[...]).astype(BF16)
        columns = dot(down_ref[...], side_by_side(spread, slices))
        turned = [turn_columns(block_of(columns, i, slices, 1), table.columns(), -1) for i in range(slices)]
        second = dot(up_ref[here], jnp.concatenate(turned, axis=1)).astype(BF16)
        last = dot(stacked(second, slices), forward_ref[...])
        chip_rows = table.chip_rows(pair // 2)
        turned = [
            jnp.concatenate(turn_rows(block_of(last, i, slices, 0), chip_rows, -1), axis=1)
            for i in range(slices)
        ]
        totals = turned if totals is None else [old + new for old, new in zip(totals, turned)]
    total = jnp.concatenate([value.astype(BF16) for value in totals], axis=0)
    out_ref[...] = dot(total, inverse_ref[...]).astype(BF16).reshape(out_ref.shape)


def update_kernel(groups, first, last, aliased, *refs):
    bases, halos, shares, consts, table_refs, unused, (volume_ref,), lines_refs, sides = take(
        refs, 2, 2, 2, 4, 3 * groups, aliased, 1, groups, 2
    )
    own_ref, other_ref = bases
    mine_ref, theirs_ref = shares
    slices, share, length = own_ref.shape
    half = length // 2
    slab = []
    for z in range(slices):
        own = own_ref[z] - tau_step * (
            mine_ref[z, :share, :].astype(F32) + theirs_ref[z, share:, :].astype(F32)
        )
        other = other_ref[z].astype(F32) - tau_step * (
            mine_ref[z, share:, :].astype(F32) + theirs_ref[z, :share, :].astype(F32)
        )
        for needed, halo_ref in ((first and z == 0, halos[0]), (last and z == slices - 1, halos[1])):
            if needed:
                halo = (tau_step * smooth_weight) * halo_ref[...].astype(F32)
                own, other = own + halo[:share], other + halo[share:]
        for side in range(2):
            sides[side][pl.ds(z, share, stride=slices), :] = own[:, side * half : (side + 1) * half]
        slab += [own.astype(BF16), other.astype(BF16)]
    project_slices(
        jnp.concatenate(slab, axis=0), slices, share, as_tables(table_refs), consts, lines_refs
    )
    whole = jnp.concatenate([ref[...] for ref in sides], axis=1)
    volume_ref[...] = whole.reshape(volume_ref.shape)


def gradient_kernel(
    offsets_ref, image_ref, measured_ref, probe_r_ref, probe_i_ref,
    right_ref, left_ref, left_conj_ref, right_conj_ref, out_ref,
):
    positions, height, width = measured_ref.shape
    length = image_ref.shape[1]
    image = image_ref[...]
    cos_image, sin_image = jnp.cos(image), jnp.sin(image)
    probe_r, probe_i = probe_r_ref[...], probe_i_ref[...]
    waves = []
    for p in range(positions):
        back = length - offsets_ref[0, p]
        cos_p = pltpu.roll(cos_image, back, 1)[:, :width]
        sin_p = pltpu.roll(sin_image, back, 1)[:, :width]
        waves.append((probe_r * cos_p - probe_i * sin_p, probe_r * sin_p + probe_i * cos_p))

    def to_columns(value):
        parts = [block_of(value, p, positions, 0) for p in range(positions)]
        return jnp.concatenate(
            [jnp.concatenate([part[:, i * width : (i + 1) * width] for part in parts], axis=1) for i in range(2)],
            axis=0,
        )

    def to_rows(value):
        parts = [block_of(value, p, positions, 1) for p in range(positions)]
        return jnp.concatenate(
            [jnp.concatenate([part[:height], part[height:]], axis=1) for part in parts], axis=0
        )

    entry = jnp.concatenate([jnp.concatenate(wave, axis=1) for wave in waves], axis=0)
    far = dot_split(left_ref[...], to_columns(dot_split(entry, right_ref[...])))
    far_r, far_i = far[:height], far[height:]
    measured = jnp.concatenate([measured_ref[p] for p in range(positions)], axis=1)
    misfit = far_r * far_r + far_i * far_i - measured
    weighted = jnp.concatenate([misfit * far_r, misfit * far_i], axis=0)
    chi = dot_split(to_rows(dot_split(left_conj_ref[...], weighted)), right_conj_ref[...])
    total = jnp.zeros((height, length), F32)
    for p in range(positions):
        part = block_of(chi, p, positions, 0)
        wave_r, wave_i = waves[p]
        term = 2.0 * (part[:, width:] * wave_r - part[:, :width] * wave_i)
        padded = jnp.concatenate([term, jnp.zeros((height, length - width), F32)], axis=1)
        total = total + pltpu.roll(padded, offsets_ref[0, p], 1)
    out_ref[...] = total.astype(out_ref.dtype).reshape(out_ref.shape)


def projected(line_refs, inverse_ref):
    line = line_refs[0][...]
    for other in line_refs[1:]:
        line = line + other[...]
    return dot_split(line, inverse_ref[...]) * (1.0 / math.sqrt(line.shape[1]))


def line_kernel(peers, phase_ref, dual_ref, inverse_ref, *refs):
    line_refs, (phase_part_ref, resid_part_ref) = take(refs, peers, 2)
    proj_old = projected(line_refs, inverse_ref)
    phase, dual = phase_ref[...], dual_ref[...]
    phase_part = phase - eta_step * (dual + rho_weight * (phase - proj_old))
    phase_part_ref[...] = phase_part
    resid_part_ref[...] = rho_weight * (proj_old - phase_part) - dual


def phase_kernel(grad_ref, phase_part_ref, resid_part_ref, forward_ref, phase_new_ref, spectrum_ref):
    grad = grad_ref[0].astype(F32)
    for t in range(1, grad_ref.shape[0]):
        grad = grad + grad_ref[t].astype(F32)
    grad = eta_step * grad
    phase_new_ref[...] = phase_part_ref[...] - grad
    resid = resid_part_ref[...] + rho_weight * grad
    spectrum_ref[...] = dot_split(resid, forward_ref[...]) * (1.0 / math.sqrt(resid.shape[1]))


def dual_kernel(peers, phase_ref, dual_ref, inverse_ref, *refs):
    line_refs, (dual_new_ref,) = take(refs, peers, 1)
    proj_new = projected(line_refs, inverse_ref)
    dual_new_ref[...] = dual_ref[...] + rho_weight * (phase_ref[...] - proj_new)


def call(kernel, outs, args, specs=None, out_specs=None, scratch=(), flops=0, name=None, grid=(), aliases=None, vmem=4):
    return pl.pallas_call(
        kernel,
        grid=grid,
        out_shape=tuple(outs),
        in_specs=specs or [VMEM_SPEC] * len(args),
        out_specs=tuple(out_specs or [VMEM_SPEC] * len(outs)),
        scratch_shapes=list(scratch),
        input_output_aliases=aliases or {},
        cost_estimate=pl.CostEstimate(flops=flops, bytes_accessed=1 << 20, transcendentals=0),
        name=name,
        compiler_params=pltpu.CompilerParams(vmem_limit_bytes=vmem * MIB),
    )(*args)


def shards(volume, phase, dual, probe_real, probe_imag, intensity, offsets, angle_index):
    share, slices, length = volume.shape
    width = probe_real.shape[1]
    half = length // 2
    ang = lax.axis_size("ang")
    tiles = lax.axis_size("tile")
    groups = ang // 2
    pair = 2 * share
    parts = 2 if slices % 16 == 0 else 1
    some = slices // parts
    shape = jax.ShapeDtypeStruct

    (forward_full, inverse_full), (forward, inverse) = packed_tables(length)
    forward_full, inverse_full = split_pair(forward_full), split_pair(inverse_full)
    down, up = forward.T, inverse.T
    owners = [
        np.r_[i * share : (i + 1) * share, (i ^ 1) * share : ((i ^ 1) + 1) * share] for i in range(ang)
    ]
    down_part = np.stack([down[:, rows] for rows in owners])
    up_part = np.stack([up[rows] for rows in owners])
    right, left, left_conj, right_conj = patch_tables(width)
    line = shape((slices, length), F32)
    work = 2 * 2 * length * length * length * slices * groups

    def swap(value):
        return lax.ppermute(value, "ang", [(i, i ^ 1) for i in range(ang)])

    def from_peer(value, j):
        return lax.ppermute(value, "ang", [((i + 2 * j) % ang, i) for i in range(ang)])

    def to_peer(value, j):
        return lax.ppermute(value, "ang", [(i, (i + 2 * j) % ang) for i in range(ang)])

    def lanes(side):
        return pl.BlockSpec((share * slices, half), lambda _: (0, side))

    def gathered(lines):
        return [lines[0]] + [to_peer(lines[j], j) for j in range(1, groups)]

    image = lax.all_to_all(
        jnp.broadcast_to(phase, (tiles, slices, length)), "tile", split_axis=0, concat_axis=0, tiled=True
    ).reshape(tiles * slices, length)
    flat = volume.reshape(share * slices, length)
    other = swap(flat)
    angles = [angle_index] + [from_peer(angle_index, j) for j in range(1, groups)]

    tables_shape = [
        shape((3, length, half), F32), shape((2, half, length), F32), shape((8, length), F32)
    ] * groups
    outs = call(
        functools.partial(project_kernel, groups, slices),
        [line] * groups
        + [shape((slices, share, length), F32), shape((slices, share, length), BF16)]
        + [shape((pair, length), BF16)] * 2
        + tables_shape,
        angles + [flat, flat, other, other, forward, inverse, down_part, up],
        [SMEM_SPEC] * groups + [lanes(0), lanes(1)] * 2 + [VMEM_SPEC] * 4,
        grid=(1,),
        flops=3 * work,
        vmem=28,
        name="project_old",
    )
    lines, bases, edges, tables = take(outs, groups, 2, 2, 3 * groups)
    old = gathered(lines)

    image, edges = lax.optimization_barrier((image, edges))
    (grad,) = call(
        gradient_kernel,
        [shape((tiles, slices, length), BF16)],
        [offsets, image, intensity[0], probe_real, probe_imag, right, left, left_conj, right_conj],
        [SMEM_SPEC] + [VMEM_SPEC] * 8,
        flops=2 * work,
        vmem=12,
        name="gradient",
    )
    grad, edges, old = lax.optimization_barrier((grad, edges, old))
    grad = lax.all_to_all(grad, "tile", split_axis=0, concat_axis=0, tiled=True)

    before = lax.ppermute(edges[0], "tile", [(i, i + 1) for i in range(tiles - 1)])
    after = lax.ppermute(edges[1], "tile", [(i + 1, i) for i in range(tiles - 1)])

    phase_part, resid_part = call(
        functools.partial(line_kernel, groups), [line, line], [phase[0], dual[0], inverse_full] + old,
        name="line_step",
    )
    grad, before, after = lax.optimization_barrier((grad, before, after))
    phase_new, spectrum = call(
        phase_kernel, [line, line], [grad, phase_part, resid_part, forward_full], name="phase_step"
    )
    spectra = [spectrum] + [from_peer(spectrum, j) for j in range(1, groups)]

    halves = []
    for h in range(parts):
        (mine,) = call(
            functools.partial(back_kernel, groups),
            [shape((some, pair, length), BF16)],
            spectra + [forward, inverse, down, up_part] + tables,
            [pl.BlockSpec((some, length), lambda _, h=h: (h, 0))] * groups + [VMEM_SPEC] * (4 + 3 * groups),
            grid=(1,),
            flops=3 * work // parts,
            vmem=24,
            name="backproject",
        )
        halves.append((mine, swap(mine)))

    results = []
    for h in range(parts):
        block = pl.BlockSpec((some, share, length), lambda _, h=h: (h, 0, 0))
        args = bases + [before, after] + list(halves[h]) + [forward, inverse, down_part, up] + tables
        results = call(
            functools.partial(update_kernel, groups, h == 0, h == parts - 1, len(results)),
            [shape((share, slices, length), F32)] + [line] * groups,
            args + list(results),
            [block] * 2 + [VMEM_SPEC] * (8 + 3 * groups) + [pl.BlockSpec(memory_space=pl.ANY)] * len(results),
            [pl.BlockSpec((share, some, length), lambda _, h=h: (0, h, 0))]
            + [pl.BlockSpec((some, length), lambda _, h=h: (h, 0))] * groups,
            scratch=[pltpu.VMEM((share * some, half), F32)] * 2,
            grid=(1,),
            flops=3 * work // parts,
            vmem=24,
            aliases={len(args) + i: i for i in range(len(results))},
            name="project_new",
        )
    volume_new, lines = results[0], results[1:]
    (dual_new,) = call(
        functools.partial(dual_kernel, groups), [line],
        [phase_new, dual[0], inverse_full] + gathered(lines),
        name="dual_step",
    )
    return phase_new[None], volume_new, dual_new[None]


def solution(mesh):
    placed = (
        P("ang", "tile", None),
        P("ang", "tile", None),
        P("ang", "tile", None),
        P(),
        P(),
        P("ang", "tile", None, None),
        P("ang", "tile"),
        P("ang"),
    )
    return jax.shard_map(
        shards,
        mesh=mesh,
        in_specs=placed,
        out_specs=(P("ang", "tile", None), P("ang", "tile", None), P("ang", "tile", None)),
        check_vma=False,
    )
```

```python
import functools
import math

import jax
import jax.numpy as jnp
import numpy as np
from jax import lax
from jax.experimental import pallas as pl
from jax.experimental.pallas import tpu as pltpu
from jax.sharding import PartitionSpec as P

angle_center = 90.0
rho_weight = 1.0
eta_step = 0.01
tau_step = 1.0
smooth_weight = 0.25

F32 = jnp.float32
BF16 = jnp.bfloat16
VMEM_SPEC = pl.BlockSpec(memory_space=pltpu.VMEM)
SMEM_SPEC = pl.BlockSpec(memory_space=pltpu.SMEM)
MIB = 1024 * 1024


def table_pair(length):
    index = np.arange(length)
    phases = (index[:, None] * index[None, :] % length) * (2.0 * np.pi / length)
    return np.cos(phases).astype(np.float32), np.sin(phases).astype(np.float32)


def packed_tables(length):
    half = length // 2
    cos_t, sin_t = table_pair(length)
    bf = np.asarray(jnp.bfloat16).dtype if False else jnp.bfloat16
    out = []
    for kind in (np.float32, bf):
        c = cos_t.astype(kind).astype(np.float32)
        s = sin_t.astype(kind).astype(np.float32)
        forward = np.concatenate([c[:, : half + 1], -s[:, 1:half]], axis=1)
        weight = np.full((length, 1), 2.0 / length, np.float32)
        weight[0] = weight[half] = 1.0 / length
        inverse = forward.T * weight
        out.append((forward.astype(kind), inverse.astype(kind)))
    return out


def split_pair(array):
    high = array.astype(jnp.bfloat16)
    low = (array - high.astype(np.float32)).astype(jnp.bfloat16)
    return np.stack([high, low])


def patch_tables(width):
    cos_t, sin_t = table_pair(width)
    c = cos_t / np.float32(math.sqrt(width))
    s = sin_t / np.float32(math.sqrt(width))
    right = np.block([[c, -s], [s, c]])
    left = np.block([[c, s], [-s, c]])
    right_conj = np.block([[c, s], [-s, c]])
    left_conj = np.block([[c, -s], [s, c]])
    return tuple(split_pair(m.astype(np.float32)) for m in (right, left, left_conj, right_conj))


def dot(left, right):
    return jnp.dot(left, right, preferred_element_type=F32)


def dot_high(left, right):
    return jnp.dot(left, right, precision=lax.Precision.HIGHEST, preferred_element_type=F32)


def dot_split(left, right):
    def parts(value):
        if value.dtype == BF16:
            return value[0], value[1]
        high = value.astype(BF16)
        return high, (value - high.astype(F32)).astype(BF16)

    left_high, left_low = parts(left)
    right_high, right_low = parts(right)
    return dot(left_high, right_high) + dot(left_low, right_high) + dot(left_high, right_low)


def turn(re, im, c1, s, c2, sign):
    if sign > 0:
        return re * c1 + im * s, im * c2 - re * s
    return re * c1 - im * s, im * c2 + re * s


def fill_turn_tables(angle, length, row_ref, col_ref, nyq_ref):
    half = length // 2
    unit = 2.0 * math.pi / length
    theta = (jnp.full((8, half), angle, jnp.int32).astype(F32) - angle_center) * (math.pi / 360.0)
    coef_a = -(jnp.sin(0.5 * theta) / jnp.cos(0.5 * theta))
    coef_b = jnp.sin(theta)

    lane = lax.broadcasted_iota(jnp.int32, (8, half), 1)
    sub = lax.broadcasted_iota(jnp.int32, (8, half), 0)
    freq = jnp.where(lane == 0, half, lane).astype(F32)
    phase = unit * coef_a * freq
    base = phase * sub.astype(F32)
    base_c, base_s = jnp.cos(base), jnp.sin(base)
    for block in range(length // 64):
        first = 8 * block * 8 - half
        step = phase * (first + 8 * sub).astype(F32)
        step_c, step_s = jnp.cos(step), jnp.sin(step)
        for q in range(8):
            sc, ss = step_c[q : q + 1], step_s[q : q + 1]
            c2 = base_c * sc - base_s * ss
            s = base_s * sc + base_c * ss
            rows = pl.ds((block * 8 + q) * 8, 8)
            row_ref[0, rows, :] = jnp.where(lane == 0, 1.0, c2)
            row_ref[1, rows, :] = jnp.where(lane == 0, 0.0, s)
            row_ref[2, rows, :] = c2

    for side in range(2):
        place = (lane + (side * half - half)).astype(F32)
        phase = unit * coef_b * place
        lanes = slice(side * half, side * half + half)
        base = phase * sub.astype(F32)
        base_c, base_s = jnp.cos(base), jnp.sin(base)
        for block in range(half // 64):
            step = phase * (block * 64 + 8 * sub).astype(F32)
            step_c, step_s = jnp.cos(step), jnp.sin(step)
            for q in range(8):
                sc, ss = step_c[q : q + 1], step_s[q : q + 1]
                rows = pl.ds((block * 8 + q) * 8, 8)
                col_ref[0, rows, lanes] = base_c * sc - base_s * ss
                col_ref[1, rows, lanes] = base_s * sc + base_c * ss
        top = jnp.where(sub == 0, jnp.cos(phase * float(half)), base_c)
        nyq_ref[:, lanes] = top


class Tables:
    def __init__(self, row, col, nyq):
        self.row, self.col, self.nyq = row, col, nyq

    def rows(self):
        return self.row[0], self.row[1], self.row[2]

    def chip_rows(self, share):
        here = lax.axis_index("ang")
        other = here + 1 - 2 * lax.rem(here, 2)
        places = [pl.ds(pl.multiple_of(which * share, 8), share) for which in (here, other)]
        return tuple(jnp.concatenate([self.row[part, rows, :] for rows in places], axis=0) for part in range(3))

    def columns(self):
        c1 = self.col[0]
        return c1, self.col[1], jnp.concatenate([self.nyq[...], c1[8:]], axis=0)


def turn_rows(spectrum, tables, sign):
    half = spectrum.shape[1] // 2
    return turn(spectrum[:, :half], spectrum[:, half:], *tables, sign)


def turn_columns(spectrum, tables, sign):
    half = spectrum.shape[0] // 2
    pair = turn(spectrum[:half], spectrum[half:], *tables, sign)
    return jnp.concatenate(pair, axis=0).astype(BF16)


def side_by_side(value, count):
    rows = value.shape[0] // count
    return jnp.concatenate([value[i * rows : (i + 1) * rows] for i in range(count)], axis=1)


def stacked(value, count):
    columns = value.shape[1] // count
    return jnp.concatenate([value[:, i * columns : (i + 1) * columns] for i in range(count)], axis=0)


def block_of(value, i, count, axis):
    size = value.shape[axis] // count
    return lax.slice_in_dim(value, i * size, (i + 1) * size, axis=axis)


def project_slices(slab, count, share, tables, consts, lines_refs):
    forward_ref, inverse_ref, down_ref, up_ref = consts
    here = lax.axis_index("ang")
    spectrum = dot(slab, forward_ref[...])
    for table, lines_ref in zip(tables, lines_refs):
        chip_rows = table.chip_rows(share)
        turned = [
            jnp.concatenate(turn_rows(block_of(spectrum, i, count, 0), chip_rows, 1), axis=1).astype(BF16)
            for i in range(count)
        ]
        first = dot(jnp.concatenate(turned, axis=0), inverse_ref[...]).astype(BF16)
        columns = dot(down_ref[here], side_by_side(first, count))
        turned = [turn_columns(block_of(columns, i, count, 1), table.columns(), 1) for i in range(count)]
        second = dot(up_ref[...], jnp.concatenate(turned, axis=1)).astype(BF16)
        last = dot(stacked(second, count), forward_ref[...])
        for i in range(count):
            re, im = turn_rows(block_of(last, i, count, 0), table.rows(), 1)
            sums = [jnp.sum(part, axis=0, keepdims=True) for part in (re, im)]
            lines_ref[pl.ds(i, 1), :] = jnp.concatenate(sums, axis=1)


def take(refs, *counts):
    refs, out = list(refs), []
    for count in counts:
        out.append(refs[:count])
        refs = refs[count:]
    return out


def as_tables(refs):
    return [Tables(*refs[i : i + 3]) for i in range(0, len(refs), 3)]


def tables_kernel(groups, *refs):
    angle_refs, table_refs = take(refs, groups, 3 * groups)
    for g in range(groups):
        row_ref, col_ref, nyq_ref = table_refs[3 * g : 3 * g + 3]
        fill_turn_tables(angle_refs[g][0], row_ref.shape[1], row_ref, col_ref, nyq_ref)


def project_kernel(groups, slices, part, parts, aliased, *refs):
    angle_refs, sides, (const_ref, down_ref), unused, lines_refs, bases, rest = take(
        refs, groups, 4, 2, aliased, groups, 2, len(refs)
    )
    edges, table_refs = take(rest, 2 if part == 0 else 0, 3 * groups)
    some, share, length = bases[0].shape
    tables_kernel(groups, *angle_refs, *table_refs)

    def rows(z):
        pieces = [ref[pl.ds(z, share, stride=slices), :] for ref in sides]
        return [jnp.concatenate(pieces[:2], axis=1), jnp.concatenate(pieces[2:], axis=1)]

    if part == 0:
        for edge_ref, z in zip(edges, (slices - 1, 0)):
            edge_ref[...] = jnp.concatenate(rows(z), axis=0).astype(BF16)
    slab = []
    start = part * some
    past = rows(start - 1) if start > 0 else None
    now = rows(start)
    for z in range(some):
        later = rows(start + z + 1) if start + z + 1 < slices else None
        for place in range(2):
            slab.append(now[place].astype(BF16))
            near = [side[place] for side in (past, later) if side is not None]
            base = (1.0 - 2.0 * tau_step * smooth_weight) * now[place]
            base = base + (tau_step * smooth_weight) * sum(near[1:], near[0])
            bases[place][z] = base.astype(bases[place].dtype)
        past, now = now, later
    consts = [const_ref.at[0], const_ref.at[1], down_ref, const_ref.at[3]]
    project_slices(
        jnp.concatenate(slab, axis=0), some, share, as_tables(table_refs), consts, lines_refs
    )


def back_kernel(groups, *refs):
    spectra_refs, (const_ref, up_ref), table_refs, (out_ref,) = take(refs, groups, 2, 3 * groups, 1)
    forward_ref, inverse_ref, down_ref = const_ref.at[0], const_ref.at[1], const_ref.at[2]
    slices, pair, length = out_ref.shape
    half = length // 2
    here = lax.axis_index("ang")
    totals = None
    for table, spectra_ref in zip(as_tables(table_refs), spectra_refs):
        turned = []
        for z in range(slices):
            line = spectra_ref[pl.ds(z, 1), :]
            pieces = turn(line[:, :half], line[:, half:], *table.rows(), -1)
            turned.append(jnp.concatenate(pieces, axis=1).astype(BF16))
        spread = dot(jnp.concatenate(turned, axis=0), inverse_ref[...]).astype(BF16)
        columns = dot(down_ref[...], side_by_side(spread, slices))
        turned = [turn_columns(block_of(columns, i, slices, 1), table.columns(), -1) for i in range(slices)]
        second = dot(up_ref[here], jnp.concatenate(turned, axis=1)).astype(BF16)
        last = dot(stacked(second, slices), forward_ref[...])
        chip_rows = table.chip_rows(pair // 2)
        turned = [
            jnp.concatenate(turn_rows(block_of(last, i, slices, 0), chip_rows, -1), axis=1)
            for i in range(slices)
        ]
        totals = turned if totals is None else [old + new for old, new in zip(totals, turned)]
    total = jnp.concatenate([value.astype(BF16) for value in totals], axis=0)
    out_ref[...] = dot(total, inverse_ref[...]).astype(BF16).reshape(out_ref.shape)


def update_kernel(groups, first, last, aliased, *refs):
    bases, halos, shares, (const_ref, down_ref), table_refs, unused, (volume_ref,), lines_refs, sides = take(
        refs, 2, 2, 2, 2, 3 * groups, aliased, 1, groups, 2
    )
    consts = [const_ref.at[0], const_ref.at[1], down_ref, const_ref.at[3]]
    own_ref, other_ref = bases
    mine_ref, theirs_ref = shares
    slices, share, length = own_ref.shape
    half = length // 2
    slab = []
    for z in range(slices):
        own = own_ref[z] - tau_step * (
            mine_ref[z, :share, :].astype(F32) + theirs_ref[z, share:, :].astype(F32)
        )
        other = other_ref[z].astype(F32) - tau_step * (
            mine_ref[z, share:, :].astype(F32) + theirs_ref[z, :share, :].astype(F32)
        )
        for needed, halo_ref in ((first and z == 0, halos[0]), (last and z == slices - 1, halos[1])):
            if needed:
                halo = (tau_step * smooth_weight) * halo_ref[...].astype(F32)
                own, other = own + halo[:share], other + halo[share:]
        for side in range(2):
            sides[side][pl.ds(z, share, stride=slices), :] = own[:, side * half : (side + 1) * half]
        slab += [own.astype(BF16), other.astype(BF16)]
    project_slices(
        jnp.concatenate(slab, axis=0), slices, share, as_tables(table_refs), consts, lines_refs
    )
    whole = jnp.concatenate([ref[...] for ref in sides], axis=1)
    volume_ref[...] = whole.reshape(volume_ref.shape)


def gradient_kernel(
    offsets_ref, image_ref, measured_ref, probe_r_ref, probe_i_ref,
    right_ref, left_ref, left_conj_ref, right_conj_ref, out_ref,
):
    positions, height, width = measured_ref.shape
    length = image_ref.shape[1]
    image = image_ref[...]
    cos_image, sin_image = jnp.cos(image), jnp.sin(image)
    probe_r, probe_i = probe_r_ref[...], probe_i_ref[...]
    waves = []
    for p in range(positions):
        back = length - offsets_ref[0, p]
        cos_p = pltpu.roll(cos_image, back, 1)[:, :width]
        sin_p = pltpu.roll(sin_image, back, 1)[:, :width]
        waves.append((probe_r * cos_p - probe_i * sin_p, probe_r * sin_p + probe_i * cos_p))

    def to_columns(value):
        parts = [block_of(value, p, positions, 0) for p in range(positions)]
        return jnp.concatenate(
            [jnp.concatenate([part[:, i * width : (i + 1) * width] for part in parts], axis=1) for i in range(2)],
            axis=0,
        )

    def to_rows(value):
        parts = [block_of(value, p, positions, 1) for p in range(positions)]
        return jnp.concatenate(
            [jnp.concatenate([part[:height], part[height:]], axis=1) for part in parts], axis=0
        )

    entry = jnp.concatenate([jnp.concatenate(wave, axis=1) for wave in waves], axis=0)
    far = dot_split(left_ref[...], to_columns(dot_split(entry, right_ref[...])))
    far_r, far_i = far[:height], far[height:]
    measured = jnp.concatenate([measured_ref[p] for p in range(positions)], axis=1)
    misfit = far_r * far_r + far_i * far_i - measured
    weighted = jnp.concatenate([misfit * far_r, misfit * far_i], axis=0)
    chi = dot_split(to_rows(dot_split(left_conj_ref[...], weighted)), right_conj_ref[...])
    total = jnp.zeros((height, length), F32)
    for p in range(positions):
        part = block_of(chi, p, positions, 0)
        wave_r, wave_i = waves[p]
        term = 2.0 * (part[:, width:] * wave_r - part[:, :width] * wave_i)
        padded = jnp.concatenate([term, jnp.zeros((height, length - width), F32)], axis=1)
        total = total + pltpu.roll(padded, offsets_ref[0, p], 1)
    out_ref[...] = total.astype(out_ref.dtype).reshape(out_ref.shape)


def projected(line_refs, inverse_ref):
    line = line_refs[0][...]
    for other in line_refs[1:]:
        line = line + other[...]
    return dot_split(line, inverse_ref[...]) * (1.0 / math.sqrt(line.shape[1]))


def line_kernel(peers, phase_ref, dual_ref, inverse_ref, *refs):
    line_refs, (phase_part_ref, resid_part_ref) = take(refs, peers, 2)
    proj_old = projected(line_refs, inverse_ref)
    phase, dual = phase_ref[...], dual_ref[...]
    phase_part = phase - eta_step * (dual + rho_weight * (phase - proj_old))
    phase_part_ref[...] = phase_part
    resid_part_ref[...] = rho_weight * (proj_old - phase_part) - dual


def phase_kernel(grad_ref, phase_part_ref, resid_part_ref, forward_ref, phase_new_ref, spectrum_ref):
    grad = grad_ref[0].astype(F32)
    for t in range(1, grad_ref.shape[0]):
        grad = grad + grad_ref[t].astype(F32)
    grad = eta_step * grad
    phase_new_ref[...] = phase_part_ref[...] - grad
    resid = resid_part_ref[...] + rho_weight * grad
    spectrum_ref[...] = dot_split(resid, forward_ref[...]) * (1.0 / math.sqrt(resid.shape[1]))


def dual_kernel(peers, phase_ref, dual_ref, inverse_ref, *refs):
    line_refs, (dual_new_ref,) = take(refs, peers, 1)
    proj_new = projected(line_refs, inverse_ref)
    dual_new_ref[...] = dual_ref[...] + rho_weight * (phase_ref[...] - proj_new)


def call(kernel, outs, args, specs=None, out_specs=None, scratch=(), flops=0, name=None, grid=(), aliases=None, vmem=4):
    return pl.pallas_call(
        kernel,
        grid=grid,
        out_shape=tuple(outs),
        in_specs=specs or [VMEM_SPEC] * len(args),
        out_specs=tuple(out_specs or [VMEM_SPEC] * len(outs)),
        scratch_shapes=list(scratch),
        input_output_aliases=aliases or {},
        cost_estimate=pl.CostEstimate(flops=flops, bytes_accessed=1 << 20, transcendentals=0),
        name=name,
        compiler_params=pltpu.CompilerParams(vmem_limit_bytes=vmem * MIB),
    )(*args)


def shards(volume, phase, dual, probe_real, probe_imag, intensity, offsets, angle_index):
    share, slices, length = volume.shape
    width = probe_real.shape[1]
    half = length // 2
    ang = lax.axis_size("ang")
    tiles = lax.axis_size("tile")
    groups = ang // 2
    pair = 2 * share
    parts = 2 if slices % 16 == 0 else 1
    some = slices // parts
    shape = jax.ShapeDtypeStruct

    (forward_full, inverse_full), (forward, inverse) = packed_tables(length)
    forward_full, inverse_full = split_pair(forward_full), split_pair(inverse_full)
    down, up = forward.T, inverse.T
    owners = [
        np.r_[i * share : (i + 1) * share, (i ^ 1) * share : ((i ^ 1) + 1) * share] for i in range(ang)
    ]
    down_part = np.stack([down[:, rows] for rows in owners])
    up_part = np.stack([up[rows] for rows in owners])
    square = np.stack([forward, inverse, down, up])
    right, left, left_conj, right_conj = patch_tables(width)
    line = shape((slices, length), F32)
    work = 2 * 2 * length * length * length * slices * groups

    def swap(value):
        return lax.ppermute(value, "ang", [(i, i ^ 1) for i in range(ang)])

    def from_peer(value, j):
        return lax.ppermute(value, "ang", [((i + 2 * j) % ang, i) for i in range(ang)])

    def to_peer(value, j):
        return lax.ppermute(value, "ang", [(i, (i + 2 * j) % ang) for i in range(ang)])

    def lanes(side):
        return pl.BlockSpec((share * slices, half), lambda _: (0, side))

    def gathered(lines):
        return [lines[0]] + [to_peer(lines[j], j) for j in range(1, groups)]

    tables_shape = [
        shape((3, length, half), F32), shape((2, half, length), F32), shape((8, length), F32)
    ] * groups
    block_lines = [
        pl.BlockSpec((some, length), functools.partial(lambda h, _: (h, 0), h)) for h in range(parts)
    ]

    image = lax.all_to_all(
        jnp.broadcast_to(phase, (tiles, slices, length)), "tile", split_axis=0, concat_axis=0, tiled=True
    ).reshape(tiles * slices, length)
    flat = volume.reshape(share * slices, length)
    other = swap(flat)
    angles = [angle_index] + [from_peer(angle_index, j) for j in range(1, groups)]

    def project_part(h, lines, angles):
        outs = [line] * groups + [shape((some, share, length), F32), shape((some, share, length), BF16)]
        outs = outs + [shape((pair, length), BF16)] * (2 if h == 0 else 0)
        extra = len(outs) - groups
        args = angles + [flat, flat, other, other, square, down_part]
        outs = call(
            functools.partial(project_kernel, groups, slices, h, parts, len(lines)),
            outs,
            args + lines,
            [SMEM_SPEC] * groups + [lanes(0), lanes(1)] * 2 + [VMEM_SPEC] * 2
            + [pl.BlockSpec(memory_space=pl.ANY)] * len(lines),
            [block_lines[h]] * groups + [VMEM_SPEC] * extra,
            scratch=[pltpu.VMEM(t.shape, F32) for t in tables_shape],
            grid=(1,),
            flops=3 * work // parts,
            vmem=24,
            aliases={len(args) + i: i for i in range(len(lines))},
            name="project_old",
        )
        return take(outs, groups, 2, 2)

    bases = []
    lines, base, edges = project_part(0, [], angles)
    bases.append(base)
    image, lines = lax.optimization_barrier((image, lines))
    (grad,) = call(
        gradient_kernel,
        [shape((tiles, slices, length), BF16)],
        [offsets, image, intensity[0], probe_real, probe_imag, right, left, left_conj, right_conj],
        [SMEM_SPEC] + [VMEM_SPEC] * 8,
        flops=2 * work,
        vmem=12,
        name="gradient",
    )
    grad, lines, edges = lax.optimization_barrier((grad, lines, edges))
    grad = lax.all_to_all(grad, "tile", split_axis=0, concat_axis=0, tiled=True)
    for h in range(1, parts):
        lines, base, _ = project_part(h, lines, angles)
        bases.append(base)
    old = gathered(lines)

    before = lax.ppermute(edges[0], "tile", [(i, i + 1) for i in range(tiles - 1)])
    after = lax.ppermute(edges[1], "tile", [(i + 1, i) for i in range(tiles - 1)])

    phase_part, resid_part = call(
        functools.partial(line_kernel, groups), [line, line], [phase[0], dual[0], inverse_full] + old,
        name="line_step",
    )
    phase_new, spectrum = call(
        phase_kernel, [line, line], [grad, phase_part, resid_part, forward_full], name="phase_step"
    )
    spectrum, angles = lax.optimization_barrier((spectrum, angles))
    tables = call(
        functools.partial(tables_kernel, groups), tables_shape, angles, [SMEM_SPEC] * groups,
        flops=work, name="turn_tables",
    )
    tables = list(tables)
    spectra = [spectrum] + [from_peer(spectrum, j) for j in range(1, groups)]

    halves = []
    for h in range(parts):
        (mine,) = call(
            functools.partial(back_kernel, groups),
            [shape((some, pair, length), BF16)],
            spectra + [square, up_part] + tables,
            [block_lines[h]] * groups + [VMEM_SPEC] * (2 + 3 * groups),
            grid=(1,),
            flops=3 * work // parts,
            vmem=24,
            name="backproject",
        )
        halves.append((mine, swap(mine)))

    results = []
    for h in range(parts):
        args = bases[h] + [before, after] + list(halves[h]) + [square, down_part] + tables
        results = call(
            functools.partial(update_kernel, groups, h == 0, h == parts - 1, len(results)),
            [shape((share, slices, length), F32)] + [line] * groups,
            args + list(results),
            [VMEM_SPEC] * len(args) + [pl.BlockSpec(memory_space=pl.ANY)] * len(results),
            [pl.BlockSpec((share, some, length), lambda _, h=h: (0, h, 0))]
            + [block_lines[h]] * groups,
            scratch=[pltpu.VMEM((share * some, half), F32)] * 2,
            grid=(1,),
            flops=3 * work // parts,
            vmem=24,
            aliases={len(args) + i: i for i in range(len(results))},
            name="project_new",
        )
    volume_new, lines = results[0], results[1:]
    (dual_new,) = call(
        functools.partial(dual_kernel, groups), [line],
        [phase_new, dual[0], inverse_full] + gathered(lines),
        name="dual_step",
    )
    return phase_new[None], volume_new, dual_new[None]


def solution(mesh):
    placed = (
        P("ang", "tile", None),
        P("ang", "tile", None),
        P("ang", "tile", None),
        P(),
        P(),
        P("ang", "tile", None, None),
        P("ang", "tile"),
        P("ang"),
    )
    return jax.shard_map(
        shards,
        mesh=mesh,
        in_specs=placed,
        out_specs=(P("ang", "tile", None), P("ang", "tile", None), P("ang", "tile", None)),
        check_vma=False,
    )
```

```python
import functools
import math

import jax
import jax.numpy as jnp
import numpy as np
from jax import lax
from jax.experimental import pallas as pl
from jax.experimental.pallas import tpu as pltpu
from jax.sharding import PartitionSpec as P

angle_center = 90.0
rho_weight = 1.0
eta_step = 0.01
tau_step = 1.0
smooth_weight = 0.25

F32 = jnp.float32
BF16 = jnp.bfloat16
VMEM_SPEC = pl.BlockSpec(memory_space=pltpu.VMEM)
SMEM_SPEC = pl.BlockSpec(memory_space=pltpu.SMEM)
MIB = 1024 * 1024


def table_pair(length):
    index = np.arange(length)
    phases = (index[:, None] * index[None, :] % length) * (2.0 * np.pi / length)
    return np.cos(phases).astype(np.float32), np.sin(phases).astype(np.float32)


def packed_tables(length):
    half = length // 2
    cos_t, sin_t = table_pair(length)
    bf = np.asarray(jnp.bfloat16).dtype if False else jnp.bfloat16
    out = []
    for kind in (np.float32, bf):
        c = cos_t.astype(kind).astype(np.float32)
        s = sin_t.astype(kind).astype(np.float32)
        forward = np.concatenate([c[:, : half + 1], -s[:, 1:half]], axis=1)
        weight = np.full((length, 1), 2.0 / length, np.float32)
        weight[0] = weight[half] = 1.0 / length
        inverse = forward.T * weight
        out.append((forward.astype(kind), inverse.astype(kind)))
    return out


def split_pair(array):
    high = array.astype(jnp.bfloat16)
    low = (array - high.astype(np.float32)).astype(jnp.bfloat16)
    return np.stack([high, low])


def patch_tables(width):
    cos_t, sin_t = table_pair(width)
    c = cos_t / np.float32(math.sqrt(width))
    s = sin_t / np.float32(math.sqrt(width))
    right = np.block([[c, -s], [s, c]])
    left = np.block([[c, s], [-s, c]])
    return split_pair(right.astype(np.float32)), split_pair(left.astype(np.float32))


def dot(left, right):
    return jnp.dot(left, right, preferred_element_type=F32)


def dot_high(left, right):
    return jnp.dot(left, right, precision=lax.Precision.HIGHEST, preferred_element_type=F32)


def dot_split(left, right):
    def parts(value):
        if value.dtype == BF16:
            return value[0], value[1]
        high = value.astype(BF16)
        return high, (value - high.astype(F32)).astype(BF16)

    left_high, left_low = parts(left)
    right_high, right_low = parts(right)
    return dot(left_high, right_high) + dot(left_low, right_high) + dot(left_high, right_low)


def turn(re, im, c1, s, c2, sign):
    if sign > 0:
        return re * c1 + im * s, im * c2 - re * s
    return re * c1 - im * s, im * c2 + re * s


def fill_turn_tables(angle, length, row_ref, col_ref, nyq_ref):
    half = length // 2
    unit = 2.0 * math.pi / length
    theta = (jnp.full((8, half), angle, jnp.int32).astype(F32) - angle_center) * (math.pi / 360.0)
    coef_a = -(jnp.sin(0.5 * theta) / jnp.cos(0.5 * theta))
    coef_b = jnp.sin(theta)

    lane = lax.broadcasted_iota(jnp.int32, (8, half), 1)
    sub = lax.broadcasted_iota(jnp.int32, (8, half), 0)
    freq = jnp.where(lane == 0, half, lane).astype(F32)
    phase = unit * coef_a * freq
    base = phase * sub.astype(F32)
    base_c, base_s = jnp.cos(base), jnp.sin(base)
    for block in range(length // 64):
        first = 8 * block * 8 - half
        step = phase * (first + 8 * sub).astype(F32)
        step_c, step_s = jnp.cos(step), jnp.sin(step)
        for q in range(8):
            sc, ss = step_c[q : q + 1], step_s[q : q + 1]
            c2 = base_c * sc - base_s * ss
            s = base_s * sc + base_c * ss
            rows = pl.ds((block * 8 + q) * 8, 8)
            row_ref[0, rows, :] = jnp.where(lane == 0, 1.0, c2)
            row_ref[1, rows, :] = jnp.where(lane == 0, 0.0, s)
            row_ref[2, rows, :] = c2

    for side in range(2):
        place = (lane + (side * half - half)).astype(F32)
        phase = unit * coef_b * place
        lanes = slice(side * half, side * half + half)
        base = phase * sub.astype(F32)
        base_c, base_s = jnp.cos(base), jnp.sin(base)
        for block in range(half // 64):
            step = phase * (block * 64 + 8 * sub).astype(F32)
            step_c, step_s = jnp.cos(step), jnp.sin(step)
            for q in range(8):
                sc, ss = step_c[q : q + 1], step_s[q : q + 1]
                rows = pl.ds((block * 8 + q) * 8, 8)
                col_ref[0, rows, lanes] = base_c * sc - base_s * ss
                col_ref[1, rows, lanes] = base_s * sc + base_c * ss
        top = jnp.where(sub == 0, jnp.cos(phase * float(half)), base_c)
        nyq_ref[:, lanes] = top


class Tables:
    def __init__(self, row, col, nyq):
        self.row, self.col, self.nyq = row, col, nyq

    def rows(self):
        return self.row[0], self.row[1], self.row[2]

    def chip_rows(self, share):
        here = lax.axis_index("ang")
        other = here + 1 - 2 * lax.rem(here, 2)
        places = [pl.ds(pl.multiple_of(which * share, 8), share) for which in (here, other)]
        return tuple(jnp.concatenate([self.row[part, rows, :] for rows in places], axis=0) for part in range(3))

    def columns(self):
        c1 = self.col[0]
        return c1, self.col[1], jnp.concatenate([self.nyq[...], c1[8:]], axis=0)


def turn_rows(spectrum, tables, sign):
    half = spectrum.shape[1] // 2
    return turn(spectrum[:, :half], spectrum[:, half:], *tables, sign)


def turn_columns(spectrum, tables, sign):
    half = spectrum.shape[0] // 2
    pair = turn(spectrum[:half], spectrum[half:], *tables, sign)
    return jnp.concatenate(pair, axis=0).astype(BF16)


def side_by_side(value, count):
    rows = value.shape[0] // count
    return jnp.concatenate([value[i * rows : (i + 1) * rows] for i in range(count)], axis=1)


def stacked(value, count):
    columns = value.shape[1] // count
    return jnp.concatenate([value[:, i * columns : (i + 1) * columns] for i in range(count)], axis=0)


def block_of(value, i, count, axis):
    size = value.shape[axis] // count
    return lax.slice_in_dim(value, i * size, (i + 1) * size, axis=axis)


def project_slices(slab, count, share, tables, consts, lines_refs):
    forward_ref, inverse_ref, down_ref, up_ref = consts
    here = lax.axis_index("ang")
    spectrum = dot(slab, forward_ref[...])
    for table, lines_ref in zip(tables, lines_refs):
        chip_rows = table.chip_rows(share)
        turned = [
            jnp.concatenate(turn_rows(block_of(spectrum, i, count, 0), chip_rows, 1), axis=1).astype(BF16)
            for i in range(count)
        ]
        first = dot(jnp.concatenate(turned, axis=0), inverse_ref[...]).astype(BF16)
        columns = dot(down_ref[here], side_by_side(first, count))
        turned = [turn_columns(block_of(columns, i, count, 1), table.columns(), 1) for i in range(count)]
        second = dot(up_ref[...], jnp.concatenate(turned, axis=1)).astype(BF16)
        last = dot(stacked(second, count), forward_ref[...])
        for i in range(count):
            re, im = turn_rows(block_of(last, i, count, 0), table.rows(), 1)
            sums = [jnp.sum(part, axis=0, keepdims=True) for part in (re, im)]
            lines_ref[pl.ds(i, 1), :] = jnp.concatenate(sums, axis=1)


def take(refs, *counts):
    refs, out = list(refs), []
    for count in counts:
        out.append(refs[:count])
        refs = refs[count:]
    return out


def as_tables(refs):
    return [Tables(*refs[i : i + 3]) for i in range(0, len(refs), 3)]


def tables_kernel(groups, *refs):
    angle_refs, table_refs = take(refs, groups, 3 * groups)
    for g in range(groups):
        row_ref, col_ref, nyq_ref = table_refs[3 * g : 3 * g + 3]
        fill_turn_tables(angle_refs[g][0], row_ref.shape[1], row_ref, col_ref, nyq_ref)


def edge_kernel(slices, *refs):
    sides, edges = take(refs, 4, 2)
    share = sides[0].shape[0] // slices
    for edge_ref, z in zip(edges, (slices - 1, 0)):
        pieces = [ref[pl.ds(z, share, stride=slices), :].astype(BF16) for ref in sides]
        edge_ref[:share, :] = jnp.concatenate(pieces[:2], axis=1)
        edge_ref[share:, :] = jnp.concatenate(pieces[2:], axis=1)


def project_kernel(groups, slices, *refs):
    angle_refs, sides, (const_ref, down_ref), lines_refs, bases, table_refs = take(
        refs, groups, 4, 2, groups, 2, 3 * groups
    )
    share = sides[0].shape[0] // slices
    tables_kernel(groups, *angle_refs, *table_refs)

    def rows(z):
        pieces = [ref[pl.ds(z, share, stride=slices), :] for ref in sides]
        return [jnp.concatenate(pieces[:2], axis=1), jnp.concatenate(pieces[2:], axis=1)]

    slab = []
    past, now = None, rows(0)
    for z in range(slices):
        later = rows(z + 1) if z + 1 < slices else None
        for place in range(2):
            slab.append(now[place].astype(BF16))
            near = [side[place] for side in (past, later) if side is not None]
            base = (1.0 - 2.0 * tau_step * smooth_weight) * now[place]
            base = base + (tau_step * smooth_weight) * sum(near[1:], near[0])
            bases[place][z] = base.astype(bases[place].dtype)
        past, now = now, later
    consts = [const_ref.at[0], const_ref.at[1], down_ref, const_ref.at[3]]
    project_slices(
        jnp.concatenate(slab, axis=0), slices, share, as_tables(table_refs), consts, lines_refs
    )


def back_kernel(groups, *refs):
    spectra_refs, (const_ref, up_ref), table_refs, (out_ref,) = take(refs, groups, 2, 3 * groups, 1)
    forward_ref, inverse_ref, down_ref = const_ref.at[0], const_ref.at[1], const_ref.at[2]
    slices, pair, length = out_ref.shape
    half = length // 2
    here = lax.axis_index("ang")
    totals = None
    for table, spectra_ref in zip(as_tables(table_refs), spectra_refs):
        turned = []
        for z in range(slices):
            line = spectra_ref[pl.ds(z, 1), :]
            pieces = turn(line[:, :half], line[:, half:], *table.rows(), -1)
            turned.append(jnp.concatenate(pieces, axis=1).astype(BF16))
        spread = dot(jnp.concatenate(turned, axis=0), inverse_ref[...]).astype(BF16)
        columns = dot(down_ref[...], side_by_side(spread, slices))
        turned = [turn_columns(block_of(columns, i, slices, 1), table.columns(), -1) for i in range(slices)]
        second = dot(up_ref[here], jnp.concatenate(turned, axis=1)).astype(BF16)
        last = dot(stacked(second, slices), forward_ref[...])
        chip_rows = table.chip_rows(pair // 2)
        turned = [
            jnp.concatenate(turn_rows(block_of(last, i, slices, 0), chip_rows, -1), axis=1)
            for i in range(slices)
        ]
        totals = turned if totals is None else [old + new for old, new in zip(totals, turned)]
    total = jnp.concatenate([value.astype(BF16) for value in totals], axis=0)
    out_ref[...] = dot(total, inverse_ref[...]).astype(BF16).reshape(out_ref.shape)


def update_kernel(groups, first, last, aliased, *refs):
    bases, halos, shares, (const_ref, down_ref), table_refs, unused, (volume_ref,), lines_refs, sides = take(
        refs, 2, 2, 2, 2, 3 * groups, aliased, 1, groups, 2
    )
    consts = [const_ref.at[0], const_ref.at[1], down_ref, const_ref.at[3]]
    own_ref, other_ref = bases
    mine_ref, theirs_ref = shares
    slices, share, length = own_ref.shape
    half = length // 2
    slab = []
    for z in range(slices):
        own = own_ref[z] - tau_step * (
            mine_ref[z, :share, :].astype(F32) + theirs_ref[z, share:, :].astype(F32)
        )
        other = other_ref[z].astype(F32) - tau_step * (
            mine_ref[z, share:, :].astype(F32) + theirs_ref[z, :share, :].astype(F32)
        )
        for needed, halo_ref in ((first and z == 0, halos[0]), (last and z == slices - 1, halos[1])):
            if needed:
                halo = (tau_step * smooth_weight) * halo_ref[...].astype(F32)
                own, other = own + halo[:share], other + halo[share:]
        for side in range(2):
            sides[side][pl.ds(z, share, stride=slices), :] = own[:, side * half : (side + 1) * half]
        slab += [own.astype(BF16), other.astype(BF16)]
    project_slices(
        jnp.concatenate(slab, axis=0), slices, share, as_tables(table_refs), consts, lines_refs
    )
    whole = jnp.concatenate([ref[...] for ref in sides], axis=1)
    volume_ref[...] = whole.reshape(volume_ref.shape)


def gradient_kernel(
    offsets_ref, image_ref, measured_ref, probe_r_ref, probe_i_ref,
    const_ref, out_ref,
):
    right_ref, left_ref = const_ref.at[0], const_ref.at[1]
    left_conj_ref, right_conj_ref = right_ref, left_ref
    positions, height, width = measured_ref.shape
    length = image_ref.shape[1]
    image = image_ref[...]
    cos_image, sin_image = jnp.cos(image), jnp.sin(image)
    probe_r, probe_i = probe_r_ref[...], probe_i_ref[...]
    waves = []
    for p in range(positions):
        back = length - offsets_ref[0, p]
        cos_p = pltpu.roll(cos_image, back, 1)[:, :width]
        sin_p = pltpu.roll(sin_image, back, 1)[:, :width]
        waves.append((probe_r * cos_p - probe_i * sin_p, probe_r * sin_p + probe_i * cos_p))

    def to_columns(value):
        parts = [block_of(value, p, positions, 0) for p in range(positions)]
        return jnp.concatenate(
            [jnp.concatenate([part[:, i * width : (i + 1) * width] for part in parts], axis=1) for i in range(2)],
            axis=0,
        )

    def to_rows(value):
        parts = [block_of(value, p, positions, 1) for p in range(positions)]
        return jnp.concatenate(
            [jnp.concatenate([part[:height], part[height:]], axis=1) for part in parts], axis=0
        )

    entry = jnp.concatenate([jnp.concatenate(wave, axis=1) for wave in waves], axis=0)
    far = dot_split(left_ref[...], to_columns(dot_split(entry, right_ref[...])))
    far_r, far_i = far[:height], far[height:]
    measured = jnp.concatenate([measured_ref[p] for p in range(positions)], axis=1)
    misfit = far_r * far_r + far_i * far_i - measured
    weighted = jnp.concatenate([misfit * far_r, misfit * far_i], axis=0)
    chi = dot_split(to_rows(dot_split(left_conj_ref[...], weighted)), right_conj_ref[...])
    total = jnp.zeros((height, length), F32)
    for p in range(positions):
        part = block_of(chi, p, positions, 0)
        wave_r, wave_i = waves[p]
        term = 2.0 * (part[:, width:] * wave_r - part[:, :width] * wave_i)
        padded = jnp.concatenate([term, jnp.zeros((height, length - width), F32)], axis=1)
        total = total + pltpu.roll(padded, offsets_ref[0, p], 1)
    out_ref[...] = total.astype(out_ref.dtype).reshape(out_ref.shape)


def projected(line_refs, inverse_ref):
    line = line_refs[0][...]
    for other in line_refs[1:]:
        line = line + other[...]
    return dot_split(line, inverse_ref[...]) * (1.0 / math.sqrt(line.shape[1]))


def line_kernel(peers, phase_ref, dual_ref, inverse_ref, *refs):
    line_refs, (phase_part_ref, resid_part_ref) = take(refs, peers, 2)
    proj_old = projected(line_refs, inverse_ref)
    phase, dual = phase_ref[...], dual_ref[...]
    phase_part = phase - eta_step * (dual + rho_weight * (phase - proj_old))
    phase_part_ref[...] = phase_part
    resid_part_ref[...] = rho_weight * (proj_old - phase_part) - dual


def phase_kernel(grad_ref, phase_part_ref, resid_part_ref, forward_ref, phase_new_ref, spectrum_ref):
    grad = grad_ref[0].astype(F32)
    for t in range(1, grad_ref.shape[0]):
        grad = grad + grad_ref[t].astype(F32)
    grad = eta_step * grad
    phase_new_ref[...] = phase_part_ref[...] - grad
    resid = resid_part_ref[...] + rho_weight * grad
    spectrum_ref[...] = dot_split(resid, forward_ref[...]) * (1.0 / math.sqrt(resid.shape[1]))


def dual_kernel(peers, phase_ref, dual_ref, inverse_ref, *refs):
    line_refs, (dual_new_ref,) = take(refs, peers, 1)
    proj_new = projected(line_refs, inverse_ref)
    dual_new_ref[...] = dual_ref[...] + rho_weight * (phase_ref[...] - proj_new)


def call(kernel, outs, args, specs=None, out_specs=None, scratch=(), flops=0, name=None, grid=(), aliases=None, vmem=4):
    return pl.pallas_call(
        kernel,
        grid=grid,
        out_shape=tuple(outs),
        in_specs=specs or [VMEM_SPEC] * len(args),
        out_specs=tuple(out_specs or [VMEM_SPEC] * len(outs)),
        scratch_shapes=list(scratch),
        input_output_aliases=aliases or {},
        cost_estimate=pl.CostEstimate(flops=flops, bytes_accessed=1 << 20, transcendentals=0),
        name=name,
        compiler_params=pltpu.CompilerParams(vmem_limit_bytes=vmem * MIB),
    )(*args)


def shards(volume, phase, dual, probe_real, probe_imag, intensity, offsets, angle_index):
    share, slices, length = volume.shape
    width = probe_real.shape[1]
    half = length // 2
    ang = lax.axis_size("ang")
    tiles = lax.axis_size("tile")
    groups = ang // 2
    pair = 2 * share
    parts = 2 if slices % 16 == 0 else 1
    some = slices // parts
    shape = jax.ShapeDtypeStruct

    (forward_full, inverse_full), (forward, inverse) = packed_tables(length)
    forward_full, inverse_full = split_pair(forward_full), split_pair(inverse_full)
    down, up = forward.T, inverse.T
    owners = [
        np.r_[i * share : (i + 1) * share, (i ^ 1) * share : ((i ^ 1) + 1) * share] for i in range(ang)
    ]
    down_part = np.stack([down[:, rows] for rows in owners])
    up_part = np.stack([up[rows] for rows in owners])
    square = np.stack([forward, inverse, down, up])
    right, left = patch_tables(width)
    line = shape((slices, length), F32)
    work = 2 * 2 * length * length * length * slices * groups

    def swap(value):
        return lax.ppermute(value, "ang", [(i, i ^ 1) for i in range(ang)])

    def from_peer(value, j):
        return lax.ppermute(value, "ang", [((i + 2 * j) % ang, i) for i in range(ang)])

    def to_peer(value, j):
        return lax.ppermute(value, "ang", [(i, (i + 2 * j) % ang) for i in range(ang)])

    def lanes(side):
        return pl.BlockSpec((share * slices, half), lambda _: (0, side))

    def gathered(lines):
        return [lines[0]] + [to_peer(lines[j], j) for j in range(1, groups)]

    tables_shape = [
        shape((3, length, half), F32), shape((2, half, length), F32), shape((8, length), F32)
    ] * groups
    block_lines = [
        pl.BlockSpec((some, length), functools.partial(lambda h, _: (h, 0), h)) for h in range(parts)
    ]

    phases = jnp.broadcast_to(phase, (tiles, slices, length))
    phases, volume = lax.optimization_barrier((phases, volume))
    image = lax.all_to_all(phases, "tile", split_axis=0, concat_axis=0, tiled=True)
    image = image.reshape(tiles * slices, length)

    flat = volume.reshape(share * slices, length)
    other = swap(flat)
    edges = call(
        functools.partial(edge_kernel, slices),
        [shape((pair, length), BF16)] * 2,
        [flat, flat, other, other],
        [lanes(0), lanes(1)] * 2,
        grid=(1,),
        vmem=6,
        name="edges",
    )
    before = lax.ppermute(edges[0], "tile", [(i, i + 1) for i in range(tiles - 1)])
    after = lax.ppermute(edges[1], "tile", [(i + 1, i) for i in range(tiles - 1)])
    angle_index, edges = lax.optimization_barrier((angle_index, edges))
    angles = [angle_index] + [from_peer(angle_index, j) for j in range(1, groups)]
    image, before, after, angles = lax.optimization_barrier((image, before, after, angles))

    (grad,) = call(
        gradient_kernel,
        [shape((tiles, slices, length), BF16)],
        [offsets, image, intensity[0], probe_real, probe_imag, np.stack([right, left])],
        [SMEM_SPEC] + [VMEM_SPEC] * 5,
        flops=2 * work,
        vmem=12,
        name="gradient",
    )
    grad, angles = lax.optimization_barrier((grad, angles))
    grad = lax.all_to_all(grad, "tile", split_axis=0, concat_axis=0, tiled=True)

    outs = call(
        functools.partial(project_kernel, groups, slices),
        [line] * groups + [shape((slices, share, length), F32), shape((slices, share, length), BF16)],
        angles + [flat, flat, other, other, square, down_part],
        [SMEM_SPEC] * groups + [lanes(0), lanes(1)] * 2 + [VMEM_SPEC] * 2,
        scratch=[pltpu.VMEM(t.shape, F32) for t in tables_shape],
        grid=(1,),
        flops=3 * work,
        vmem=28,
        name="project_old",
    )
    lines, bases = take(outs, groups, 2)
    old = gathered(lines)

    phase_part, resid_part = call(
        functools.partial(line_kernel, groups), [line, line], [phase[0], dual[0], inverse_full] + old,
        name="line_step",
    )
    phase_new, spectrum = call(
        phase_kernel, [line, line], [grad, phase_part, resid_part, forward_full], name="phase_step"
    )
    spectrum, angles = lax.optimization_barrier((spectrum, angles))
    tables = call(
        functools.partial(tables_kernel, groups), tables_shape, angles, [SMEM_SPEC] * groups,
        flops=work, name="turn_tables",
    )
    tables = list(tables)
    spectra = [spectrum] + [from_peer(spectrum, j) for j in range(1, groups)]

    halves = []
    for h in range(parts):
        (mine,) = call(
            functools.partial(back_kernel, groups),
            [shape((some, pair, length), BF16)],
            spectra + [square, up_part] + tables,
            [block_lines[h]] * groups + [VMEM_SPEC] * (2 + 3 * groups),
            grid=(1,),
            flops=3 * work // parts,
            vmem=24,
            name="backproject",
        )
        halves.append((mine, swap(mine)))

    results = []
    for h in range(parts):
        args = bases + [before, after] + list(halves[h]) + [square, down_part] + tables
        results = call(
            functools.partial(update_kernel, groups, h == 0, h == parts - 1, len(results)),
            [shape((share, slices, length), F32)] + [line] * groups,
            args + list(results),
            [pl.BlockSpec((some, share, length), lambda _, h=h: (h, 0, 0))] * 2
            + [VMEM_SPEC] * (len(args) - 2) + [pl.BlockSpec(memory_space=pl.ANY)] * len(results),
            [pl.BlockSpec((share, some, length), lambda _, h=h: (0, h, 0))]
            + [block_lines[h]] * groups,
            scratch=[pltpu.VMEM((share * some, half), F32)] * 2,
            grid=(1,),
            flops=3 * work // parts,
            vmem=24,
            aliases={len(args) + i: i for i in range(len(results))},
            name="project_new",
        )
    volume_new, lines = results[0], results[1:]
    (dual_new,) = call(
        functools.partial(dual_kernel, groups), [line],
        [phase_new, dual[0], inverse_full] + gathered(lines),
        name="dual_step",
    )
    return phase_new[None], volume_new, dual_new[None]


def solution(mesh):
    placed = (
        P("ang", "tile", None),
        P("ang", "tile", None),
        P("ang", "tile", None),
        P(),
        P(),
        P("ang", "tile", None, None),
        P("ang", "tile"),
        P("ang"),
    )
    return jax.shard_map(
        shards,
        mesh=mesh,
        in_specs=placed,
        out_specs=(P("ang", "tile", None), P("ang", "tile", None), P("ang", "tile", None)),
        check_vma=False,
    )
```

```python
import functools
import math

import jax
import jax.numpy as jnp
import numpy as np
from jax import lax
from jax.experimental import pallas as pl
from jax.experimental.pallas import tpu as pltpu
from jax.sharding import PartitionSpec as P

angle_center = 90.0
rho_weight = 1.0
eta_step = 0.01
tau_step = 1.0
smooth_weight = 0.25

F32 = jnp.float32
BF16 = jnp.bfloat16
VMEM_SPEC = pl.BlockSpec(memory_space=pltpu.VMEM)
SMEM_SPEC = pl.BlockSpec(memory_space=pltpu.SMEM)
MIB = 1024 * 1024


def table_pair(length):
    index = np.arange(length)
    phases = (index[:, None] * index[None, :] % length) * (2.0 * np.pi / length)
    return np.cos(phases).astype(np.float32), np.sin(phases).astype(np.float32)


def packed_tables(length):
    half = length // 2
    cos_t, sin_t = table_pair(length)
    bf = np.asarray(jnp.bfloat16).dtype if False else jnp.bfloat16
    out = []
    for kind in (np.float32, bf):
        c = cos_t.astype(kind).astype(np.float32)
        s = sin_t.astype(kind).astype(np.float32)
        forward = np.concatenate([c[:, : half + 1], -s[:, 1:half]], axis=1)
        weight = np.full((length, 1), 2.0 / length, np.float32)
        weight[0] = weight[half] = 1.0 / length
        inverse = forward.T * weight
        out.append((forward.astype(kind), inverse.astype(kind)))
    return out


def split_pair(array):
    high = array.astype(jnp.bfloat16)
    low = (array - high.astype(np.float32)).astype(jnp.bfloat16)
    return np.stack([high, low])


def patch_tables(width):
    cos_t, sin_t = table_pair(width)
    c = cos_t / np.float32(math.sqrt(width))
    s = sin_t / np.float32(math.sqrt(width))
    right = np.block([[c, -s], [s, c]])
    left = np.block([[c, s], [-s, c]])
    return split_pair(right.astype(np.float32)), split_pair(left.astype(np.float32))


def dot(left, right):
    return jnp.dot(left, right, preferred_element_type=F32)


def dot_high(left, right):
    return jnp.dot(left, right, precision=lax.Precision.HIGHEST, preferred_element_type=F32)


def dot_split(left, right):
    def parts(value):
        if value.dtype == BF16:
            return value[0], value[1]
        high = value.astype(BF16)
        return high, (value - high.astype(F32)).astype(BF16)

    left_high, left_low = parts(left)
    right_high, right_low = parts(right)
    return dot(left_high, right_high) + dot(left_low, right_high) + dot(left_high, right_low)


def turn(re, im, c1, s, c2, sign):
    if sign > 0:
        return re * c1 + im * s, im * c2 - re * s
    return re * c1 - im * s, im * c2 + re * s


def fill_turn_tables(angle, length, row_ref, col_ref, nyq_ref):
    half = length // 2
    unit = 2.0 * math.pi / length
    theta = (jnp.full((8, half), angle, jnp.int32).astype(F32) - angle_center) * (math.pi / 360.0)
    coef_a = -(jnp.sin(0.5 * theta) / jnp.cos(0.5 * theta))
    coef_b = jnp.sin(theta)

    lane = lax.broadcasted_iota(jnp.int32, (8, half), 1)
    sub = lax.broadcasted_iota(jnp.int32, (8, half), 0)
    freq = jnp.where(lane == 0, half, lane).astype(F32)
    phase = unit * coef_a * freq
    base = phase * sub.astype(F32)
    base_c, base_s = jnp.cos(base), jnp.sin(base)
    for block in range(length // 64):
        first = 8 * block * 8 - half
        step = phase * (first + 8 * sub).astype(F32)
        step_c, step_s = jnp.cos(step), jnp.sin(step)
        for q in range(8):
            sc, ss = step_c[q : q + 1], step_s[q : q + 1]
            c2 = base_c * sc - base_s * ss
            s = base_s * sc + base_c * ss
            rows = pl.ds((block * 8 + q) * 8, 8)
            row_ref[0, rows, :] = jnp.where(lane == 0, 1.0, c2)
            row_ref[1, rows, :] = jnp.where(lane == 0, 0.0, s)
            row_ref[2, rows, :] = c2

    for side in range(2):
        place = (lane + (side * half - half)).astype(F32)
        phase = unit * coef_b * place
        lanes = slice(side * half, side * half + half)
        base = phase * sub.astype(F32)
        base_c, base_s = jnp.cos(base), jnp.sin(base)
        for block in range(half // 64):
            step = phase * (block * 64 + 8 * sub).astype(F32)
            step_c, step_s = jnp.cos(step), jnp.sin(step)
            for q in range(8):
                sc, ss = step_c[q : q + 1], step_s[q : q + 1]
                rows = pl.ds((block * 8 + q) * 8, 8)
                col_ref[0, rows, lanes] = base_c * sc - base_s * ss
                col_ref[1, rows, lanes] = base_s * sc + base_c * ss
        top = jnp.where(sub == 0, jnp.cos(phase * float(half)), base_c)
        nyq_ref[:, lanes] = top


class Tables:
    def __init__(self, row, col, nyq):
        self.row, self.col, self.nyq = row, col, nyq

    def rows(self):
        return self.row[0], self.row[1], self.row[2]

    def chip_rows(self, share):
        here = lax.axis_index("ang")
        other = here + 1 - 2 * lax.rem(here, 2)
        places = [pl.ds(pl.multiple_of(which * share, 8), share) for which in (here, other)]
        return tuple(jnp.concatenate([self.row[part, rows, :] for rows in places], axis=0) for part in range(3))

    def columns(self):
        c1 = self.col[0]
        return c1, self.col[1], jnp.concatenate([self.nyq[...], c1[8:]], axis=0)


def turn_rows(spectrum, tables, sign):
    half = spectrum.shape[1] // 2
    return turn(spectrum[:, :half], spectrum[:, half:], *tables, sign)


def turn_columns(spectrum, tables, sign):
    half = spectrum.shape[0] // 2
    pair = turn(spectrum[:half], spectrum[half:], *tables, sign)
    return jnp.concatenate(pair, axis=0).astype(BF16)


def side_by_side(value, count):
    rows = value.shape[0] // count
    return jnp.concatenate([value[i * rows : (i + 1) * rows] for i in range(count)], axis=1)


def stacked(value, count):
    columns = value.shape[1] // count
    return jnp.concatenate([value[:, i * columns : (i + 1) * columns] for i in range(count)], axis=0)


def block_of(value, i, count, axis):
    size = value.shape[axis] // count
    return lax.slice_in_dim(value, i * size, (i + 1) * size, axis=axis)


def project_slices(slab, count, share, tables, consts, lines_refs):
    forward_ref, inverse_ref, down_ref, up_ref = consts
    here = lax.axis_index("ang")
    spectrum = dot(slab, forward_ref[...])
    for table, lines_ref in zip(tables, lines_refs):
        chip_rows = table.chip_rows(share)
        turned = [
            jnp.concatenate(turn_rows(block_of(spectrum, i, count, 0), chip_rows, 1), axis=1).astype(BF16)
            for i in range(count)
        ]
        first = dot(jnp.concatenate(turned, axis=0), inverse_ref[...]).astype(BF16)
        columns = dot(down_ref[here], side_by_side(first, count))
        turned = [turn_columns(block_of(columns, i, count, 1), table.columns(), 1) for i in range(count)]
        second = dot(up_ref[...], jnp.concatenate(turned, axis=1)).astype(BF16)
        last = dot(stacked(second, count), forward_ref[...])
        for i in range(count):
            re, im = turn_rows(block_of(last, i, count, 0), table.rows(), 1)
            sums = [jnp.sum(part, axis=0, keepdims=True) for part in (re, im)]
            lines_ref[pl.ds(i, 1), :] = jnp.concatenate(sums, axis=1)


def take(refs, *counts):
    refs, out = list(refs), []
    for count in counts:
        out.append(refs[:count])
        refs = refs[count:]
    return out


def as_tables(refs):
    return [Tables(*refs[i : i + 3]) for i in range(0, len(refs), 3)]


def tables_kernel(groups, *refs):
    angle_refs, table_refs = take(refs, groups, 3 * groups)
    for g in range(groups):
        row_ref, col_ref, nyq_ref = table_refs[3 * g : 3 * g + 3]
        fill_turn_tables(angle_refs[g][0], row_ref.shape[1], row_ref, col_ref, nyq_ref)


def edge_kernel(slices, *refs):
    sides, edges = take(refs, 4, 2)
    share = sides[0].shape[0] // slices
    for edge_ref, z in zip(edges, (slices - 1, 0)):
        pieces = [ref[pl.ds(z, share, stride=slices), :].astype(BF16) for ref in sides]
        edge_ref[:share, :] = jnp.concatenate(pieces[:2], axis=1)
        edge_ref[share:, :] = jnp.concatenate(pieces[2:], axis=1)


def project_kernel(groups, slices, *refs):
    angle_refs, sides, (const_ref, down_ref), lines_refs, bases, (slab_ref,), table_refs = take(
        refs, groups, 4, 2, groups, 2, 1, 3 * groups
    )
    share = sides[0].shape[0] // slices
    tables_kernel(groups, *angle_refs, *table_refs)

    def rows(z):
        pieces = [ref[pl.ds(z, share, stride=slices), :] for ref in sides]
        return [jnp.concatenate(pieces[:2], axis=1), jnp.concatenate(pieces[2:], axis=1)]

    slab = []
    past, now = None, rows(0)
    for z in range(slices):
        later = rows(z + 1) if z + 1 < slices else None
        for place in range(2):
            slab.append(now[place].astype(BF16))
            near = [side[place] for side in (past, later) if side is not None]
            base = (1.0 - 2.0 * tau_step * smooth_weight) * now[place]
            base = base + (tau_step * smooth_weight) * sum(near[1:], near[0])
            bases[place][z] = base.astype(bases[place].dtype)
        past, now = now, later
    slab = jnp.concatenate(slab, axis=0)
    slab_ref[...] = slab.reshape(slab_ref.shape)
    consts = [const_ref.at[0], const_ref.at[1], down_ref, const_ref.at[3]]
    project_slices(slab, slices, share, as_tables(table_refs), consts, lines_refs)


def own_line_kernel(pieces, made, *refs):
    slabs, (const_ref, down_ref), given, (line_ref,), table_refs = take(
        refs, pieces, 2, 3 if made else 1, 1, 0 if made else 3
    )
    if not made:
        tables_kernel(1, *given, *table_refs)
    slab = jnp.concatenate([ref[...].reshape(-1, ref.shape[2]) for ref in slabs], axis=0)
    consts = [const_ref.at[0], const_ref.at[1], down_ref, const_ref.at[3]]
    tables = as_tables(given if made else table_refs)
    project_slices(slab, line_ref.shape[0], slabs[0].shape[1] // 2, tables, consts, [line_ref])


def back_kernel(groups, *refs):
    spectra_refs, (const_ref, up_ref), table_refs, (out_ref,) = take(refs, groups, 2, 3 * groups, 1)
    forward_ref, inverse_ref, down_ref = const_ref.at[0], const_ref.at[1], const_ref.at[2]
    slices, pair, length = out_ref.shape
    half = length // 2
    here = lax.axis_index("ang")
    totals = None
    for table, spectra_ref in zip(as_tables(table_refs), spectra_refs):
        turned = []
        for z in range(slices):
            line = spectra_ref[pl.ds(z, 1), :]
            pieces = turn(line[:, :half], line[:, half:], *table.rows(), -1)
            turned.append(jnp.concatenate(pieces, axis=1).astype(BF16))
        spread = dot(jnp.concatenate(turned, axis=0), inverse_ref[...]).astype(BF16)
        columns = dot(down_ref[...], side_by_side(spread, slices))
        turned = [turn_columns(block_of(columns, i, slices, 1), table.columns(), -1) for i in range(slices)]
        second = dot(up_ref[here], jnp.concatenate(turned, axis=1)).astype(BF16)
        last = dot(stacked(second, slices), forward_ref[...])
        chip_rows = table.chip_rows(pair // 2)
        turned = [
            jnp.concatenate(turn_rows(block_of(last, i, slices, 0), chip_rows, -1), axis=1)
            for i in range(slices)
        ]
        totals = turned if totals is None else [old + new for old, new in zip(totals, turned)]
    total = jnp.concatenate([value.astype(BF16) for value in totals], axis=0)
    out_ref[...] = dot(total, inverse_ref[...]).astype(BF16).reshape(out_ref.shape)


def update_kernel(groups, first, last, aliased, *refs):
    bases, halos, shares, (const_ref, down_ref), table_refs, unused, (volume_ref, slab_ref), lines_refs, sides = take(
        refs, 2, 2, 2, 2, 3 * groups, aliased, 2, groups, 2
    )
    consts = [const_ref.at[0], const_ref.at[1], down_ref, const_ref.at[3]]
    own_ref, other_ref = bases
    mine_ref, theirs_ref = shares
    slices, share, length = own_ref.shape
    half = length // 2
    slab = []
    for z in range(slices):
        own = own_ref[z] - tau_step * (
            mine_ref[z, :share, :].astype(F32) + theirs_ref[z, share:, :].astype(F32)
        )
        other = other_ref[z].astype(F32) - tau_step * (
            mine_ref[z, share:, :].astype(F32) + theirs_ref[z, :share, :].astype(F32)
        )
        for needed, halo_ref in ((first and z == 0, halos[0]), (last and z == slices - 1, halos[1])):
            if needed:
                halo = (tau_step * smooth_weight) * halo_ref[...].astype(F32)
                own, other = own + halo[:share], other + halo[share:]
        for side in range(2):
            sides[side][pl.ds(z, share, stride=slices), :] = own[:, side * half : (side + 1) * half]
        slab += [own.astype(BF16), other.astype(BF16)]
    slab = jnp.concatenate(slab, axis=0)
    slab_ref[...] = slab.reshape(slab_ref.shape)
    project_slices(slab, slices, share, as_tables(table_refs), consts, lines_refs)
    whole = jnp.concatenate([ref[...] for ref in sides], axis=1)
    volume_ref[...] = whole.reshape(volume_ref.shape)


def gradient_kernel(
    offsets_ref, image_ref, measured_ref, probe_r_ref, probe_i_ref,
    const_hbm_ref, out_ref, const_ref, sem,
):
    fetch = pltpu.make_async_copy(const_hbm_ref, const_ref, sem)
    fetch.start()
    right_ref, left_ref = const_ref.at[0], const_ref.at[1]
    left_conj_ref, right_conj_ref = right_ref, left_ref
    positions, height, width = measured_ref.shape
    length = image_ref.shape[1]
    image = image_ref[...]
    cos_image, sin_image = jnp.cos(image), jnp.sin(image)
    probe_r, probe_i = probe_r_ref[...], probe_i_ref[...]
    waves = []
    for p in range(positions):
        back = length - offsets_ref[0, p]
        cos_p = pltpu.roll(cos_image, back, 1)[:, :width]
        sin_p = pltpu.roll(sin_image, back, 1)[:, :width]
        waves.append((probe_r * cos_p - probe_i * sin_p, probe_r * sin_p + probe_i * cos_p))

    def to_columns(value):
        parts = [block_of(value, p, positions, 0) for p in range(positions)]
        return jnp.concatenate(
            [jnp.concatenate([part[:, i * width : (i + 1) * width] for part in parts], axis=1) for i in range(2)],
            axis=0,
        )

    def to_rows(value):
        parts = [block_of(value, p, positions, 1) for p in range(positions)]
        return jnp.concatenate(
            [jnp.concatenate([part[:height], part[height:]], axis=1) for part in parts], axis=0
        )

    entry = jnp.concatenate([jnp.concatenate(wave, axis=1) for wave in waves], axis=0)
    fetch.wait()
    far = dot_split(left_ref[...], to_columns(dot_split(entry, right_ref[...])))
    far_r, far_i = far[:height], far[height:]
    measured = jnp.concatenate([measured_ref[p] for p in range(positions)], axis=1)
    misfit = far_r * far_r + far_i * far_i - measured
    weighted = jnp.concatenate([misfit * far_r, misfit * far_i], axis=0)
    chi = dot_split(to_rows(dot_split(left_conj_ref[...], weighted)), right_conj_ref[...])
    total = jnp.zeros((height, length), F32)
    for p in range(positions):
        part = block_of(chi, p, positions, 0)
        wave_r, wave_i = waves[p]
        term = 2.0 * (part[:, width:] * wave_r - part[:, :width] * wave_i)
        padded = jnp.concatenate([term, jnp.zeros((height, length - width), F32)], axis=1)
        total = total + pltpu.roll(padded, offsets_ref[0, p], 1)
    out_ref[...] = total.astype(out_ref.dtype).reshape(out_ref.shape)


def projected(line_refs, inverse_ref):
    line = line_refs[0][...]
    for other in line_refs[1:]:
        line = line + other[...]
    return dot_split(line, inverse_ref[...]) * (1.0 / math.sqrt(line.shape[1]))


def line_kernel(peers, phase_ref, dual_ref, inverse_ref, *refs):
    line_refs, (phase_part_ref, resid_part_ref) = take(refs, peers, 2)
    proj_old = projected(line_refs, inverse_ref)
    phase, dual = phase_ref[...], dual_ref[...]
    phase_part = phase - eta_step * (dual + rho_weight * (phase - proj_old))
    phase_part_ref[...] = phase_part
    resid_part_ref[...] = rho_weight * (proj_old - phase_part) - dual


def phase_kernel(grad_ref, phase_part_ref, resid_part_ref, forward_ref, phase_new_ref, spectrum_ref):
    grad = grad_ref[0].astype(F32)
    for t in range(1, grad_ref.shape[0]):
        grad = grad + grad_ref[t].astype(F32)
    grad = eta_step * grad
    phase_new_ref[...] = phase_part_ref[...] - grad
    resid = resid_part_ref[...] + rho_weight * grad
    spectrum_ref[...] = dot_split(resid, forward_ref[...]) * (1.0 / math.sqrt(resid.shape[1]))


def dual_kernel(peers, phase_ref, dual_ref, inverse_ref, *refs):
    line_refs, (dual_new_ref,) = take(refs, peers, 1)
    proj_new = projected(line_refs, inverse_ref)
    dual_new_ref[...] = dual_ref[...] + rho_weight * (phase_ref[...] - proj_new)


def call(kernel, outs, args, specs=None, out_specs=None, scratch=(), flops=0, name=None, grid=(), aliases=None, vmem=4):
    return pl.pallas_call(
        kernel,
        grid=grid,
        out_shape=tuple(outs),
        in_specs=specs or [VMEM_SPEC] * len(args),
        out_specs=tuple(out_specs or [VMEM_SPEC] * len(outs)),
        scratch_shapes=list(scratch),
        input_output_aliases=aliases or {},
        cost_estimate=pl.CostEstimate(flops=flops, bytes_accessed=1 << 20, transcendentals=0),
        name=name,
        compiler_params=pltpu.CompilerParams(vmem_limit_bytes=vmem * MIB),
    )(*args)


def shards(volume, phase, dual, probe_real, probe_imag, intensity, offsets, angle_index):
    share, slices, length = volume.shape
    width = probe_real.shape[1]
    half = length // 2
    ang = lax.axis_size("ang")
    tiles = lax.axis_size("tile")
    groups = ang // 2
    pair = 2 * share
    parts = 2 if slices % 16 == 0 else 1
    some = slices // parts
    shape = jax.ShapeDtypeStruct

    (forward_full, inverse_full), (forward, inverse) = packed_tables(length)
    forward_full, inverse_full = split_pair(forward_full), split_pair(inverse_full)
    down, up = forward.T, inverse.T
    owners = [
        np.r_[i * share : (i + 1) * share, (i ^ 1) * share : ((i ^ 1) + 1) * share] for i in range(ang)
    ]
    down_part = np.stack([down[:, rows] for rows in owners])
    up_part = np.stack([up[rows] for rows in owners])
    square = np.stack([forward, inverse, down, up])
    right, left = patch_tables(width)
    line = shape((slices, length), F32)
    work = 2 * 2 * length * length * length * slices * groups

    def swap(value):
        return lax.ppermute(value, "ang", [(i, i ^ 1) for i in range(ang)])

    def from_peer(value, j):
        return lax.ppermute(value, "ang", [((i + 2 * j) % ang, i) for i in range(ang)])

    def to_peer(value, j):
        return lax.ppermute(value, "ang", [(i, (i + 2 * j) % ang) for i in range(ang)])

    def lanes(side):
        return pl.BlockSpec((share * slices, half), lambda _: (0, side))

    tables_shape = [
        shape((3, length, half), F32), shape((2, half, length), F32), shape((8, length), F32)
    ] * groups
    block_lines = [
        pl.BlockSpec((some, length), functools.partial(lambda h, _: (h, 0), h)) for h in range(parts)
    ]

    phases = jnp.broadcast_to(phase, (tiles, slices, length))
    phases, volume, angle_sent = lax.optimization_barrier((phases, volume, angle_index))
    image = lax.all_to_all(phases, "tile", split_axis=0, concat_axis=0, tiled=True)
    image = image.reshape(tiles * slices, length)

    flat = volume.reshape(share * slices, length)
    other = swap(flat)
    edges = call(
        functools.partial(edge_kernel, slices),
        [shape((pair, length), BF16)] * 2,
        [flat, flat, other, other],
        [lanes(0), lanes(1)] * 2,
        grid=(1,),
        vmem=6,
        name="edges",
    )
    before = lax.ppermute(edges[0], "tile", [(i, i + 1) for i in range(tiles - 1)])
    after = lax.ppermute(edges[1], "tile", [(i + 1, i) for i in range(tiles - 1)])
    angles = [from_peer(angle_sent, j) for j in range(1, groups)]
    image, before, angles = lax.optimization_barrier((image, before, angles))

    (grad,) = call(
        gradient_kernel,
        [shape((tiles, slices, length), BF16)],
        [offsets, image, intensity[0], probe_real, probe_imag, np.stack([right, left])],
        [SMEM_SPEC] + [VMEM_SPEC] * 4 + [pl.BlockSpec(memory_space=pl.ANY)],
        scratch=[pltpu.VMEM((2,) + right.shape, BF16), pltpu.SemaphoreType.DMA],
        flops=2 * work,
        vmem=12,
        name="gradient",
    )
    grad, after, angles = lax.optimization_barrier((grad, after, angles))
    grad = lax.all_to_all(grad, "tile", split_axis=0, concat_axis=0, tiled=True)

    far = groups - 1
    outs = call(
        functools.partial(project_kernel, far, slices),
        [line] * far
        + [shape((slices, share, length), F32), shape((slices, share, length), BF16)]
        + [shape((slices, pair, length), BF16)],
        angles + [flat, flat, other, other, square, down_part],
        [SMEM_SPEC] * far + [lanes(0), lanes(1)] * 2 + [VMEM_SPEC] * 2,
        scratch=[pltpu.VMEM(t.shape, F32) for t in tables_shape[3:]],
        grid=(1,),
        flops=3 * work * far // groups,
        vmem=28,
        name="project_old",
    )
    lines, bases, slab = take(outs, far, 2, 1)
    old = [to_peer(lines[j], j + 1) for j in range(far)]
    old += call(
        functools.partial(own_line_kernel, 1, False),
        [line],
        slab + [square, down_part, angle_index],
        [VMEM_SPEC] * 3 + [SMEM_SPEC],
        scratch=[pltpu.VMEM(t.shape, F32) for t in tables_shape[:3]],
        flops=3 * work // groups,
        vmem=24,
        name="project_old_own",
    )

    phase_part, resid_part = call(
        functools.partial(line_kernel, groups), [line, line], [phase[0], dual[0], inverse_full] + old,
        name="line_step",
    )
    phase_new, spectrum = call(
        phase_kernel, [line, line], [grad, phase_part, resid_part, forward_full], name="phase_step"
    )
    spectrum, angles = lax.optimization_barrier((spectrum, [angle_index] + angles))
    tables = call(
        functools.partial(tables_kernel, groups), tables_shape, angles, [SMEM_SPEC] * groups,
        flops=work, name="turn_tables",
    )
    tables = list(tables)
    spectra = [spectrum] + [from_peer(spectrum, j) for j in range(1, groups)]

    halves = []
    for h in range(parts):
        (mine,) = call(
            functools.partial(back_kernel, groups),
            [shape((some, pair, length), BF16)],
            spectra + [square, up_part] + tables,
            [block_lines[h]] * groups + [VMEM_SPEC] * (2 + 3 * groups),
            grid=(1,),
            flops=3 * work // parts,
            vmem=24,
            name="backproject",
        )
        halves.append((mine, swap(mine)))

    results, slabs = [], []
    for h in range(parts):
        args = bases + [before, after] + list(halves[h]) + [square, down_part] + tables[3:]
        outs = call(
            functools.partial(update_kernel, far, h == 0, h == parts - 1, len(results)),
            [shape((share, slices, length), F32), shape((some, pair, length), BF16)] + [line] * far,
            args + results,
            [pl.BlockSpec((some, share, length), lambda _, h=h: (h, 0, 0))] * 2
            + [VMEM_SPEC] * (len(args) - 2) + [pl.BlockSpec(memory_space=pl.ANY)] * len(results),
            [pl.BlockSpec((share, some, length), lambda _, h=h: (0, h, 0)), VMEM_SPEC]
            + [block_lines[h]] * far,
            scratch=[pltpu.VMEM((share * some, half), F32)] * 2,
            grid=(1,),
            flops=3 * work * far // groups // parts,
            vmem=24,
            aliases={len(args) + i: i + (1 if i else 0) for i in range(len(results))},
            name="project_new",
        )
        slabs.append(outs[1])
        results = [outs[0]] + list(outs[2:])
    volume_new, lines = results[0], results[1:]
    new = [to_peer(lines[j], j + 1) for j in range(far)]
    new += call(
        functools.partial(own_line_kernel, parts, True),
        [line],
        slabs + [square, down_part] + tables[:3],
        flops=3 * work // groups,
        vmem=24,
        name="project_new_own",
    )
    (dual_new,) = call(
        functools.partial(dual_kernel, groups), [line], [phase_new, dual[0], inverse_full] + new,
        name="dual_step",
    )
    return phase_new[None], volume_new, dual_new[None]


def solution(mesh):
    placed = (
        P("ang", "tile", None),
        P("ang", "tile", None),
        P("ang", "tile", None),
        P(),
        P(),
        P("ang", "tile", None, None),
        P("ang", "tile"),
        P("ang"),
    )
    return jax.shard_map(
        shards,
        mesh=mesh,
        in_specs=placed,
        out_specs=(P("ang", "tile", None), P("ang", "tile", None), P("ang", "tile", None)),
        check_vma=False,
    )
```

```python
import functools
import math

import jax
import jax.numpy as jnp
import numpy as np
from jax import lax
from jax.experimental import pallas as pl
from jax.experimental.pallas import tpu as pltpu
from jax.sharding import PartitionSpec as P

angle_center = 90.0
rho_weight = 1.0
eta_step = 0.01
tau_step = 1.0
smooth_weight = 0.25

F32 = jnp.float32
BF16 = jnp.bfloat16
VMEM_SPEC = pl.BlockSpec(memory_space=pltpu.VMEM)
SMEM_SPEC = pl.BlockSpec(memory_space=pltpu.SMEM)
MIB = 1024 * 1024


def table_pair(length):
    index = np.arange(length)
    phases = (index[:, None] * index[None, :] % length) * (2.0 * np.pi / length)
    return np.cos(phases).astype(np.float32), np.sin(phases).astype(np.float32)


def packed_tables(length):
    half = length // 2
    cos_t, sin_t = table_pair(length)
    bf = np.asarray(jnp.bfloat16).dtype if False else jnp.bfloat16
    out = []
    for kind in (np.float32, bf):
        c = cos_t.astype(kind).astype(np.float32)
        s = sin_t.astype(kind).astype(np.float32)
        forward = np.concatenate([c[:, : half + 1], -s[:, 1:half]], axis=1)
        weight = np.full((length, 1), 2.0 / length, np.float32)
        weight[0] = weight[half] = 1.0 / length
        inverse = forward.T * weight
        out.append((forward.astype(kind), inverse.astype(kind)))
    return out


def split_pair(array):
    high = array.astype(jnp.bfloat16)
    low = (array - high.astype(np.float32)).astype(jnp.bfloat16)
    return np.stack([high, low])


def patch_tables(width):
    cos_t, sin_t = table_pair(width)
    scale = np.float32(math.sqrt(width))
    return np.stack([split_pair(cos_t / scale), split_pair(sin_t / scale)], axis=1)


def dot(left, right):
    return jnp.dot(left, right, preferred_element_type=F32)


def dot_high(left, right):
    return jnp.dot(left, right, precision=lax.Precision.HIGHEST, preferred_element_type=F32)


def dot_split(left, right):
    def parts(value):
        if isinstance(value, list) or value.dtype == BF16:
            return value[0], value[1]
        high = value.astype(BF16)
        return high, (value - high.astype(F32)).astype(BF16)

    left_high, left_low = parts(left)
    right_high, right_low = parts(right)
    return dot(left_high, right_high) + dot(left_low, right_high) + dot(left_high, right_low)


def turn(re, im, c1, s, c2, sign):
    if sign > 0:
        return re * c1 + im * s, im * c2 - re * s
    return re * c1 - im * s, im * c2 + re * s


def fill_turn_tables(angle, length, row_ref, col_ref, nyq_ref):
    half = length // 2
    unit = 2.0 * math.pi / length
    theta = (jnp.full((8, half), angle, jnp.int32).astype(F32) - angle_center) * (math.pi / 360.0)
    coef_a = -(jnp.sin(0.5 * theta) / jnp.cos(0.5 * theta))
    coef_b = jnp.sin(theta)

    lane = lax.broadcasted_iota(jnp.int32, (8, half), 1)
    sub = lax.broadcasted_iota(jnp.int32, (8, half), 0)
    freq = jnp.where(lane == 0, half, lane).astype(F32)
    phase = unit * coef_a * freq
    base = phase * sub.astype(F32)
    base_c, base_s = jnp.cos(base), jnp.sin(base)
    for block in range(length // 64):
        first = 8 * block * 8 - half
        step = phase * (first + 8 * sub).astype(F32)
        step_c, step_s = jnp.cos(step), jnp.sin(step)
        for q in range(8):
            sc, ss = step_c[q : q + 1], step_s[q : q + 1]
            c2 = base_c * sc - base_s * ss
            s = base_s * sc + base_c * ss
            rows = pl.ds((block * 8 + q) * 8, 8)
            row_ref[0, rows, :] = jnp.where(lane == 0, 1.0, c2)
            row_ref[1, rows, :] = jnp.where(lane == 0, 0.0, s)
            row_ref[2, rows, :] = c2

    for side in range(2):
        place = (lane + (side * half - half)).astype(F32)
        phase = unit * coef_b * place
        lanes = slice(side * half, side * half + half)
        base = phase * sub.astype(F32)
        base_c, base_s = jnp.cos(base), jnp.sin(base)
        for block in range(half // 64):
            step = phase * (block * 64 + 8 * sub).astype(F32)
            step_c, step_s = jnp.cos(step), jnp.sin(step)
            for q in range(8):
                sc, ss = step_c[q : q + 1], step_s[q : q + 1]
                rows = pl.ds((block * 8 + q) * 8, 8)
                col_ref[0, rows, lanes] = base_c * sc - base_s * ss
                col_ref[1, rows, lanes] = base_s * sc + base_c * ss
        top = jnp.where(sub == 0, jnp.cos(phase * float(half)), base_c)
        nyq_ref[:, lanes] = top


class Tables:
    def __init__(self, row, col, nyq):
        self.row, self.col, self.nyq = row, col, nyq

    def rows(self):
        return self.row[0], self.row[1], self.row[2]

    def chip_rows(self, share):
        here = lax.axis_index("ang")
        other = here + 1 - 2 * lax.rem(here, 2)
        places = [pl.ds(pl.multiple_of(which * share, 8), share) for which in (here, other)]
        return tuple(jnp.concatenate([self.row[part, rows, :] for rows in places], axis=0) for part in range(3))

    def columns(self):
        c1 = self.col[0]
        return c1, self.col[1], jnp.concatenate([self.nyq[...], c1[8:]], axis=0)


def turn_rows(spectrum, tables, sign):
    half = spectrum.shape[1] // 2
    return turn(spectrum[:, :half], spectrum[:, half:], *tables, sign)


def turn_columns(spectrum, tables, sign):
    half = spectrum.shape[0] // 2
    pair = turn(spectrum[:half], spectrum[half:], *tables, sign)
    return jnp.concatenate(pair, axis=0).astype(BF16)


def side_by_side(value, count):
    rows = value.shape[0] // count
    return jnp.concatenate([value[i * rows : (i + 1) * rows] for i in range(count)], axis=1)


def stacked(value, count):
    columns = value.shape[1] // count
    return jnp.concatenate([value[:, i * columns : (i + 1) * columns] for i in range(count)], axis=0)


def block_of(value, i, count, axis):
    size = value.shape[axis] // count
    return lax.slice_in_dim(value, i * size, (i + 1) * size, axis=axis)


def project_slices(slab, count, share, tables, consts, lines_refs):
    forward_ref, inverse_ref, down_ref, up_ref = consts
    here = lax.axis_index("ang")
    spectrum = dot(slab, forward_ref[...])
    for table, lines_ref in zip(tables, lines_refs):
        chip_rows = table.chip_rows(share)
        turned = [
            jnp.concatenate(turn_rows(block_of(spectrum, i, count, 0), chip_rows, 1), axis=1).astype(BF16)
            for i in range(count)
        ]
        first = dot(jnp.concatenate(turned, axis=0), inverse_ref[...]).astype(BF16)
        columns = dot(down_ref[here], side_by_side(first, count))
        turned = [turn_columns(block_of(columns, i, count, 1), table.columns(), 1) for i in range(count)]
        second = dot(up_ref[...], jnp.concatenate(turned, axis=1)).astype(BF16)
        last = dot(stacked(second, count), forward_ref[...])
        for i in range(count):
            re, im = turn_rows(block_of(last, i, count, 0), table.rows(), 1)
            sums = [jnp.sum(part, axis=0, keepdims=True) for part in (re, im)]
            lines_ref[pl.ds(i, 1), :] = jnp.concatenate(sums, axis=1)


def take(refs, *counts):
    refs, out = list(refs), []
    for count in counts:
        out.append(refs[:count])
        refs = refs[count:]
    return out


def as_tables(refs):
    return [Tables(*refs[i : i + 3]) for i in range(0, len(refs), 3)]


def tables_kernel(groups, *refs):
    angle_refs, table_refs = take(refs, groups, 3 * groups)
    for g in range(groups):
        row_ref, col_ref, nyq_ref = table_refs[3 * g : 3 * g + 3]
        fill_turn_tables(angle_refs[g][0], row_ref.shape[1], row_ref, col_ref, nyq_ref)


def copies_kernel(phase_ref, out_ref):
    out_ref[...] = jnp.broadcast_to(phase_ref[...][None], out_ref.shape)


def edge_kernel(slices, *refs):
    sides, edges = take(refs, 4, 2)
    share = sides[0].shape[0] // slices
    for edge_ref, z in zip(edges, (slices - 1, 0)):
        pieces = [ref[pl.ds(z, share, stride=slices), :].astype(BF16) for ref in sides]
        edge_ref[:share, :] = jnp.concatenate(pieces[:2], axis=1)
        edge_ref[share:, :] = jnp.concatenate(pieces[2:], axis=1)


def project_kernel(groups, slices, *refs):
    angle_refs, sides, (const_ref, down_ref), lines_refs, bases, (slab_ref,), table_refs = take(
        refs, groups, 4, 2, groups, 2, 1, 3 * groups
    )
    share = sides[0].shape[0] // slices
    tables_kernel(groups, *angle_refs, *table_refs)

    def rows(z):
        pieces = [ref[pl.ds(z, share, stride=slices), :] for ref in sides]
        return [jnp.concatenate(pieces[:2], axis=1), jnp.concatenate(pieces[2:], axis=1)]

    slab = []
    past, now = None, rows(0)
    for z in range(slices):
        later = rows(z + 1) if z + 1 < slices else None
        for place in range(2):
            slab.append(now[place].astype(BF16))
            near = [side[place] for side in (past, later) if side is not None]
            base = (1.0 - 2.0 * tau_step * smooth_weight) * now[place]
            base = base + (tau_step * smooth_weight) * sum(near[1:], near[0])
            bases[place][z] = base.astype(bases[place].dtype)
        past, now = now, later
    slab = jnp.concatenate(slab, axis=0)
    slab_ref[...] = slab.reshape(slab_ref.shape)
    consts = [const_ref.at[0], const_ref.at[1], down_ref, const_ref.at[3]]
    project_slices(slab, slices, share, as_tables(table_refs), consts, lines_refs)


def own_line_kernel(pieces, made, aliased, *refs):
    slabs, (const_ref, down_ref), given, unused, (line_ref,), table_refs = take(
        refs, pieces, 2, 3 if made else 1, aliased, 1, 0 if made else 3
    )
    if not made:
        tables_kernel(1, *given, *table_refs)
    slab = jnp.concatenate([ref[...].reshape(-1, ref.shape[2]) for ref in slabs], axis=0)
    consts = [const_ref.at[0], const_ref.at[1], down_ref, const_ref.at[3]]
    tables = as_tables(given if made else table_refs)
    project_slices(slab, line_ref.shape[0], slabs[0].shape[1] // 2, tables, consts, [line_ref])


def back_kernel(groups, *refs):
    spectra_refs, (const_ref, up_ref), table_refs, (out_ref,) = take(refs, groups, 2, 3 * groups, 1)
    forward_ref, inverse_ref, down_ref = const_ref.at[0], const_ref.at[1], const_ref.at[2]
    slices, pair, length = out_ref.shape
    half = length // 2
    here = lax.axis_index("ang")
    totals = None
    for table, spectra_ref in zip(as_tables(table_refs), spectra_refs):
        turned = []
        for z in range(slices):
            line = spectra_ref[pl.ds(z, 1), :]
            pieces = turn(line[:, :half], line[:, half:], *table.rows(), -1)
            turned.append(jnp.concatenate(pieces, axis=1).astype(BF16))
        spread = dot(jnp.concatenate(turned, axis=0), inverse_ref[...]).astype(BF16)
        columns = dot(down_ref[...], side_by_side(spread, slices))
        turned = [turn_columns(block_of(columns, i, slices, 1), table.columns(), -1) for i in range(slices)]
        second = dot(up_ref[here], jnp.concatenate(turned, axis=1)).astype(BF16)
        last = dot(stacked(second, slices), forward_ref[...])
        chip_rows = table.chip_rows(pair // 2)
        turned = [
            jnp.concatenate(turn_rows(block_of(last, i, slices, 0), chip_rows, -1), axis=1)
            for i in range(slices)
        ]
        totals = turned if totals is None else [old + new for old, new in zip(totals, turned)]
    total = jnp.concatenate([value.astype(BF16) for value in totals], axis=0)
    out_ref[...] = dot(total, inverse_ref[...]).astype(BF16).reshape(out_ref.shape)


def update_kernel(groups, first, last, aliased, *refs):
    bases, halos, shares, (const_ref, down_ref), table_refs, unused, (volume_ref,), lines_refs, slabs, sides = take(
        refs, 2, 2, 2, 2, 3 * groups, aliased, 1, groups, 1 if last else 0, 2
    )
    consts = [const_ref.at[0], const_ref.at[1], down_ref, const_ref.at[3]]
    own_ref, other_ref = bases
    mine_ref, theirs_ref = shares
    slices, share, length = own_ref.shape
    half = length // 2
    slab = []
    for z in range(slices):
        own = own_ref[z] - tau_step * (
            mine_ref[z, :share, :].astype(F32) + theirs_ref[z, share:, :].astype(F32)
        )
        other = other_ref[z].astype(F32) - tau_step * (
            mine_ref[z, share:, :].astype(F32) + theirs_ref[z, :share, :].astype(F32)
        )
        for needed, halo_ref in ((first and z == 0, halos[0]), (last and z == slices - 1, halos[1])):
            if needed:
                halo = (tau_step * smooth_weight) * halo_ref[...].astype(F32)
                own, other = own + halo[:share], other + halo[share:]
        for side in range(2):
            sides[side][pl.ds(z, share, stride=slices), :] = own[:, side * half : (side + 1) * half]
        slab += [own.astype(BF16), other.astype(BF16)]
    slab = jnp.concatenate(slab, axis=0)
    for slab_ref in slabs:
        slab_ref[...] = slab.reshape(slab_ref.shape)
    project_slices(slab, slices, share, as_tables(table_refs), consts, lines_refs)
    whole = jnp.concatenate([ref[...] for ref in sides], axis=1)
    volume_ref[...] = whole.reshape(volume_ref.shape)


def gradient_kernel(
    offsets_ref, image_ref, measured_ref, probe_r_ref, probe_i_ref,
    const_ref, out_ref,
):
    right, left = [], []
    for part in range(2):
        c, s = const_ref[part, 0], const_ref[part, 1]
        plus = [jnp.concatenate([c, s], axis=1), jnp.concatenate([-s, c], axis=1)]
        minus = [jnp.concatenate([c, -s], axis=1), jnp.concatenate([s, c], axis=1)]
        left.append(jnp.concatenate(plus, axis=0))
        right.append(jnp.concatenate(minus, axis=0))
    positions, height, width = measured_ref.shape
    length = image_ref.shape[1]
    image = image_ref[...]
    cos_image, sin_image = jnp.cos(image), jnp.sin(image)
    probe_r, probe_i = probe_r_ref[...], probe_i_ref[...]
    waves = []
    for p in range(positions):
        back = length - offsets_ref[p]
        cos_p = pltpu.roll(cos_image, back, 1)[:, :width]
        sin_p = pltpu.roll(sin_image, back, 1)[:, :width]
        waves.append((probe_r * cos_p - probe_i * sin_p, probe_r * sin_p + probe_i * cos_p))

    def to_columns(value):
        parts = [block_of(value, p, positions, 0) for p in range(positions)]
        return jnp.concatenate(
            [jnp.concatenate([part[:, i * width : (i + 1) * width] for part in parts], axis=1) for i in range(2)],
            axis=0,
        )

    def to_rows(value):
        parts = [block_of(value, p, positions, 1) for p in range(positions)]
        return jnp.concatenate(
            [jnp.concatenate([part[:height], part[height:]], axis=1) for part in parts], axis=0
        )

    entry = jnp.concatenate([jnp.concatenate(wave, axis=1) for wave in waves], axis=0)
    far = dot_split(left, to_columns(dot_split(entry, right)))
    far_r, far_i = far[:height], far[height:]
    measured = jnp.concatenate([measured_ref[p] for p in range(positions)], axis=1)
    misfit = far_r * far_r + far_i * far_i - measured
    weighted = jnp.concatenate([misfit * far_r, misfit * far_i], axis=0)
    chi = dot_split(to_rows(dot_split(right, weighted)), left)
    total = jnp.zeros((height, length), F32)
    for p in range(positions):
        part = block_of(chi, p, positions, 0)
        wave_r, wave_i = waves[p]
        term = 2.0 * (part[:, width:] * wave_r - part[:, :width] * wave_i)
        padded = jnp.concatenate([term, jnp.zeros((height, length - width), F32)], axis=1)
        total = total + pltpu.roll(padded, offsets_ref[p], 1)
    out_ref[...] = total.astype(out_ref.dtype).reshape(out_ref.shape)


def projected(line_refs, inverse_ref):
    line = line_refs[0][...]
    for other in line_refs[1:]:
        line = line + other[...]
    return dot_split(line, inverse_ref[...]) * (1.0 / math.sqrt(line.shape[1]))


def line_kernel(peers, phase_ref, dual_ref, inverse_ref, *refs):
    line_refs, (phase_part_ref, resid_part_ref) = take(refs, peers, 2)
    proj_old = projected(line_refs, inverse_ref)
    phase, dual = phase_ref[...], dual_ref[...]
    phase_part = phase - eta_step * (dual + rho_weight * (phase - proj_old))
    phase_part_ref[...] = phase_part
    resid_part_ref[...] = rho_weight * (proj_old - phase_part) - dual


def phase_kernel(grad_ref, phase_part_ref, resid_part_ref, forward_ref, phase_new_ref, spectrum_ref):
    grad = grad_ref[0].astype(F32)
    for t in range(1, grad_ref.shape[0]):
        grad = grad + grad_ref[t].astype(F32)
    grad = eta_step * grad
    phase_new_ref[...] = phase_part_ref[...] - grad
    resid = resid_part_ref[...] + rho_weight * grad
    spectrum_ref[...] = dot_split(resid, forward_ref[...]) * (1.0 / math.sqrt(resid.shape[1]))


def dual_kernel(peers, phase_ref, dual_ref, inverse_ref, *refs):
    line_refs, (dual_new_ref,) = take(refs, peers, 1)
    proj_new = projected(line_refs, inverse_ref)
    dual_new_ref[...] = dual_ref[...] + rho_weight * (phase_ref[...] - proj_new)


def call(kernel, outs, args, specs=None, out_specs=None, scratch=(), flops=0, name=None, grid=(), aliases=None, vmem=4):
    return pl.pallas_call(
        kernel,
        grid=grid,
        out_shape=tuple(outs),
        in_specs=specs or [VMEM_SPEC] * len(args),
        out_specs=tuple(out_specs or [VMEM_SPEC] * len(outs)),
        scratch_shapes=list(scratch),
        input_output_aliases=aliases or {},
        cost_estimate=pl.CostEstimate(flops=flops, bytes_accessed=1 << 20, transcendentals=0),
        name=name,
        compiler_params=pltpu.CompilerParams(vmem_limit_bytes=vmem * MIB),
    )(*args)


def shards(volume, phase, dual, probe_real, probe_imag, intensity, offsets, angle_index):
    share, slices, length = volume.shape
    width = probe_real.shape[1]
    half = length // 2
    ang = lax.axis_size("ang")
    tiles = lax.axis_size("tile")
    groups = ang // 2
    pair = 2 * share
    parts = 2 if slices % 16 == 0 else 1
    some = slices // parts
    shape = jax.ShapeDtypeStruct

    (forward_full, inverse_full), (forward, inverse) = packed_tables(length)
    forward_full, inverse_full = split_pair(forward_full), split_pair(inverse_full)
    down, up = forward.T, inverse.T
    owners = [
        np.r_[i * share : (i + 1) * share, (i ^ 1) * share : ((i ^ 1) + 1) * share] for i in range(ang)
    ]
    down_part = np.stack([down[:, rows] for rows in owners])
    up_part = np.stack([up[rows] for rows in owners])
    square = np.stack([forward, inverse, down, up])
    line = shape((slices, length), F32)
    work = 2 * 2 * length * length * length * slices * groups

    def swap(value):
        return lax.ppermute(value, "ang", [(i, i ^ 1) for i in range(ang)])

    def from_peer(value, j):
        return lax.ppermute(value, "ang", [((i + 2 * j) % ang, i) for i in range(ang)])

    def to_peer(value, j):
        return lax.ppermute(value, "ang", [(i, (i + 2 * j) % ang) for i in range(ang)])

    def lanes(side):
        return pl.BlockSpec((share * slices, half), lambda _: (0, side))

    tables_shape = [
        shape((3, length, half), F32), shape((2, half, length), F32), shape((8, length), F32)
    ] * groups
    block_lines = [
        pl.BlockSpec((some, length), functools.partial(lambda h, _: (h, 0), h)) for h in range(parts)
    ]

    (phases,) = call(copies_kernel, [shape((tiles, slices, length), F32)], [phase[0]], name="phase_copies")
    phases, volume, angle_sent = lax.optimization_barrier((phases, volume, angle_index))
    image = lax.all_to_all(phases, "tile", split_axis=0, concat_axis=0, tiled=True)
    image = image.reshape(tiles * slices, length)

    flat = volume.reshape(share * slices, length)
    other = swap(flat)
    edges = call(
        functools.partial(edge_kernel, slices),
        [shape((pair, length), BF16)] * 2,
        [flat, flat, other, other],
        [lanes(0), lanes(1)] * 2,
        grid=(1,),
        vmem=6,
        name="edges",
    )
    before = lax.ppermute(edges[0], "tile", [(i, i + 1) for i in range(tiles - 1)])
    after = lax.ppermute(edges[1], "tile", [(i + 1, i) for i in range(tiles - 1)])
    angles = [from_peer(angle_sent, j) for j in range(1, groups)]
    image, before, angles = lax.optimization_barrier((image, before, angles))

    (grad,) = call(
        gradient_kernel,
        [shape((tiles, slices, length), BF16)],
        [offsets[0], image, intensity[0], probe_real, probe_imag, patch_tables(width)],
        [SMEM_SPEC] + [VMEM_SPEC] * 5,
        flops=2 * work,
        vmem=12,
        name="gradient",
    )
    grad, after, angles = lax.optimization_barrier((grad, after, angles))
    grad = lax.all_to_all(grad, "tile", split_axis=0, concat_axis=0, tiled=True)

    far = groups - 1
    outs = call(
        functools.partial(project_kernel, far, slices),
        [line] * far
        + [shape((slices, share, length), F32), shape((slices, share, length), BF16)]
        + [shape((slices, pair, length), BF16)],
        angles + [flat, flat, other, other, square, down_part],
        [SMEM_SPEC] * far + [lanes(0), lanes(1)] * 2 + [VMEM_SPEC] * 2,
        scratch=[pltpu.VMEM(t.shape, F32) for t in tables_shape[3:]],
        grid=(1,),
        flops=3 * work * far // groups,
        vmem=28,
        name="project_old",
    )
    lines, bases, slab = take(outs, far, 2, 1)
    old = [to_peer(lines[j], j + 1) for j in range(far)]
    old += call(
        functools.partial(own_line_kernel, 1, False, 0),
        [line],
        slab + [square, down_part, angle_index],
        [VMEM_SPEC] * 3 + [SMEM_SPEC],
        scratch=[pltpu.VMEM(t.shape, F32) for t in tables_shape[:3]],
        flops=3 * work // groups,
        vmem=24,
        name="project_old_own",
    )

    phase_part, resid_part = call(
        functools.partial(line_kernel, groups), [line, line], [phase[0], dual[0], inverse_full] + old,
        name="line_step",
    )
    phase_new, spectrum = call(
        phase_kernel, [line, line], [grad, phase_part, resid_part, forward_full], name="phase_step"
    )
    spectrum, angles = lax.optimization_barrier((spectrum, [angle_index] + angles))
    tables = call(
        functools.partial(tables_kernel, groups), tables_shape, angles, [SMEM_SPEC] * groups,
        flops=work, name="turn_tables",
    )
    tables = list(tables)
    spectra = [spectrum] + [from_peer(spectrum, j) for j in range(1, groups)]

    halves = []
    for h in range(parts):
        (mine,) = call(
            functools.partial(back_kernel, groups),
            [shape((some, pair, length), BF16)],
            spectra + [square, up_part] + tables,
            [block_lines[h]] * groups + [VMEM_SPEC] * (2 + 3 * groups),
            grid=(1,),
            flops=3 * work // parts,
            vmem=24,
            name="backproject",
        )
        halves.append((mine, swap(mine)))

    results = []
    for h in range(parts):
        last = h == parts - 1
        count = far if last else groups
        args = bases + [before, after] + list(halves[h]) + [square, down_part]
        args = args + (tables[3:] if last else tables[3:] + tables[:3])
        carried = results[: 1 + count]
        outs = call(
            functools.partial(update_kernel, count, h == 0, last, len(carried)),
            [shape((share, slices, length), F32)]
            + [line] * count
            + ([shape((some, pair, length), BF16)] if last else []),
            args + carried,
            [pl.BlockSpec((some, share, length), lambda _, h=h: (h, 0, 0))] * 2
            + [VMEM_SPEC] * (len(args) - 2) + [pl.BlockSpec(memory_space=pl.ANY)] * len(carried),
            [pl.BlockSpec((share, some, length), lambda _, h=h: (0, h, 0))]
            + [block_lines[h]] * count
            + ([VMEM_SPEC] if last else []),
            scratch=[pltpu.VMEM((share * some, half), F32)] * 2,
            grid=(1,),
            flops=3 * work * count // groups // parts,
            vmem=24,
            aliases={len(args) + i: i for i in range(len(carried))},
            name="project_new",
        )
        results = list(outs[: 1 + count]) + results[1 + count :]
    volume_new, lines, slab = results[0], results[1:groups], outs[-1]
    new = [to_peer(lines[j], j + 1) for j in range(far)]
    own_line = results[groups:]
    args = [slab, square, down_part] + tables[:3] + own_line
    new += call(
        functools.partial(own_line_kernel, 1, True, len(own_line)),
        [line],
        args,
        [VMEM_SPEC] * 6 + [pl.BlockSpec(memory_space=pl.ANY)] * len(own_line),
        [block_lines[parts - 1]],
        grid=(1,),
        flops=3 * work // groups // parts,
        vmem=24,
        aliases={6: 0} if own_line else None,
        name="project_new_own",
    )
    (dual_new,) = call(
        functools.partial(dual_kernel, groups), [line], [phase_new, dual[0], inverse_full] + new,
        name="dual_step",
    )
    return phase_new[None], volume_new, dual_new[None]


def solution(mesh):
    placed = (
        P("ang", "tile", None),
        P("ang", "tile", None),
        P("ang", "tile", None),
        P(),
        P(),
        P("ang", "tile", None, None),
        P("ang", "tile"),
        P("ang"),
    )
    return jax.shard_map(
        shards,
        mesh=mesh,
        in_specs=placed,
        out_specs=(P("ang", "tile", None), P("ang", "tile", None), P("ang", "tile", None)),
        check_vma=False,
    )
```

```python
import functools
import math

import jax
import jax.numpy as jnp
import numpy as np
from jax import lax
from jax.experimental import pallas as pl
from jax.experimental.pallas import tpu as pltpu
from jax.sharding import PartitionSpec as P

angle_center = 90.0
rho_weight = 1.0
eta_step = 0.01
tau_step = 1.0
smooth_weight = 0.25

F32 = jnp.float32
BF16 = jnp.bfloat16
VMEM_SPEC = pl.BlockSpec(memory_space=pltpu.VMEM)
SMEM_SPEC = pl.BlockSpec(memory_space=pltpu.SMEM)
MIB = 1024 * 1024


def table_pair(length):
    index = np.arange(length)
    phases = (index[:, None] * index[None, :] % length) * (2.0 * np.pi / length)
    return np.cos(phases).astype(np.float32), np.sin(phases).astype(np.float32)


def packed_tables(length):
    half = length // 2
    cos_t, sin_t = table_pair(length)
    bf = np.asarray(jnp.bfloat16).dtype if False else jnp.bfloat16
    out = []
    for kind in (np.float32, bf):
        c = cos_t.astype(kind).astype(np.float32)
        s = sin_t.astype(kind).astype(np.float32)
        forward = np.concatenate([c[:, : half + 1], -s[:, 1:half]], axis=1)
        weight = np.full((length, 1), 2.0 / length, np.float32)
        weight[0] = weight[half] = 1.0 / length
        inverse = forward.T * weight
        out.append((forward.astype(kind), inverse.astype(kind)))
    return out


def split_pair(array):
    high = array.astype(jnp.bfloat16)
    low = (array - high.astype(np.float32)).astype(jnp.bfloat16)
    return np.stack([high, low])


def patch_tables(width):
    cos_t, sin_t = table_pair(width)
    scale = np.float32(math.sqrt(width))
    return np.stack([split_pair(cos_t / scale), split_pair(sin_t / scale)], axis=1)


def dot(left, right):
    return jnp.dot(left, right, preferred_element_type=F32)


def dot_high(left, right):
    return jnp.dot(left, right, precision=lax.Precision.HIGHEST, preferred_element_type=F32)


def dot_split(left, right):
    def parts(value):
        if isinstance(value, list) or value.dtype == BF16:
            return value[0], value[1]
        high = value.astype(BF16)
        return high, (value - high.astype(F32)).astype(BF16)

    left_high, left_low = parts(left)
    right_high, right_low = parts(right)
    return dot(
        jnp.concatenate([left_high, left_low, left_high], axis=1),
        jnp.concatenate([right_high, right_high, right_low], axis=0),
    )


def turn(re, im, c1, s, c2, sign):
    if sign > 0:
        return re * c1 + im * s, im * c2 - re * s
    return re * c1 - im * s, im * c2 + re * s


def fill_turn_tables(angle, length, row_ref, col_ref, nyq_ref):
    half = length // 2
    unit = 2.0 * math.pi / length
    theta = (jnp.full((8, half), angle, jnp.int32).astype(F32) - angle_center) * (math.pi / 360.0)
    coef_a = -(jnp.sin(0.5 * theta) / jnp.cos(0.5 * theta))
    coef_b = jnp.sin(theta)

    lane = lax.broadcasted_iota(jnp.int32, (8, half), 1)
    sub = lax.broadcasted_iota(jnp.int32, (8, half), 0)
    freq = jnp.where(lane == 0, half, lane).astype(F32)
    phase = unit * coef_a * freq
    base = phase * sub.astype(F32)
    base_c, base_s = jnp.cos(base), jnp.sin(base)
    for block in range(length // 64):
        first = 8 * block * 8 - half
        step = phase * (first + 8 * sub).astype(F32)
        step_c, step_s = jnp.cos(step), jnp.sin(step)
        for q in range(8):
            sc, ss = step_c[q : q + 1], step_s[q : q + 1]
            c2 = base_c * sc - base_s * ss
            s = base_s * sc + base_c * ss
            rows = pl.ds((block * 8 + q) * 8, 8)
            row_ref[0, rows, :] = jnp.where(lane == 0, 1.0, c2)
            row_ref[1, rows, :] = jnp.where(lane == 0, 0.0, s)
            row_ref[2, rows, :] = c2

    for side in range(2):
        place = (lane + (side * half - half)).astype(F32)
        phase = unit * coef_b * place
        lanes = slice(side * half, side * half + half)
        base = phase * sub.astype(F32)
        base_c, base_s = jnp.cos(base), jnp.sin(base)
        for block in range(half // 64):
            step = phase * (block * 64 + 8 * sub).astype(F32)
            step_c, step_s = jnp.cos(step), jnp.sin(step)
            for q in range(8):
                sc, ss = step_c[q : q + 1], step_s[q : q + 1]
                rows = pl.ds((block * 8 + q) * 8, 8)
                col_ref[0, rows, lanes] = base_c * sc - base_s * ss
                col_ref[1, rows, lanes] = base_s * sc + base_c * ss
        top = jnp.where(sub == 0, jnp.cos(phase * float(half)), base_c)
        nyq_ref[:, lanes] = top


def chip_places(share):
    here = lax.axis_index("ang")
    other = here + 1 - 2 * lax.rem(here, 2)
    return [pl.ds(pl.multiple_of(which * share, share), share) for which in (here, other)]


def chip_table(table_ref, share):
    return jnp.concatenate([table_ref[rows, :] for rows in chip_places(share)], axis=0)


class Tables:
    def __init__(self, row, col, nyq):
        self.row, self.col, self.nyq = row, col, nyq

    def rows(self):
        return self.row[0], self.row[1], self.row[2]

    def chip_rows(self, share):
        return tuple(chip_table(self.row.at[part], share) for part in range(3))

    def columns(self):
        c1 = self.col[0]
        return c1, self.col[1], jnp.concatenate([self.nyq[...], c1[8:]], axis=0)


def turn_rows(spectrum, tables, sign):
    half = spectrum.shape[1] // 2
    return turn(spectrum[:, :half], spectrum[:, half:], *tables, sign)


def turn_columns(spectrum, tables, sign):
    half = spectrum.shape[0] // 2
    pair = turn(spectrum[:half], spectrum[half:], *tables, sign)
    return jnp.concatenate(pair, axis=0).astype(BF16)


def side_by_side(value, count):
    rows = value.shape[0] // count
    return jnp.concatenate([value[i * rows : (i + 1) * rows] for i in range(count)], axis=1)


def stacked(value, count):
    columns = value.shape[1] // count
    return jnp.concatenate([value[:, i * columns : (i + 1) * columns] for i in range(count)], axis=0)


def block_of(value, i, count, axis):
    size = value.shape[axis] // count
    return lax.slice_in_dim(value, i * size, (i + 1) * size, axis=axis)


def project_slices(slab, count, share, tables, consts, lines_refs):
    forward_ref, inverse_ref, up_ref = consts
    down = jnp.transpose(chip_table(forward_ref, share).astype(F32)).astype(BF16)
    spectrum = dot(slab, forward_ref[...])
    for table, lines_ref in zip(tables, lines_refs):
        chip_rows = table.chip_rows(share)
        turned = [
            jnp.concatenate(turn_rows(block_of(spectrum, i, count, 0), chip_rows, 1), axis=1).astype(BF16)
            for i in range(count)
        ]
        first = dot(jnp.concatenate(turned, axis=0), inverse_ref[...]).astype(BF16)
        columns = dot(down, side_by_side(first, count))
        turned = [turn_columns(block_of(columns, i, count, 1), table.columns(), 1) for i in range(count)]
        second = dot(up_ref[...], jnp.concatenate(turned, axis=1)).astype(BF16)
        last = dot(stacked(second, count), forward_ref[...])
        for i in range(count):
            re, im = turn_rows(block_of(last, i, count, 0), table.rows(), 1)
            sums = [jnp.sum(part, axis=0, keepdims=True) for part in (re, im)]
            lines_ref[pl.ds(i, 1), :] = jnp.concatenate(sums, axis=1)


def take(refs, *counts):
    refs, out = list(refs), []
    for count in counts:
        out.append(refs[:count])
        refs = refs[count:]
    return out


def as_tables(refs):
    return [Tables(*refs[i : i + 3]) for i in range(0, len(refs), 3)]


def tables_kernel(groups, *refs):
    angle_refs, table_refs = take(refs, groups, 3 * groups)
    for g in range(groups):
        row_ref, col_ref, nyq_ref = table_refs[3 * g : 3 * g + 3]
        fill_turn_tables(angle_refs[g][0], row_ref.shape[1], row_ref, col_ref, nyq_ref)


def copies_kernel(phase_ref, out_ref):
    out_ref[...] = jnp.broadcast_to(phase_ref[...][None], out_ref.shape)


def edge_kernel(slices, *refs):
    sides, edges = take(refs, 4, 2)
    share = sides[0].shape[0] // slices
    for edge_ref, z in zip(edges, (slices - 1, 0)):
        pieces = [ref[pl.ds(z, share, stride=slices), :].astype(BF16) for ref in sides]
        edge_ref[:share, :] = jnp.concatenate(pieces[:2], axis=1)
        edge_ref[share:, :] = jnp.concatenate(pieces[2:], axis=1)


def project_kernel(groups, slices, *refs):
    angle_refs, sides, (const_ref,), lines_refs, bases, (slab_ref,), table_refs = take(
        refs, groups, 4, 1, groups, 2, 1, 3 * groups
    )
    share = sides[0].shape[0] // slices
    tables_kernel(groups, *angle_refs, *table_refs)

    def rows(z):
        pieces = [ref[pl.ds(z, share, stride=slices), :] for ref in sides]
        return [jnp.concatenate(pieces[:2], axis=1), jnp.concatenate(pieces[2:], axis=1)]

    slab = []
    past, now = None, rows(0)
    for z in range(slices):
        later = rows(z + 1) if z + 1 < slices else None
        for place in range(2):
            slab.append(now[place].astype(BF16))
            near = [side[place] for side in (past, later) if side is not None]
            base = (1.0 - 2.0 * tau_step * smooth_weight) * now[place]
            base = base + (tau_step * smooth_weight) * sum(near[1:], near[0])
            bases[place][z] = base.astype(bases[place].dtype)
        past, now = now, later
    slab = jnp.concatenate(slab, axis=0)
    slab_ref[...] = slab.reshape(slab_ref.shape)
    consts = [const_ref.at[0], const_ref.at[1], const_ref.at[3]]
    project_slices(slab, slices, share, as_tables(table_refs), consts, lines_refs)


def own_line_kernel(pieces, made, aliased, *refs):
    slabs, (const_ref,), given, unused, (line_ref,), table_refs = take(
        refs, pieces, 1, 3 if made else 1, aliased, 1, 0 if made else 3
    )
    if not made:
        tables_kernel(1, *given, *table_refs)
    slab = jnp.concatenate([ref[...].reshape(-1, ref.shape[2]) for ref in slabs], axis=0)
    consts = [const_ref.at[0], const_ref.at[1], const_ref.at[3]]
    tables = as_tables(given if made else table_refs)
    project_slices(slab, line_ref.shape[0], slabs[0].shape[1] // 2, tables, consts, [line_ref])


def back_kernel(groups, *refs):
    spectra_refs, (const_ref,), table_refs, (out_ref,) = take(refs, groups, 1, 3 * groups, 1)
    forward_ref, inverse_ref, down_ref = const_ref.at[0], const_ref.at[1], const_ref.at[2]
    slices, pair, length = out_ref.shape
    half = length // 2
    up = chip_table(const_ref.at[3], pair // 2)
    totals = None
    for table, spectra_ref in zip(as_tables(table_refs), spectra_refs):
        turned = []
        for z in range(slices):
            line = spectra_ref[pl.ds(z, 1), :]
            pieces = turn(line[:, :half], line[:, half:], *table.rows(), -1)
            turned.append(jnp.concatenate(pieces, axis=1).astype(BF16))
        spread = dot(jnp.concatenate(turned, axis=0), inverse_ref[...]).astype(BF16)
        columns = dot(down_ref[...], side_by_side(spread, slices))
        turned = [turn_columns(block_of(columns, i, slices, 1), table.columns(), -1) for i in range(slices)]
        second = dot(up, jnp.concatenate(turned, axis=1)).astype(BF16)
        last = dot(stacked(second, slices), forward_ref[...])
        chip_rows = table.chip_rows(pair // 2)
        turned = [
            jnp.concatenate(turn_rows(block_of(last, i, slices, 0), chip_rows, -1), axis=1)
            for i in range(slices)
        ]
        totals = turned if totals is None else [old + new for old, new in zip(totals, turned)]
    total = jnp.concatenate([value.astype(BF16) for value in totals], axis=0)
    out_ref[...] = dot(total, inverse_ref[...]).astype(BF16).reshape(out_ref.shape)


def update_kernel(groups, first, last, aliased, *refs):
    bases, halos, shares, (const_ref,), table_refs, unused, (volume_ref,), lines_refs, slabs, sides = take(
        refs, 2, 2, 2, 1, 3 * groups, aliased, 1, groups, 1 if last else 0, 2
    )
    consts = [const_ref.at[0], const_ref.at[1], const_ref.at[3]]
    own_ref, other_ref = bases
    mine_ref, theirs_ref = shares
    slices, share, length = own_ref.shape
    half = length // 2
    slab = []
    for z in range(slices):
        own = own_ref[z] - tau_step * (
            mine_ref[z, :share, :].astype(F32) + theirs_ref[z, share:, :].astype(F32)
        )
        other = other_ref[z].astype(F32) - tau_step * (
            mine_ref[z, share:, :].astype(F32) + theirs_ref[z, :share, :].astype(F32)
        )
        for needed, halo_ref in ((first and z == 0, halos[0]), (last and z == slices - 1, halos[1])):
            if needed:
                halo = (tau_step * smooth_weight) * halo_ref[...].astype(F32)
                own, other = own + halo[:share], other + halo[share:]
        for side in range(2):
            sides[side][pl.ds(z, share, stride=slices), :] = own[:, side * half : (side + 1) * half]
        slab += [own.astype(BF16), other.astype(BF16)]
    slab = jnp.concatenate(slab, axis=0)
    for slab_ref in slabs:
        slab_ref[...] = slab.reshape(slab_ref.shape)
    project_slices(slab, slices, share, as_tables(table_refs), consts, lines_refs)
    whole = jnp.concatenate([ref[...] for ref in sides], axis=1)
    volume_ref[...] = whole.reshape(volume_ref.shape)


def gradient_kernel(
    offsets_ref, image_ref, measured_ref, probe_r_ref, probe_i_ref,
    const_ref, out_ref,
):
    right, left = [], []
    for part in range(2):
        c, s = const_ref[part, 0], const_ref[part, 1]
        plus = [jnp.concatenate([c, s], axis=1), jnp.concatenate([-s, c], axis=1)]
        minus = [jnp.concatenate([c, -s], axis=1), jnp.concatenate([s, c], axis=1)]
        left.append(jnp.concatenate(plus, axis=0))
        right.append(jnp.concatenate(minus, axis=0))
    positions, height, width = measured_ref.shape
    length = image_ref.shape[1]
    image = image_ref[...]
    cos_image, sin_image = jnp.cos(image), jnp.sin(image)
    probe_r, probe_i = probe_r_ref[...], probe_i_ref[...]
    waves = []
    for p in range(positions):
        back = length - offsets_ref[p]
        cos_p = pltpu.roll(cos_image, back, 1)[:, :width]
        sin_p = pltpu.roll(sin_image, back, 1)[:, :width]
        waves.append((probe_r * cos_p - probe_i * sin_p, probe_r * sin_p + probe_i * cos_p))

    def to_columns(value):
        parts = [block_of(value, p, positions, 0) for p in range(positions)]
        return jnp.concatenate(
            [jnp.concatenate([part[:, i * width : (i + 1) * width] for part in parts], axis=1) for i in range(2)],
            axis=0,
        )

    def to_rows(value):
        parts = [block_of(value, p, positions, 1) for p in range(positions)]
        return jnp.concatenate(
            [jnp.concatenate([part[:height], part[height:]], axis=1) for part in parts], axis=0
        )

    entry = jnp.concatenate([jnp.concatenate(wave, axis=1) for wave in waves], axis=0)
    far = dot_split(left, to_columns(dot_split(entry, right)))
    far_r, far_i = far[:height], far[height:]
    measured = jnp.concatenate([measured_ref[p] for p in range(positions)], axis=1)
    misfit = far_r * far_r + far_i * far_i - measured
    weighted = jnp.concatenate([misfit * far_r, misfit * far_i], axis=0)
    chi = dot_split(to_rows(dot_split(right, weighted)), left)
    total = jnp.zeros((height, length), F32)
    for p in range(positions):
        part = block_of(chi, p, positions, 0)
        wave_r, wave_i = waves[p]
        term = 2.0 * (part[:, width:] * wave_r - part[:, :width] * wave_i)
        padded = jnp.concatenate([term, jnp.zeros((height, length - width), F32)], axis=1)
        total = total + pltpu.roll(padded, offsets_ref[p], 1)
    out_ref[...] = total.astype(out_ref.dtype).reshape(out_ref.shape)


def projected(line_refs, inverse_ref):
    line = line_refs[0][...]
    for other in line_refs[1:]:
        line = line + other[...]
    return dot_split(line, inverse_ref[...]) * (1.0 / math.sqrt(line.shape[1]))


def line_kernel(peers, phase_ref, dual_ref, full_ref, *refs):
    line_refs, (phase_part_ref, resid_part_ref) = take(refs, peers, 2)
    proj_old = projected(line_refs, full_ref.at[1])
    phase, dual = phase_ref[...], dual_ref[...]
    phase_part = phase - eta_step * (dual + rho_weight * (phase - proj_old))
    phase_part_ref[...] = phase_part
    resid_part_ref[...] = rho_weight * (proj_old - phase_part) - dual


def phase_kernel(grad_ref, phase_part_ref, resid_part_ref, full_ref, phase_new_ref, spectrum_ref):
    grad = grad_ref[0].astype(F32)
    for t in range(1, grad_ref.shape[0]):
        grad = grad + grad_ref[t].astype(F32)
    grad = eta_step * grad
    phase_new_ref[...] = phase_part_ref[...] - grad
    resid = resid_part_ref[...] + rho_weight * grad
    spectrum_ref[...] = dot_split(resid, full_ref[0]) * (1.0 / math.sqrt(resid.shape[1]))


def dual_kernel(peers, phase_ref, dual_ref, full_ref, *refs):
    line_refs, (dual_new_ref,) = take(refs, peers, 1)
    proj_new = projected(line_refs, full_ref.at[1])
    dual_new_ref[...] = dual_ref[...] + rho_weight * (phase_ref[...] - proj_new)


def call(kernel, outs, args, specs=None, out_specs=None, scratch=(), flops=0, name=None, grid=(), aliases=None, vmem=4):
    return pl.pallas_call(
        kernel,
        grid=grid,
        out_shape=tuple(outs),
        in_specs=specs or [VMEM_SPEC] * len(args),
        out_specs=tuple(out_specs or [VMEM_SPEC] * len(outs)),
        scratch_shapes=list(scratch),
        input_output_aliases=aliases or {},
        cost_estimate=pl.CostEstimate(flops=flops, bytes_accessed=1 << 20, transcendentals=0),
        name=name,
        compiler_params=pltpu.CompilerParams(vmem_limit_bytes=vmem * MIB),
    )(*args)


def shards(volume, phase, dual, probe_real, probe_imag, intensity, offsets, angle_index):
    share, slices, length = volume.shape
    width = probe_real.shape[1]
    half = length // 2
    ang = lax.axis_size("ang")
    tiles = lax.axis_size("tile")
    groups = ang // 2
    pair = 2 * share
    parts = 2 if slices % 16 == 0 else 1
    some = slices // parts
    shape = jax.ShapeDtypeStruct

    (forward_full, inverse_full), (forward, inverse) = packed_tables(length)
    full = np.stack([split_pair(forward_full), split_pair(inverse_full)])
    down, up = forward.T, inverse.T
    square = np.stack([forward, inverse, down, up])
    line = shape((slices, length), F32)
    work = 2 * 2 * length * length * length * slices * groups

    def swap(value):
        return lax.ppermute(value, "ang", [(i, i ^ 1) for i in range(ang)])

    def from_peer(value, j):
        return lax.ppermute(value, "ang", [((i + 2 * j) % ang, i) for i in range(ang)])

    def to_peer(value, j):
        return lax.ppermute(value, "ang", [(i, (i + 2 * j) % ang) for i in range(ang)])

    def lanes(side):
        return pl.BlockSpec((share * slices, half), lambda _: (0, side))

    tables_shape = [
        shape((3, length, half), F32), shape((2, half, length), F32), shape((8, length), F32)
    ] * groups
    block_lines = [
        pl.BlockSpec((some, length), functools.partial(lambda h, _: (h, 0), h)) for h in range(parts)
    ]

    (phases,) = call(copies_kernel, [shape((tiles, slices, length), F32)], [phase[0]], name="phase_copies")
    phases, volume, angle_sent = lax.optimization_barrier((phases, volume, angle_index))
    image = lax.all_to_all(phases, "tile", split_axis=0, concat_axis=0, tiled=True)
    image = image.reshape(tiles * slices, length)

    flat = volume.reshape(share * slices, length)
    other = swap(flat)
    edges = call(
        functools.partial(edge_kernel, slices),
        [shape((pair, length), BF16)] * 2,
        [flat, flat, other, other],
        [lanes(0), lanes(1)] * 2,
        grid=(1,),
        vmem=6,
        name="edges",
    )
    before = lax.ppermute(edges[0], "tile", [(i, i + 1) for i in range(tiles - 1)])
    after = lax.ppermute(edges[1], "tile", [(i + 1, i) for i in range(tiles - 1)])
    angles = [from_peer(angle_sent, j) for j in range(1, groups)]
    image, before, angles = lax.optimization_barrier((image, before, angles))

    (grad,) = call(
        gradient_kernel,
        [shape((tiles, slices, length), BF16)],
        [offsets[0], image, intensity[0], probe_real, probe_imag, patch_tables(width)],
        [SMEM_SPEC] + [VMEM_SPEC] * 5,
        flops=2 * work,
        vmem=12,
        name="gradient",
    )
    grad, after, angles = lax.optimization_barrier((grad, after, angles))
    grad = lax.all_to_all(grad, "tile", split_axis=0, concat_axis=0, tiled=True)

    far = groups - 1
    outs = call(
        functools.partial(project_kernel, far, slices),
        [line] * far
        + [shape((slices, share, length), F32), shape((slices, share, length), BF16)]
        + [shape((slices, pair, length), BF16)],
        angles + [flat, flat, other, other, square],
        [SMEM_SPEC] * far + [lanes(0), lanes(1)] * 2 + [VMEM_SPEC],
        scratch=[pltpu.VMEM(t.shape, F32) for t in tables_shape[3:]],
        grid=(1,),
        flops=3 * work * far // groups,
        vmem=28,
        name="project_old",
    )
    lines, bases, slab = take(outs, far, 2, 1)
    old = [to_peer(lines[j], j + 1) for j in range(far)]
    old += call(
        functools.partial(own_line_kernel, 1, False, 0),
        [line],
        slab + [square, angle_index],
        [VMEM_SPEC] * 2 + [SMEM_SPEC],
        scratch=[pltpu.VMEM(t.shape, F32) for t in tables_shape[:3]],
        flops=3 * work // groups,
        vmem=24,
        name="project_old_own",
    )

    phase_part, resid_part = call(
        functools.partial(line_kernel, groups), [line, line], [phase[0], dual[0], full] + old,
        name="line_step",
    )
    phase_new, spectrum = call(
        phase_kernel, [line, line], [grad, phase_part, resid_part, full], name="phase_step"
    )
    spectrum, angles = lax.optimization_barrier((spectrum, [angle_index] + angles))
    tables = call(
        functools.partial(tables_kernel, groups), tables_shape, angles, [SMEM_SPEC] * groups,
        flops=work, name="turn_tables",
    )
    tables = list(tables)
    spectra = [spectrum] + [from_peer(spectrum, j) for j in range(1, groups)]

    halves = []
    for h in range(parts):
        (mine,) = call(
            functools.partial(back_kernel, groups),
            [shape((some, pair, length), BF16)],
            spectra + [square] + tables,
            [block_lines[h]] * groups + [VMEM_SPEC] * (1 + 3 * groups),
            grid=(1,),
            flops=3 * work // parts,
            vmem=24,
            name="backproject",
        )
        halves.append((mine, swap(mine)))

    results = []
    for h in range(parts):
        last = h == parts - 1
        count = far if last else groups
        args = bases + [before, after] + list(halves[h]) + [square]
        args = args + (tables[3:] if last else tables[3:] + tables[:3])
        carried = results[: 1 + count]
        outs = call(
            functools.partial(update_kernel, count, h == 0, last, len(carried)),
            [shape((share, slices, length), F32)]
            + [line] * count
            + ([shape((some, pair, length), BF16)] if last else []),
            args + carried,
            [pl.BlockSpec((some, share, length), lambda _, h=h: (h, 0, 0))] * 2
            + [VMEM_SPEC] * (len(args) - 2) + [pl.BlockSpec(memory_space=pl.ANY)] * len(carried),
            [pl.BlockSpec((share, some, length), lambda _, h=h: (0, h, 0))]
            + [block_lines[h]] * count
            + ([VMEM_SPEC] if last else []),
            scratch=[pltpu.VMEM((share * some, half), F32)] * 2,
            grid=(1,),
            flops=3 * work * count // groups // parts,
            vmem=24,
            aliases={len(args) + i: i for i in range(len(carried))},
            name="project_new",
        )
        results = list(outs[: 1 + count]) + results[1 + count :]
    volume_new, lines, slab = results[0], results[1:groups], outs[-1]
    new = [to_peer(lines[j], j + 1) for j in range(far)]
    own_line = results[groups:]
    args = [slab, square] + tables[:3] + own_line
    new += call(
        functools.partial(own_line_kernel, 1, True, len(own_line)),
        [line],
        args,
        [VMEM_SPEC] * 5 + [pl.BlockSpec(memory_space=pl.ANY)] * len(own_line),
        [block_lines[parts - 1]],
        grid=(1,),
        flops=3 * work // groups // parts,
        vmem=24,
        aliases={5: 0} if own_line else None,
        name="project_new_own",
    )
    (dual_new,) = call(
        functools.partial(dual_kernel, groups), [line], [phase_new, dual[0], full] + new,
        name="dual_step",
    )
    return phase_new[None], volume_new, dual_new[None]


def solution(mesh):
    placed = (
        P("ang", "tile", None),
        P("ang", "tile", None),
        P("ang", "tile", None),
        P(),
        P(),
        P("ang", "tile", None, None),
        P("ang", "tile"),
        P("ang"),
    )
    return jax.shard_map(
        shards,
        mesh=mesh,
        in_specs=placed,
        out_specs=(P("ang", "tile", None), P("ang", "tile", None), P("ang", "tile", None)),
        check_vma=False,
    )
```

```python
import functools
import math

import jax
import jax.numpy as jnp
import numpy as np
from jax import lax
from jax.experimental import pallas as pl
from jax.experimental.pallas import tpu as pltpu
from jax.sharding import PartitionSpec as P

angle_center = 90.0
rho_weight = 1.0
eta_step = 0.01
tau_step = 1.0
smooth_weight = 0.25

F32 = jnp.float32
BF16 = jnp.bfloat16
VMEM_SPEC = pl.BlockSpec(memory_space=pltpu.VMEM)
SMEM_SPEC = pl.BlockSpec(memory_space=pltpu.SMEM)
MIB = 1024 * 1024


def table_pair(length):
    index = np.arange(length)
    phases = (index[:, None] * index[None, :] % length) * (2.0 * np.pi / length)
    return np.cos(phases).astype(np.float32), np.sin(phases).astype(np.float32)


def packed_tables(length):
    half = length // 2
    cos_t, sin_t = table_pair(length)
    bf = np.asarray(jnp.bfloat16).dtype if False else jnp.bfloat16
    out = []
    for kind in (np.float32, bf):
        c = cos_t.astype(kind).astype(np.float32)
        s = sin_t.astype(kind).astype(np.float32)
        forward = np.concatenate([c[:, : half + 1], -s[:, 1:half]], axis=1)
        weight = np.full((length, 1), 2.0 / length, np.float32)
        weight[0] = weight[half] = 1.0 / length
        inverse = forward.T * weight
        out.append((forward.astype(kind), inverse.astype(kind)))
    return out


def split_pair(array):
    high = array.astype(jnp.bfloat16)
    low = (array - high.astype(np.float32)).astype(jnp.bfloat16)
    return np.stack([high, low])


def patch_tables(width):
    cos_t, sin_t = table_pair(width)
    scale = np.float32(math.sqrt(width))
    return np.stack([split_pair(cos_t / scale), split_pair(sin_t / scale)], axis=1)


def dot(left, right):
    return jnp.dot(left, right, preferred_element_type=F32)


def dot_high(left, right):
    return jnp.dot(left, right, precision=lax.Precision.HIGHEST, preferred_element_type=F32)


def dot_split(left, right):
    def parts(value):
        if isinstance(value, list) or value.dtype == BF16:
            return value[0], value[1]
        high = value.astype(BF16)
        return high, (value - high.astype(F32)).astype(BF16)

    left_high, left_low = parts(left)
    right_high, right_low = parts(right)
    return dot(
        jnp.concatenate([left_high, left_low, left_high], axis=1),
        jnp.concatenate([right_high, right_high, right_low], axis=0),
    )


def cos_sin(x):
    turns = jnp.floor(x * (2.0 / math.pi) + 0.5)
    r = x - turns * 1.5703125 - turns * 4.837512969970703125e-4 - turns * 7.54978995489188216e-8
    z = r * r
    sine = r + r * z * (-1.6666654611e-1 + z * (8.3321608736e-3 - z * 1.9515295891e-4))
    cosine = 1.0 - 0.5 * z + z * z * (
        4.166664568298827e-2 + z * (-1.388731625493765e-3 + z * 2.443315711809948e-5)
    )
    quarter = turns.astype(jnp.int32)
    odd = (quarter & 1) == 1
    first = jnp.where(odd, sine, cosine)
    second = jnp.where(odd, cosine, sine)
    return (
        jnp.where(((quarter + 1) & 2) == 2, -first, first),
        jnp.where((quarter & 2) == 2, -second, second),
    )


def turn(re, im, c1, s, c2, sign):
    if sign > 0:
        return re * c1 + im * s, im * c2 - re * s
    return re * c1 - im * s, im * c2 + re * s


def fill_turn_tables(angle, length, row_ref, col_ref, nyq_ref):
    half = length // 2
    unit = 2.0 * math.pi / length
    theta = (jnp.full((8, half), angle, jnp.int32).astype(F32) - angle_center) * (math.pi / 360.0)
    coef_a = -(jnp.sin(0.5 * theta) / jnp.cos(0.5 * theta))
    coef_b = jnp.sin(theta)

    lane = lax.broadcasted_iota(jnp.int32, (8, half), 1)
    sub = lax.broadcasted_iota(jnp.int32, (8, half), 0)
    freq = jnp.where(lane == 0, half, lane).astype(F32)
    phase = unit * coef_a * freq
    base = phase * sub.astype(F32)
    base_c, base_s = cos_sin(base)
    for block in range(length // 64):
        first = 8 * block * 8 - half
        step = phase * (first + 8 * sub).astype(F32)
        step_c, step_s = cos_sin(step)
        for q in range(8):
            sc, ss = step_c[q : q + 1], step_s[q : q + 1]
            c2 = base_c * sc - base_s * ss
            s = base_s * sc + base_c * ss
            rows = pl.ds((block * 8 + q) * 8, 8)
            row_ref[0, rows, :] = jnp.where(lane == 0, 1.0, c2)
            row_ref[1, rows, :] = jnp.where(lane == 0, 0.0, s)
            row_ref[2, rows, :] = c2

    for side in range(2):
        place = (lane + (side * half - half)).astype(F32)
        phase = unit * coef_b * place
        lanes = slice(side * half, side * half + half)
        base = phase * sub.astype(F32)
        base_c, base_s = cos_sin(base)
        for block in range(half // 64):
            step = phase * (block * 64 + 8 * sub).astype(F32)
            step_c, step_s = cos_sin(step)
            for q in range(8):
                sc, ss = step_c[q : q + 1], step_s[q : q + 1]
                rows = pl.ds((block * 8 + q) * 8, 8)
                col_ref[0, rows, lanes] = base_c * sc - base_s * ss
                col_ref[1, rows, lanes] = base_s * sc + base_c * ss
        top = jnp.where(sub == 0, jnp.cos(phase * float(half)), base_c)
        nyq_ref[:, lanes] = top


def chip_places(share):
    here = lax.axis_index("ang")
    other = here + 1 - 2 * lax.rem(here, 2)
    return [pl.ds(pl.multiple_of(which * share, share), share) for which in (here, other)]


def chip_table(table_ref, share):
    return jnp.concatenate([table_ref[rows, :] for rows in chip_places(share)], axis=0)


class Tables:
    def __init__(self, row, col, nyq):
        self.row, self.col, self.nyq = row, col, nyq

    def rows(self):
        return self.row[0], self.row[1], self.row[2]

    def chip_rows(self, share):
        return tuple(chip_table(self.row.at[part], share) for part in range(3))

    def columns(self):
        c1 = self.col[0]
        return c1, self.col[1], jnp.concatenate([self.nyq[...], c1[8:]], axis=0)


def turn_rows(spectrum, tables, sign):
    half = spectrum.shape[1] // 2
    return turn(spectrum[:, :half], spectrum[:, half:], *tables, sign)


def turn_columns(spectrum, tables, sign):
    half = spectrum.shape[0] // 2
    pair = turn(spectrum[:half], spectrum[half:], *tables, sign)
    return jnp.concatenate(pair, axis=0).astype(BF16)


def side_by_side(value, count):
    rows = value.shape[0] // count
    return jnp.concatenate([value[i * rows : (i + 1) * rows] for i in range(count)], axis=1)


def stacked(value, count):
    columns = value.shape[1] // count
    return jnp.concatenate([value[:, i * columns : (i + 1) * columns] for i in range(count)], axis=0)


def block_of(value, i, count, axis):
    size = value.shape[axis] // count
    return lax.slice_in_dim(value, i * size, (i + 1) * size, axis=axis)


def project_slices(slab, count, share, tables, consts, lines_refs):
    forward_ref, inverse_ref, up_ref = consts
    down = jnp.transpose(chip_table(forward_ref, share).astype(F32)).astype(BF16)
    spectrum = dot(slab, forward_ref[...])
    for table, lines_ref in zip(tables, lines_refs):
        chip_rows = table.chip_rows(share)
        turned = [
            jnp.concatenate(turn_rows(block_of(spectrum, i, count, 0), chip_rows, 1), axis=1).astype(BF16)
            for i in range(count)
        ]
        first = dot(jnp.concatenate(turned, axis=0), inverse_ref[...]).astype(BF16)
        columns = dot(down, side_by_side(first, count))
        turned = [turn_columns(block_of(columns, i, count, 1), table.columns(), 1) for i in range(count)]
        second = dot(up_ref[...], jnp.concatenate(turned, axis=1)).astype(BF16)
        last = dot(stacked(second, count), forward_ref[...])
        for i in range(count):
            re, im = turn_rows(block_of(last, i, count, 0), table.rows(), 1)
            sums = [jnp.sum(part, axis=0, keepdims=True) for part in (re, im)]
            lines_ref[pl.ds(i, 1), :] = jnp.concatenate(sums, axis=1)


def take(refs, *counts):
    refs, out = list(refs), []
    for count in counts:
        out.append(refs[:count])
        refs = refs[count:]
    return out


def as_tables(refs):
    return [Tables(*refs[i : i + 3]) for i in range(0, len(refs), 3)]


def tables_kernel(groups, *refs):
    angle_refs, table_refs = take(refs, groups, 3 * groups)
    for g in range(groups):
        row_ref, col_ref, nyq_ref = table_refs[3 * g : 3 * g + 3]
        fill_turn_tables(angle_refs[g][0], row_ref.shape[1], row_ref, col_ref, nyq_ref)


def copies_kernel(phase_ref, out_ref):
    out_ref[...] = jnp.broadcast_to(phase_ref[...][None], out_ref.shape)


def edge_kernel(slices, *refs):
    sides, edges = take(refs, 4, 2)
    share = sides[0].shape[0] // slices
    for edge_ref, z in zip(edges, (slices - 1, 0)):
        pieces = [ref[pl.ds(z, share, stride=slices), :].astype(BF16) for ref in sides]
        edge_ref[:share, :] = jnp.concatenate(pieces[:2], axis=1)
        edge_ref[share:, :] = jnp.concatenate(pieces[2:], axis=1)


def project_kernel(groups, slices, *refs):
    angle_refs, sides, (const_ref,), lines_refs, bases, (slab_ref,), table_refs = take(
        refs, groups, 4, 1, groups, 2, 1, 3 * groups
    )
    share = sides[0].shape[0] // slices
    tables_kernel(groups, *angle_refs, *table_refs)

    def rows(z):
        pieces = [ref[pl.ds(z, share, stride=slices), :] for ref in sides]
        return [jnp.concatenate(pieces[:2], axis=1), jnp.concatenate(pieces[2:], axis=1)]

    slab = []
    past, now = None, rows(0)
    for z in range(slices):
        later = rows(z + 1) if z + 1 < slices else None
        for place in range(2):
            slab.append(now[place].astype(BF16))
            near = [side[place] for side in (past, later) if side is not None]
            base = (1.0 - 2.0 * tau_step * smooth_weight) * now[place]
            base = base + (tau_step * smooth_weight) * sum(near[1:], near[0])
            bases[place][z] = base.astype(bases[place].dtype)
        past, now = now, later
    slab = jnp.concatenate(slab, axis=0)
    slab_ref[...] = slab.reshape(slab_ref.shape)
    consts = [const_ref.at[0], const_ref.at[1], const_ref.at[3]]
    project_slices(slab, slices, share, as_tables(table_refs), consts, lines_refs)


def own_line_kernel(pieces, made, aliased, *refs):
    slabs, (const_ref,), given, unused, (line_ref,), table_refs = take(
        refs, pieces, 1, 3 if made else 1, aliased, 1, 0 if made else 3
    )
    if not made:
        tables_kernel(1, *given, *table_refs)
    slab = jnp.concatenate([ref[...].reshape(-1, ref.shape[2]) for ref in slabs], axis=0)
    consts = [const_ref.at[0], const_ref.at[1], const_ref.at[3]]
    tables = as_tables(given if made else table_refs)
    project_slices(slab, line_ref.shape[0], slabs[0].shape[1] // 2, tables, consts, [line_ref])


def back_kernel(groups, *refs):
    spectra_refs, (const_ref,), table_refs, (out_ref,) = take(refs, groups, 1, 3 * groups, 1)
    forward_ref, inverse_ref, down_ref = const_ref.at[0], const_ref.at[1], const_ref.at[2]
    slices, pair, length = out_ref.shape
    half = length // 2
    up = chip_table(const_ref.at[3], pair // 2)
    totals = None
    for table, spectra_ref in zip(as_tables(table_refs), spectra_refs):
        turned = []
        for z in range(slices):
            line = spectra_ref[pl.ds(z, 1), :]
            pieces = turn(line[:, :half], line[:, half:], *table.rows(), -1)
            turned.append(jnp.concatenate(pieces, axis=1).astype(BF16))
        spread = dot(jnp.concatenate(turned, axis=0), inverse_ref[...]).astype(BF16)
        columns = dot(down_ref[...], side_by_side(spread, slices))
        turned = [turn_columns(block_of(columns, i, slices, 1), table.columns(), -1) for i in range(slices)]
        second = dot(up, jnp.concatenate(turned, axis=1)).astype(BF16)
        last = dot(stacked(second, slices), forward_ref[...])
        chip_rows = table.chip_rows(pair // 2)
        turned = [
            jnp.concatenate(turn_rows(block_of(last, i, slices, 0), chip_rows, -1), axis=1)
            for i in range(slices)
        ]
        totals = turned if totals is None else [old + new for old, new in zip(totals, turned)]
    total = jnp.concatenate([value.astype(BF16) for value in totals], axis=0)
    out_ref[...] = dot(total, inverse_ref[...]).astype(BF16).reshape(out_ref.shape)


def update_kernel(groups, first, last, aliased, *refs):
    bases, halos, shares, (const_ref,), table_refs, unused, (volume_ref,), lines_refs, slabs, sides = take(
        refs, 2, 2, 2, 1, 3 * groups, aliased, 1, groups, 1 if last else 0, 2
    )
    consts = [const_ref.at[0], const_ref.at[1], const_ref.at[3]]
    own_ref, other_ref = bases
    mine_ref, theirs_ref = shares
    slices, share, length = own_ref.shape
    half = length // 2
    slab = []
    for z in range(slices):
        own = own_ref[z] - tau_step * (
            mine_ref[z, :share, :].astype(F32) + theirs_ref[z, share:, :].astype(F32)
        )
        other = other_ref[z].astype(F32) - tau_step * (
            mine_ref[z, share:, :].astype(F32) + theirs_ref[z, :share, :].astype(F32)
        )
        for needed, halo_ref in ((first and z == 0, halos[0]), (last and z == slices - 1, halos[1])):
            if needed:
                halo = (tau_step * smooth_weight) * halo_ref[...].astype(F32)
                own, other = own + halo[:share], other + halo[share:]
        for side in range(2):
            sides[side][pl.ds(z, share, stride=slices), :] = own[:, side * half : (side + 1) * half]
        slab += [own.astype(BF16), other.astype(BF16)]
    slab = jnp.concatenate(slab, axis=0)
    for slab_ref in slabs:
        slab_ref[...] = slab.reshape(slab_ref.shape)
    project_slices(slab, slices, share, as_tables(table_refs), consts, lines_refs)
    whole = jnp.concatenate([ref[...] for ref in sides], axis=1)
    volume_ref[...] = whole.reshape(volume_ref.shape)


def gradient_kernel(
    offsets_ref, image_ref, measured_ref, probe_r_ref, probe_i_ref,
    const_ref, out_ref,
):
    right, left = [], []
    for part in range(2):
        c, s = const_ref[part, 0], const_ref[part, 1]
        plus = [jnp.concatenate([c, s], axis=1), jnp.concatenate([-s, c], axis=1)]
        minus = [jnp.concatenate([c, -s], axis=1), jnp.concatenate([s, c], axis=1)]
        left.append(jnp.concatenate(plus, axis=0))
        right.append(jnp.concatenate(minus, axis=0))
    positions, height, width = measured_ref.shape
    length = image_ref.shape[1]
    image = image_ref[...]
    cos_image, sin_image = cos_sin(image)
    probe_r, probe_i = probe_r_ref[...], probe_i_ref[...]
    waves = []
    for p in range(positions):
        back = length - offsets_ref[p]
        cos_p = pltpu.roll(cos_image, back, 1)[:, :width]
        sin_p = pltpu.roll(sin_image, back, 1)[:, :width]
        waves.append((probe_r * cos_p - probe_i * sin_p, probe_r * sin_p + probe_i * cos_p))

    def to_columns(value):
        parts = [block_of(value, p, positions, 0) for p in range(positions)]
        return jnp.concatenate(
            [jnp.concatenate([part[:, i * width : (i + 1) * width] for part in parts], axis=1) for i in range(2)],
            axis=0,
        )

    def to_rows(value):
        parts = [block_of(value, p, positions, 1) for p in range(positions)]
        return jnp.concatenate(
            [jnp.concatenate([part[:height], part[height:]], axis=1) for part in parts], axis=0
        )

    entry = jnp.concatenate([jnp.concatenate(wave, axis=1) for wave in waves], axis=0)
    far = dot_split(left, to_columns(dot_split(entry, right)))
    far_r, far_i = far[:height], far[height:]
    measured = jnp.concatenate([measured_ref[p] for p in range(positions)], axis=1)
    misfit = far_r * far_r + far_i * far_i - measured
    weighted = jnp.concatenate([misfit * far_r, misfit * far_i], axis=0)
    chi = dot_split(to_rows(dot_split(right, weighted)), left)
    total = jnp.zeros((height, length), F32)
    for p in range(positions):
        part = block_of(chi, p, positions, 0)
        wave_r, wave_i = waves[p]
        term = 2.0 * (part[:, width:] * wave_r - part[:, :width] * wave_i)
        padded = jnp.concatenate([term, jnp.zeros((height, length - width), F32)], axis=1)
        total = total + pltpu.roll(padded, offsets_ref[p], 1)
    out_ref[...] = total.astype(out_ref.dtype).reshape(out_ref.shape)


def projected(line_refs, inverse_ref):
    line = line_refs[0][...]
    for other in line_refs[1:]:
        line = line + other[...]
    return dot_split(line, inverse_ref[...]) * (1.0 / math.sqrt(line.shape[1]))


def line_kernel(peers, phase_ref, dual_ref, full_ref, *refs):
    line_refs, (phase_part_ref, resid_part_ref) = take(refs, peers, 2)
    proj_old = projected(line_refs, full_ref.at[1])
    phase, dual = phase_ref[...], dual_ref[...]
    phase_part = phase - eta_step * (dual + rho_weight * (phase - proj_old))
    phase_part_ref[...] = phase_part
    resid_part_ref[...] = rho_weight * (proj_old - phase_part) - dual


def phase_kernel(grad_ref, phase_part_ref, resid_part_ref, full_ref, phase_new_ref, spectrum_ref):
    grad = grad_ref[0].astype(F32)
    for t in range(1, grad_ref.shape[0]):
        grad = grad + grad_ref[t].astype(F32)
    grad = eta_step * grad
    phase_new_ref[...] = phase_part_ref[...] - grad
    resid = resid_part_ref[...] + rho_weight * grad
    spectrum_ref[...] = dot_split(resid, full_ref[0]) * (1.0 / math.sqrt(resid.shape[1]))


def dual_kernel(peers, phase_ref, dual_ref, full_ref, *refs):
    line_refs, (dual_new_ref,) = take(refs, peers, 1)
    proj_new = projected(line_refs, full_ref.at[1])
    dual_new_ref[...] = dual_ref[...] + rho_weight * (phase_ref[...] - proj_new)


def call(kernel, outs, args, specs=None, out_specs=None, scratch=(), flops=0, name=None, grid=(), aliases=None, vmem=4):
    return pl.pallas_call(
        kernel,
        grid=grid,
        out_shape=tuple(outs),
        in_specs=specs or [VMEM_SPEC] * len(args),
        out_specs=tuple(out_specs or [VMEM_SPEC] * len(outs)),
        scratch_shapes=list(scratch),
        input_output_aliases=aliases or {},
        cost_estimate=pl.CostEstimate(flops=flops, bytes_accessed=1 << 20, transcendentals=0),
        name=name,
        compiler_params=pltpu.CompilerParams(vmem_limit_bytes=vmem * MIB),
    )(*args)


def shards(volume, phase, dual, probe_real, probe_imag, intensity, offsets, angle_index):
    share, slices, length = volume.shape
    width = probe_real.shape[1]
    half = length // 2
    ang = lax.axis_size("ang")
    tiles = lax.axis_size("tile")
    groups = ang // 2
    pair = 2 * share
    parts = 2 if slices % 16 == 0 else 1
    some = slices // parts
    shape = jax.ShapeDtypeStruct

    (forward_full, inverse_full), (forward, inverse) = packed_tables(length)
    full = np.stack([split_pair(forward_full), split_pair(inverse_full)])
    down, up = forward.T, inverse.T
    square = np.stack([forward, inverse, down, up])
    line = shape((slices, length), F32)
    work = 2 * 2 * length * length * length * slices * groups

    def swap(value):
        return lax.ppermute(value, "ang", [(i, i ^ 1) for i in range(ang)])

    def from_peer(value, j):
        return lax.ppermute(value, "ang", [((i + 2 * j) % ang, i) for i in range(ang)])

    def to_peer(value, j):
        return lax.ppermute(value, "ang", [(i, (i + 2 * j) % ang) for i in range(ang)])

    def lanes(side):
        return pl.BlockSpec((share * slices, half), lambda _: (0, side))

    tables_shape = [
        shape((3, length, half), F32), shape((2, half, length), F32), shape((8, length), F32)
    ] * groups
    block_lines = [
        pl.BlockSpec((some, length), functools.partial(lambda h, _: (h, 0), h)) for h in range(parts)
    ]

    (phases,) = call(copies_kernel, [shape((tiles, slices, length), F32)], [phase[0]], name="phase_copies")
    phases, volume, angle_sent = lax.optimization_barrier((phases, volume, angle_index))
    image = lax.all_to_all(phases, "tile", split_axis=0, concat_axis=0, tiled=True)
    image = image.reshape(tiles * slices, length)

    flat = volume.reshape(share * slices, length)
    other = swap(flat)
    edges = call(
        functools.partial(edge_kernel, slices),
        [shape((pair, length), BF16)] * 2,
        [flat, flat, other, other],
        [lanes(0), lanes(1)] * 2,
        grid=(1,),
        vmem=6,
        name="edges",
    )
    before = lax.ppermute(edges[0], "tile", [(i, i + 1) for i in range(tiles - 1)])
    after = lax.ppermute(edges[1], "tile", [(i + 1, i) for i in range(tiles - 1)])
    angles = [from_peer(angle_sent, j) for j in range(1, groups)]
    image, before, angles = lax.optimization_barrier((image, before, angles))

    (grad,) = call(
        gradient_kernel,
        [shape((tiles, slices, length), BF16)],
        [offsets[0], image, intensity[0], probe_real, probe_imag, patch_tables(width)],
        [SMEM_SPEC] + [VMEM_SPEC] * 5,
        flops=2 * work,
        vmem=12,
        name="gradient",
    )
    grad, after, angles = lax.optimization_barrier((grad, after, angles))
    grad = lax.all_to_all(grad, "tile", split_axis=0, concat_axis=0, tiled=True)

    far = groups - 1
    outs = call(
        functools.partial(project_kernel, far, slices),
        [line] * far
        + [shape((slices, share, length), F32), shape((slices, share, length), BF16)]
        + [shape((slices, pair, length), BF16)],
        angles + [flat, flat, other, other, square],
        [SMEM_SPEC] * far + [lanes(0), lanes(1)] * 2 + [VMEM_SPEC],
        scratch=[pltpu.VMEM(t.shape, F32) for t in tables_shape[3:]],
        grid=(1,),
        flops=3 * work * far // groups,
        vmem=28,
        name="project_old",
    )
    lines, bases, slab = take(outs, far, 2, 1)
    old = [to_peer(lines[j], j + 1) for j in range(far)]
    old += call(
        functools.partial(own_line_kernel, 1, False, 0),
        [line],
        slab + [square, angle_index],
        [VMEM_SPEC] * 2 + [SMEM_SPEC],
        scratch=[pltpu.VMEM(t.shape, F32) for t in tables_shape[:3]],
        flops=3 * work // groups,
        vmem=24,
        name="project_old_own",
    )

    phase_part, resid_part = call(
        functools.partial(line_kernel, groups), [line, line], [phase[0], dual[0], full] + old,
        name="line_step",
    )
    phase_new, spectrum = call(
        phase_kernel, [line, line], [grad, phase_part, resid_part, full], name="phase_step"
    )
    spectrum, angles = lax.optimization_barrier((spectrum, [angle_index] + angles))
    tables = call(
        functools.partial(tables_kernel, groups), tables_shape, angles, [SMEM_SPEC] * groups,
        flops=work, name="turn_tables",
    )
    tables = list(tables)
    spectra = [spectrum] + [from_peer(spectrum, j) for j in range(1, groups)]

    halves = []
    for h in range(parts):
        (mine,) = call(
            functools.partial(back_kernel, groups),
            [shape((some, pair, length), BF16)],
            spectra + [square] + tables,
            [block_lines[h]] * groups + [VMEM_SPEC] * (1 + 3 * groups),
            grid=(1,),
            flops=3 * work // parts,
            vmem=24,
            name="backproject",
        )
        halves.append((mine, swap(mine)))

    results = []
    for h in range(parts):
        last = h == parts - 1
        count = far if last else groups
        args = bases + [before, after] + list(halves[h]) + [square]
        args = args + (tables[3:] if last else tables[3:] + tables[:3])
        carried = results[: 1 + count]
        outs = call(
            functools.partial(update_kernel, count, h == 0, last, len(carried)),
            [shape((share, slices, length), F32)]
            + [line] * count
            + ([shape((some, pair, length), BF16)] if last else []),
            args + carried,
            [pl.BlockSpec((some, share, length), lambda _, h=h: (h, 0, 0))] * 2
            + [VMEM_SPEC] * (len(args) - 2) + [pl.BlockSpec(memory_space=pl.ANY)] * len(carried),
            [pl.BlockSpec((share, some, length), lambda _, h=h: (0, h, 0))]
            + [block_lines[h]] * count
            + ([VMEM_SPEC] if last else []),
            scratch=[pltpu.VMEM((share * some, half), F32)] * 2,
            grid=(1,),
            flops=3 * work * count // groups // parts,
            vmem=24,
            aliases={len(args) + i: i for i in range(len(carried))},
            name="project_new",
        )
        results = list(outs[: 1 + count]) + results[1 + count :]
    volume_new, lines, slab = results[0], results[1:groups], outs[-1]
    new = [to_peer(lines[j], j + 1) for j in range(far)]
    own_line = results[groups:]
    args = [slab, square] + tables[:3] + own_line
    new += call(
        functools.partial(own_line_kernel, 1, True, len(own_line)),
        [line],
        args,
        [VMEM_SPEC] * 5 + [pl.BlockSpec(memory_space=pl.ANY)] * len(own_line),
        [block_lines[parts - 1]],
        grid=(1,),
        flops=3 * work // groups // parts,
        vmem=24,
        aliases={5: 0} if own_line else None,
        name="project_new_own",
    )
    (dual_new,) = call(
        functools.partial(dual_kernel, groups), [line], [phase_new, dual[0], full] + new,
        name="dual_step",
    )
    return phase_new[None], volume_new, dual_new[None]


def solution(mesh):
    placed = (
        P("ang", "tile", None),
        P("ang", "tile", None),
        P("ang", "tile", None),
        P(),
        P(),
        P("ang", "tile", None, None),
        P("ang", "tile"),
        P("ang"),
    )
    return jax.shard_map(
        shards,
        mesh=mesh,
        in_specs=placed,
        out_specs=(P("ang", "tile", None), P("ang", "tile", None), P("ang", "tile", None)),
        check_vma=False,
    )
```
